256 devices in a mesh: dp: 16 (over y, x_hi, core), seq: 16 (over z, x_lo).
Axes of the slice: x: 4 (x_hi: 2, x_lo: 2; x = x_hi * 2 + x_lo), y: 4, z: 8, core: 2. Of those that a mesh axis runs over, the one named last changes fastest.
Arguments:
- frames: bfloat16 [16, 4096, 1536], P('dp', 'seq'), may hold values from -6 to 6
- cotangent: bfloat16 [16, 4096, 1536], P('dp', 'seq'), may hold values from -6 to 6
- lengths: int32 [16], P('dp'), may hold values from 128 to 4096, as said below
- w_qkv: bfloat16 [1536, 2304], replicated, as said below
- w_out: bfloat16 [768, 1536], replicated, may hold values from -0.21875 to 0.21875
Outputs:
- block_out: bfloat16 [16, 4096, 1536], P('dp', 'seq')
- frame_grad: bfloat16 [16, 4096, 1536], P('dp', 'seq')
- weight_grads: float32 [1536, 3072], P(('dp', 'seq'))
The draws below stay inside these ranges and needn't reach their ends.
Inputs may be any that keep to these rules, and one draw needn't show every extreme that they name: `lengths`: some recording has exactly 4096 valid frames and some has exactly 128. `w_qkv`: entries of order 1536 ** -0.5 or a few times that.
All inputs are finite; a program needn't handle non-finite values.
Results may differ from the reference program's by a relative error of at most 0.015.
Values may be sent and summed in bfloat16 or wider, within the bound.
No kernel may reach another device: no remote copies, remote signals or barrier semaphores. Data moves between devices by JAX's collectives and lax.ppermute only.
A program may use at most 192 MiB of HBM per device.

```python
import jax
import jax.numpy as jnp
from jax import lax

D = 1536
HEADS = 12
HEAD_DIM = 64
GROUP = 32
LEFT = 4
F_DEV = 256
HD = 768
FRAMES = 4096
RECS = 16


def draw_lengths(key, part):
    key = jax.random.fold_in(key, 5)
    first_key = jax.random.fold_in(key, 1)
    second_key = jax.random.fold_in(key, 2)
    drawn = jax.random.randint(first_key, (RECS,), F_DEV // 2, FRAMES + 1)
    order = jax.random.permutation(second_key, RECS)
    drawn = drawn.at[order[0]].set(FRAMES).at[order[1]].set(F_DEV // 2)
    return drawn.astype(jnp.int32)


def draw_w_qkv(key, part):
    key = jax.random.fold_in(key, 11)
    inner_width = HEADS * HEAD_DIM
    matrix = jax.random.normal(key, (D, 3 * inner_width), jnp.float32) * D ** (-0.5)
    return matrix.astype(jnp.bfloat16)


def levels(key, shape, shards, smallest, top_value):
    def one(position, blocks):
        heights = jax.random.uniform(jax.random.fold_in(jax.random.fold_in(key, 6), position), (blocks,), jnp.float32, smallest / len(shards), top_value / len(shards))
        return jnp.repeat(jnp.exp(heights), shape[position] // blocks).reshape((-1,) + (1,) * (len(shape) - position - 1))

    loudness = one(*shards[0])
    for cut in shards[1:]:
        loudness = loudness * one(*cut)
    return loudness


def centred(rng, dims, scale, limit, cuts=(), dtype=jnp.bfloat16):
    values = scale * jax.random.normal(rng, dims, jnp.float32)
    if cuts:
        values = values * levels(rng, dims, cuts, -0.22, 0.18)
    return jnp.clip(values, -limit, limit).astype(dtype)


def setup_inputs(seed: int = 0) -> dict:
    arg_keys = jax.random.split(jax.random.key(seed), 6)
    return {
        "frames": centred(arg_keys[0], (RECS, FRAMES, D), 1.0, 6.0, ((0, 16), (1, 16))),
        "cotangent": centred(arg_keys[1], (RECS, FRAMES, D), 1.0, 6.0, ((0, 16), (1, 16))),
        "lengths": draw_lengths(jax.random.fold_in(arg_keys[5], 71), 0),
        "w_qkv": draw_w_qkv(jax.random.fold_in(arg_keys[5], 71), 0),
        "w_out": centred(arg_keys[4], (HD, D), HD ** -0.5, 0.21875),
    }


epsilon = 1e-05

def normalize(rows_in):
    average = lax.optimization_barrier(jnp.mean(rows_in, axis=-1, keepdims=True))
    centered = rows_in - average
    variance = lax.optimization_barrier(jnp.mean(centered * centered, axis=-1, keepdims=True))
    return centered * lax.rsqrt(variance + epsilon)

def attend(queries, key_rows, value_rows, key_valid, query_valid):
    row_count = queries.shape[0]
    blocks = row_count // GROUP
    head_count = queries.shape[1] // HEAD_DIM
    query_blocks = queries.reshape(blocks, GROUP, head_count, HEAD_DIM)
    key_blocks = key_rows.reshape(blocks + LEFT, GROUP, head_count, HEAD_DIM)
    value_blocks = value_rows.reshape(blocks + LEFT, GROUP, head_count, HEAD_DIM)
    valid_blocks = key_valid.reshape(blocks + LEFT, GROUP)
    key_window = jnp.concatenate([key_blocks[offset:offset + blocks] for offset in range(LEFT + 1)], axis=1)
    value_window = jnp.concatenate([value_blocks[offset:offset + blocks] for offset in range(LEFT + 1)], axis=1)
    valid_window = jnp.concatenate([valid_blocks[offset:offset + blocks] for offset in range(LEFT + 1)], axis=1)
    scores = jnp.einsum('bqhd,bkhd->bhqk', query_blocks, key_window) * HEAD_DIM ** (-0.5)
    scores = jnp.where(valid_window[:, None, None, :], scores, -1e+30)
    highest = lax.optimization_barrier(jnp.max(scores, axis=-1, keepdims=True))
    raised = jnp.exp(scores - highest)
    probability = raised / lax.optimization_barrier(jnp.sum(raised, axis=-1, keepdims=True))
    rounded = lax.optimization_barrier(probability.astype(jnp.bfloat16)).astype(jnp.float32)
    mixed = jnp.einsum('bhqk,bkhd->bqhd', rounded, value_window)
    mixed = mixed.reshape(row_count, head_count * HEAD_DIM)
    return jnp.where(query_valid[:, None], mixed, 0.0)

def recording(frame_rows, grad_rows, length, w_qkv, w_out):
    row_count = frame_rows.shape[0]
    inner_width = w_out.shape[0]
    context = LEFT * GROUP
    positions = jnp.arange(row_count)
    valid = positions < length
    norm_value, norm_back = jax.vjp(normalize, frame_rows.astype(jnp.float32))
    normed = norm_value.astype(jnp.bfloat16)
    projected = jnp.dot(normed, w_qkv, preferred_element_type=jnp.float32).astype(jnp.bfloat16)
    key_valid = jnp.concatenate([jnp.zeros((context,), bool), valid])
    zero_rows = jnp.zeros((context, inner_width), jnp.float32)

    def attention(query_part, key_part, value_part):
        return attend(query_part.astype(jnp.float32), jnp.concatenate([zero_rows, key_part.astype(jnp.float32)], axis=0), jnp.concatenate([zero_rows, value_part.astype(jnp.float32)], axis=0), key_valid, valid)
    attn_value, attn_back = jax.vjp(attention, projected[:, :inner_width], projected[:, inner_width:2 * inner_width], projected[:, 2 * inner_width:])
    attended = attn_value.astype(jnp.bfloat16)
    block_out = jnp.dot(attended, w_out, preferred_element_type=jnp.float32).astype(jnp.bfloat16)
    attended_grad = jnp.dot(grad_rows, w_out.T, preferred_element_type=jnp.float32).astype(jnp.bfloat16)
    query_grad, key_grad, value_grad = attn_back(attended_grad.astype(jnp.float32))
    projected_grad = jnp.concatenate([query_grad, key_grad, value_grad], axis=1).astype(jnp.bfloat16)
    normed_grad = jnp.dot(projected_grad, w_qkv.T, preferred_element_type=jnp.float32).astype(jnp.bfloat16)
    frame_grad, = norm_back(normed_grad.astype(jnp.float32))
    grad_term = jnp.concatenate([jnp.dot(normed.T, projected_grad, preferred_element_type=jnp.float32), jnp.dot(grad_rows.T, attended, preferred_element_type=jnp.float32)], axis=1)
    return (block_out, frame_grad.astype(jnp.bfloat16), grad_term)

def reference(frames, cotangent, lengths, w_qkv, w_out):

    def visit(running, item):
        frame_rows, grad_rows, length = item
        block_out, frame_grad, grad_term = recording(frame_rows, grad_rows, length, w_qkv, w_out)
        return (running + grad_term, (block_out, frame_grad))
    initial = jnp.zeros((w_qkv.shape[0], 4 * w_out.shape[0]), jnp.float32)
    running, (block_out, frame_grad) = lax.scan(visit, initial, (frames, cotangent, lengths))
    return (block_out, frame_grad, running)
```

```python
import jax
import jax.numpy as jnp
import numpy as np
from jax import lax
from jax.experimental import pallas as pl
from jax.experimental.pallas import tpu as pltpu
from jax.sharding import PartitionSpec as P

HEAD_DIM = 64
GROUP = 32
LEFT = 4
CONTEXT = LEFT * GROUP
PAIR = 2 * HEAD_DIM
F32 = jnp.float32
BF16 = jnp.bfloat16
NT = (((1,), (1,)), ((), ()))
NN = (((1,), (0,)), ((), ()))

Y, XH, CORES, Z, XL = 4, 2, 2, 8, 2
CHUNKS = Y * XH * XL

epsilon = 1e-05


def dot(a, b, dims=NN):
    return lax.dot_general(a, b, dims, preferred_element_type=F32)


def from_behind(value, axis, by):
    peers = lax.axis_size(axis)
    pairs = [(i, i + by) for i in range(peers) if 0 <= i + by < peers]
    return lax.ppermute(value, axis, pairs)


def flat(y, xh, core, z, xl):
    return ((y * XH + xh) * CORES + core) * (Z * XL) + z * XL + xl


def to_device(value, where):
    pairs = []
    for place in np.ndindex(Y, XH, CORES, Z, XL):
        pairs.append((flat(*place), flat(*where(*place))))
    return lax.ppermute(value, ("dp", "seq"), pairs)


def to_core(y, xh, core, z, xl):
    return y, xh, 1 - core, z, xl


def to_x_near(y, xh, core, z, xl):
    return y, xh, core, z, 1 - xl


def to_x_mirror(y, xh, core, z, xl):
    return y, 1 - xh, core, z, 1 - xl


def to_y_near(y, xh, core, z, xl):
    return y ^ 1, xh, core, z, xl


def to_y_mirror(y, xh, core, z, xl):
    return 3 - y, xh, core, z, xl


ROUTES = (
    (to_x_near, to_x_mirror, to_y_near, to_y_mirror),
    (to_x_mirror, to_x_near, to_y_mirror, to_y_near),
    (to_y_near, to_y_mirror, to_x_near, to_x_mirror),
    (to_y_mirror, to_y_near, to_x_mirror, to_x_near),
)


def halves(route, hi, lo):
    return (hi ^ lo, hi) if route % 2 == 0 else (hi, hi ^ lo)


def chunk_at(route, slot, y, xh, xl):
    bits = [(slot >> (3 - i)) & 1 for i in range(4)]
    x_bits, y_bits = (bits[:2], bits[2:]) if route < 2 else (bits[2:], bits[:2])
    found = []
    for (hi, lo), pair in (((y >> 1, y & 1), y_bits), ((xh, xl), x_bits)):
        first, second = halves(route, hi, lo)
        first, second = first ^ pair[0], second ^ pair[1]
        found.append((second, first ^ second) if route % 2 == 0 else (first, first ^ second))
    (yh, yl), (xh_to, xl_to) = found
    return ((yh * 2 + yl) * XH + xh_to) * XL + xl_to


def source_rows(width):
    share = width // (CHUNKS * CORES * Z)
    order = np.arange(width).reshape(Y, XH, CORES, Z, XL, share)[:, :, 0]
    return order.transpose(0, 1, 3, 2, 4).reshape(-1, 1).astype(np.int32), share


def normalize(rows_in):
    average = jnp.mean(rows_in, axis=-1, keepdims=True)
    centered = rows_in - average
    variance = jnp.mean(centered * centered, axis=-1, keepdims=True)
    return centered * lax.rsqrt(variance + epsilon)


def order_kernel(places, source_ref, normed_ref, cotangent_ref, keep_ref, send_ref):
    step = pl.program_id(0)
    steps = pl.num_programs(0) // 2
    rows = source_ref.shape[0]
    width = normed_ref.shape[1]
    offset = places[0]
    core = lax.rem(places[1] + step // steps, 2)
    column = lax.broadcasted_iota(jnp.int32, (rows, width), 1)
    pick = jnp.where(column == source_ref[...] + core * offset, 1.0, 0.0).astype(BF16)
    tokens = normed_ref.shape[0]

    def fill(ref):
        ref[:, :tokens] = dot(pick, normed_ref[...], NT).astype(BF16)
        ref[:, tokens:] = dot(pick, cotangent_ref[...], NT).astype(BF16)

    pl.when(step < steps)(lambda: fill(keep_ref))
    pl.when(step >= steps)(lambda: fill(send_ref))


def order(normed, cotangent, core):
    tokens, width = normed.shape
    source, share = source_rows(width)
    places = jnp.stack([jnp.int32(share * Z * XL), core])
    block = 256
    steps = width // CORES // block
    whole = pl.BlockSpec((tokens, width), lambda i, s: (0, 0))
    half = jax.ShapeDtypeStruct((width // CORES, 2 * tokens), BF16)
    return pl.pallas_call(
        order_kernel,
        grid_spec=pltpu.PrefetchScalarGridSpec(
            num_scalar_prefetch=1,
            grid=(2 * steps,),
            in_specs=[pl.BlockSpec((block, 1), lambda i, s: (lax.rem(i, steps), 0)), whole, whole],
            out_specs=[
                pl.BlockSpec((block, 2 * tokens), lambda i, s: (jnp.minimum(i, steps - 1), 0)),
                pl.BlockSpec((block, 2 * tokens), lambda i, s: (jnp.maximum(i - steps, 0), 0)),
            ],
        ),
        out_shape=[half, half],
        compiler_params=pltpu.CompilerParams(vmem_limit_bytes=40 * 2**20),
        cost_estimate=pl.CostEstimate(
            flops=4 * tokens * width * width, bytes_accessed=8 * tokens * width, transcendentals=0
        ),
        name="order",
    )(places, jnp.asarray(source), normed, cotangent)


def attention_kernel(places, q_ref, k_ref, v_ref, kh_ref, vh_ref, do_ref, out_ref, dkv_ref, halo_ref):
    length = places[0]
    first_row = places[1]
    rows = q_ref.shape[0]
    tiles = rows // CONTEXT
    lane = lax.broadcasted_iota(jnp.int32, (CONTEXT, PAIR), 1)
    heads = (lane < HEAD_DIM, lane >= HEAD_DIM)
    keys = lax.broadcasted_iota(jnp.int32, (2 * CONTEXT, 2 * CONTEXT), 0)
    queries = lax.broadcasted_iota(jnp.int32, (2 * CONTEXT, 2 * CONTEXT), 1)
    key_block = keys // GROUP
    query_block = (queries % CONTEXT) // GROUP
    in_window = (key_block >= query_block) & (key_block <= query_block + LEFT)
    zero = jnp.zeros((CONTEXT, PAIR), BF16)
    k_all = [kh_ref[...]] + [k_ref[i * CONTEXT : (i + 1) * CONTEXT, :] for i in range(tiles)]
    v_all = [vh_ref[...]] + [v_ref[i * CONTEXT : (i + 1) * CONTEXT, :] for i in range(tiles)]
    dk_parts = [None] * (tiles + 1)
    dv_parts = [None] * (tiles + 1)
    for t in range(tiles):
        here = slice(t * CONTEXT, (t + 1) * CONTEXT)
        begin = first_row + t * CONTEXT
        key_place = begin - CONTEXT + keys
        seen = in_window & (key_place >= 0) & (key_place < length)
        q = q_ref[here, :]
        do = do_ref[here, :]
        row_valid = begin + lax.broadcasted_iota(jnp.int32, (CONTEXT, PAIR), 0) < length
        do = jnp.where(row_valid, do, zero)
        q2 = jnp.concatenate([jnp.where(h, q, zero) for h in heads], axis=0)
        do2 = jnp.concatenate([jnp.where(h, do, zero) for h in heads], axis=0)
        k2 = jnp.concatenate([k_all[t], k_all[t + 1]], axis=0)
        v2 = jnp.concatenate([v_all[t], v_all[t + 1]], axis=0)
        scores = dot(k2, q2, NT) * HEAD_DIM ** (-0.5)
        scores = jnp.where(seen, scores, -1e30)
        highest = jnp.max(scores, axis=0, keepdims=True)
        raised = jnp.exp(scores - highest)
        prob = raised * (1.0 / jnp.sum(raised, axis=0, keepdims=True))
        rounded = prob.astype(BF16)
        mixed = dot(v2.T, rounded)
        col_valid = begin + lax.broadcasted_iota(jnp.int32, (PAIR, CONTEXT), 1) < length
        mixed = jnp.concatenate([mixed[:HEAD_DIM, :CONTEXT], mixed[HEAD_DIM:, CONTEXT:]], axis=0)
        mixed = jnp.where(col_valid, mixed, 0.0)
        out_ref[0, here, :] = mixed.T.astype(BF16)
        dprob = dot(v2, do2, NT)
        inner = jnp.sum(prob * dprob, axis=0, keepdims=True)
        dscores = (prob * (dprob - inner) * HEAD_DIM ** (-0.5)).astype(BF16)
        dq = dot(k2.T, dscores)
        dq = jnp.concatenate([dq[:HEAD_DIM, :CONTEXT], dq[HEAD_DIM:, CONTEXT:]], axis=0)
        out_ref[1, here, :] = dq.T.astype(BF16)
        dk = dot(dscores, q2)
        dv = dot(rounded, do2)
        for part, grad in ((dk_parts, dk), (dv_parts, dv)):
            for i in range(2):
                piece = grad[i * CONTEXT : (i + 1) * CONTEXT]
                part[t + i] = piece if part[t + i] is None else part[t + i] + piece
    for n, part in enumerate((dk_parts, dv_parts)):
        halo_ref[n] = part[0].astype(BF16)
        for i in range(tiles):
            dkv_ref[n, i * CONTEXT : (i + 1) * CONTEXT, :] = part[i + 1]


def attention(places, projected, received, attended_grad):
    rows, inner = attended_grad.shape
    pairs = inner // PAIR

    def at(n, base):
        return pl.BlockSpec((n, PAIR), lambda p, s: (0, base + p))

    def both(n):
        return pl.BlockSpec((2, n, PAIR), lambda p, s: (0, 0, p))

    return pl.pallas_call(
        attention_kernel,
        grid_spec=pltpu.PrefetchScalarGridSpec(
            num_scalar_prefetch=1,
            grid=(pairs,),
            in_specs=[
                at(rows, 0),
                at(rows, pairs),
                at(rows, 2 * pairs),
                at(CONTEXT, 0),
                at(CONTEXT, pairs),
                at(rows, 0),
            ],
            out_specs=[both(rows), both(rows), both(CONTEXT)],
        ),
        out_shape=[
            jax.ShapeDtypeStruct((2, rows, inner), BF16),
            jax.ShapeDtypeStruct((2, rows, inner), F32),
            jax.ShapeDtypeStruct((2, CONTEXT, inner), BF16),
        ],
        compiler_params=pltpu.CompilerParams(vmem_limit_bytes=40 * 2**20),
        cost_estimate=pl.CostEstimate(
            flops=28 * rows * 2 * CONTEXT * inner, bytes_accessed=16 * rows * inner, transcendentals=rows * 4 * inner
        ),
        name="attention",
    )(places, projected, projected, projected, received, received, attended_grad)


def weight_kernel(chunks, left_ref, left_other_ref, right_ref, right_other_ref, keep_ref, send_ref, held):
    total = dot(left_ref[...], right_ref[0]) + dot(left_other_ref[...], right_other_ref[0])
    held[...] = total.reshape(held.shape)
    half = CHUNKS // 2
    for slot in range(CHUNKS):
        ref = keep_ref if slot < half else send_ref
        ref[slot % half] = held[chunks[slot]].astype(BF16)


def weight_section(chunks, left, left_other, left_block, right, right_other, right_block):
    rows = left.shape[0]
    tokens = right.shape[1]
    columns = right.shape[2] // 2
    lefts = pl.BlockSpec((rows, tokens), lambda i, s: (0, left_block))
    rights = pl.BlockSpec((1, tokens, columns), lambda i, s: (right_block[0], 0, right_block[1]))
    size = (CHUNKS // 2, rows // CHUNKS, columns)
    result = pl.BlockSpec(size, lambda i, s: (0, 0, 0))
    return pl.pallas_call(
        weight_kernel,
        grid_spec=pltpu.PrefetchScalarGridSpec(
            num_scalar_prefetch=1,
            grid=(1,),
            in_specs=[lefts, lefts, rights, rights],
            out_specs=[result, result],
            scratch_shapes=[pltpu.VMEM((CHUNKS, rows // CHUNKS, columns), F32)],
        ),
        out_shape=[jax.ShapeDtypeStruct(size, BF16)] * 2,
        compiler_params=pltpu.CompilerParams(vmem_limit_bytes=40 * 2**20),
        cost_estimate=pl.CostEstimate(
            flops=4 * rows * tokens * columns, bytes_accessed=4 * rows * (tokens + columns), transcendentals=0
        ),
        name="weight_section",
    )(chunks, left, left_other, right, right_other)


def halved(keep, send, route):
    for step, where in enumerate(ROUTES[route]):
        total = keep.astype(F32) + to_device(send, where).astype(F32)
        count = keep.shape[0] // 2
        if step < 3:
            keep, send = total[:count].astype(BF16), total[count:].astype(BF16)
    return total[0].astype(BF16)


def pieces_kernel(places, *refs):
    ins, outs, held = refs[:8], refs[8 : 8 + Z], refs[8 + Z]
    share = outs[0].shape[0]
    columns = ins[0].shape[1]
    for n, ref in enumerate(ins):
        block = ref[...].astype(F32)
        for z in range(Z):
            held[z, :share, n * columns : (n + 1) * columns] = block[z * share : (z + 1) * share]
    for step, ref in enumerate(outs):
        ref[...] = held[lax.rem(places[0] + step, Z), :share, :].astype(BF16)


def pieces(z, sections):
    rows, columns = sections[0].shape
    share, width = rows // Z, len(sections) * columns
    whole = pl.BlockSpec((rows, columns), lambda i, s: (0, 0))
    return pl.pallas_call(
        pieces_kernel,
        grid_spec=pltpu.PrefetchScalarGridSpec(
            num_scalar_prefetch=1,
            grid=(1,),
            in_specs=[whole] * len(sections),
            out_specs=[pl.BlockSpec((share, width), lambda i, s: (0, 0))] * Z,
            scratch_shapes=[pltpu.VMEM((Z, 8, width), F32)],
        ),
        out_shape=[jax.ShapeDtypeStruct((share, width), BF16)] * Z,
        compiler_params=pltpu.CompilerParams(vmem_limit_bytes=40 * 2**20),
        name="pieces",
    )(jnp.reshape(z, (1,)), *sections)


def on_device(frames, cotangent, lengths, w_qkv, w_out):
    frame_rows = frames[0]
    grad_rows = cotangent[0]
    row_count = frame_rows.shape[0]
    inner = w_out.shape[0]
    seq_index = lax.axis_index("seq")
    dp_index = lax.axis_index("dp")
    z, xl = seq_index // XL, seq_index % XL
    core, xh, y = dp_index % CORES, dp_index // CORES % XH, dp_index // (CORES * XH)
    places = jnp.stack([lengths[0], seq_index * row_count])
    chunks = [jnp.stack([chunk_at(r, slot, y, xh, xl) for slot in range(CHUNKS)]) for r in range(len(ROUTES))]

    normed = normalize(frame_rows.astype(F32)).astype(BF16)
    projected = dot(normed, w_qkv).astype(BF16)
    received = from_behind(projected[row_count - CONTEXT :, inner:], "seq", 1)
    attended_grad = dot(grad_rows, w_out, NT).astype(BF16)
    left, left_out = order(normed, grad_rows, core)
    left_other = to_device(left_out, to_core)

    own, kv_grad, halo = attention(places, projected, received, attended_grad)
    returned = from_behind(halo, "seq", -1)
    own_other = to_device(own, to_core)
    block_out = dot(own[0], w_out).astype(BF16)

    first = [
        weight_section(chunks[r], left, left_other, 1 - r // 2, own, own_other, (r // 2, r % 2))
        for r in range(len(ROUTES))
    ]
    kv_total = jnp.concatenate(
        [kv_grad[:, : row_count - CONTEXT], kv_grad[:, row_count - CONTEXT :] + returned.astype(F32)], axis=1
    ).astype(BF16)
    kv_other = to_device(kv_total, to_core)
    second = [
        weight_section(chunks[r], left, left_other, 0, kv_total, kv_other, (r // 2, r % 2))
        for r in range(len(ROUTES))
    ]
    projected_grad = jnp.concatenate([own[1], kv_total[0], kv_total[1]], axis=1)
    normed_grad = dot(projected_grad, w_qkv, NT).astype(BF16)
    _, norm_back = jax.vjp(normalize, frame_rows.astype(F32))
    (frame_grad,) = norm_back(normed_grad.astype(F32))

    first = [halved(keep, send, r) for r, (keep, send) in enumerate(first)]
    second = [halved(keep, send, r) for r, (keep, send) in enumerate(second)]
    shares = pieces(z, first[2:] + second + first[:2])
    total = shares[0].astype(F32)
    for step in range(1, Z):
        total += to_device(shares[step], lambda y, xh, core, z, xl: (y, xh, core, (z + step) % Z, xl)).astype(F32)
    return block_out[None], frame_grad.astype(BF16)[None], total


def solution(mesh):
    placed = (P("dp", "seq", None), P("dp", "seq", None), P("dp"), P(), P())
    return jax.shard_map(
        on_device,
        mesh=mesh,
        in_specs=placed,
        out_specs=(P("dp", "seq", None), P("dp", "seq", None), P(("dp", "seq"), None)),
        check_vma=False,
    )
```

```python
import jax
import jax.numpy as jnp
import numpy as np
from jax import lax
from jax.experimental import pallas as pl
from jax.experimental.pallas import tpu as pltpu
from jax.sharding import PartitionSpec as P

HEAD_DIM = 64
GROUP = 32
LEFT = 4
CONTEXT = LEFT * GROUP
PAIR = 2 * HEAD_DIM
F32 = jnp.float32
BF16 = jnp.bfloat16
NT = (((1,), (1,)), ((), ()))
NN = (((1,), (0,)), ((), ()))

Y, XH, CORES, Z, XL = 4, 2, 2, 8, 2
CHUNKS = Y * XH * XL

epsilon = 1e-05


def dot(a, b, dims=NN):
    return lax.dot_general(a, b, dims, preferred_element_type=F32)


def from_behind(value, axis, by):
    peers = lax.axis_size(axis)
    pairs = [(i, i + by) for i in range(peers) if 0 <= i + by < peers]
    return lax.ppermute(value, axis, pairs)


def flat(y, xh, core, z, xl):
    return ((y * XH + xh) * CORES + core) * (Z * XL) + z * XL + xl


def to_device(value, where):
    pairs = []
    for place in np.ndindex(Y, XH, CORES, Z, XL):
        pairs.append((flat(*place), flat(*where(*place))))
    return lax.ppermute(value, ("dp", "seq"), pairs)


def to_core(y, xh, core, z, xl):
    return y, xh, 1 - core, z, xl


def to_x_near(y, xh, core, z, xl):
    return y, xh, core, z, 1 - xl


def to_x_mirror(y, xh, core, z, xl):
    return y, 1 - xh, core, z, 1 - xl


def to_y_near(y, xh, core, z, xl):
    return y ^ 1, xh, core, z, xl


def to_y_mirror(y, xh, core, z, xl):
    return 3 - y, xh, core, z, xl


ROUTES = (
    (to_x_near, to_x_mirror, to_y_near, to_y_mirror),
    (to_x_mirror, to_x_near, to_y_mirror, to_y_near),
    (to_y_near, to_y_mirror, to_x_near, to_x_mirror),
    (to_y_mirror, to_y_near, to_x_mirror, to_x_near),
)


def halves(route, hi, lo):
    return (hi ^ lo, hi) if route % 2 == 0 else (hi, hi ^ lo)


def chunk_at(route, slot, y, xh, xl):
    bits = [(slot >> (3 - i)) & 1 for i in range(4)]
    x_bits, y_bits = (bits[:2], bits[2:]) if route < 2 else (bits[2:], bits[:2])
    found = []
    for (hi, lo), pair in (((y >> 1, y & 1), y_bits), ((xh, xl), x_bits)):
        first, second = halves(route, hi, lo)
        first, second = first ^ pair[0], second ^ pair[1]
        found.append((second, first ^ second) if route % 2 == 0 else (first, first ^ second))
    (yh, yl), (xh_to, xl_to) = found
    return ((yh * 2 + yl) * XH + xh_to) * XL + xl_to


def row_order(width):
    share = width // (CHUNKS * CORES * Z)
    order = np.arange(width // Y).reshape(XH, CORES, Z, XL, share).transpose(1, 0, 3, 2, 4).reshape(-1)
    return jnp.asarray(np.eye(width // Y, dtype=np.float32)[order], BF16)


def normalize(rows_in):
    average = jnp.mean(rows_in, axis=-1, keepdims=True)
    centered = rows_in - average
    variance = jnp.mean(centered * centered, axis=-1, keepdims=True)
    return centered * lax.rsqrt(variance + epsilon)


def project_kernel(frames_ref, weight_ref, normed_ref, projected_ref, tail_ref, held):
    step = pl.program_id(0)

    @pl.when(step == 0)
    def _():
        held[...] = normalize(frames_ref[...].astype(F32)).astype(BF16)
        normed_ref[...] = held[...]

    out = dot(held[...], weight_ref[...]).astype(BF16)
    projected_ref[...] = out
    tail_ref[...] = out[out.shape[0] - CONTEXT :]


def project(frames, weight):
    rows, width = frames.shape
    columns = weight.shape[1]
    block = HEAD_DIM * 6
    steps = columns // block
    skipped = steps // 3
    return pl.pallas_call(
        project_kernel,
        grid=(steps,),
        in_specs=[
            pl.BlockSpec((rows, width), lambda i: (0, 0)),
            pl.BlockSpec((width, block), lambda i: (0, i)),
        ],
        out_specs=[
            pl.BlockSpec((rows, width), lambda i: (0, 0)),
            pl.BlockSpec((rows, block), lambda i: (0, i)),
            pl.BlockSpec((CONTEXT, block), lambda i: (0, jnp.maximum(i - skipped, 0))),
        ],
        out_shape=[
            jax.ShapeDtypeStruct((rows, width), BF16),
            jax.ShapeDtypeStruct((rows, columns), BF16),
            jax.ShapeDtypeStruct((CONTEXT, columns // 3 * 2), BF16),
        ],
        scratch_shapes=[pltpu.VMEM((rows, width), BF16)],
        compiler_params=pltpu.CompilerParams(vmem_limit_bytes=40 * 2**20),
        cost_estimate=pl.CostEstimate(
            flops=2 * rows * width * columns, bytes_accessed=2 * width * columns, transcendentals=0
        ),
        name="project",
    )(frames, weight)


def turn_kernel(places, order_ref, normed_ref, cotangent_ref, keep_ref, send_ref):
    rows = order_ref.shape[0]
    half = rows // CORES
    for y in range(Y):
        here = slice(y * rows, (y + 1) * rows)
        turned = jnp.concatenate([normed_ref[:, here].T, cotangent_ref[:, here].T], axis=1)
        turned = dot(order_ref[...], turned).astype(BF16)
        there = slice(y * half, (y + 1) * half)

        @pl.when(places[0] == 0)
        def _():
            keep_ref[there, :] = turned[:half]
            send_ref[there, :] = turned[half:]

        @pl.when(places[0] == 1)
        def _():
            keep_ref[there, :] = turned[half:]
            send_ref[there, :] = turned[:half]


def turn(normed, cotangent, core):
    tokens, width = normed.shape
    order = row_order(width)
    whole = pl.BlockSpec((tokens, width), lambda i, s: (0, 0))
    result = pl.BlockSpec((width // CORES, 2 * tokens), lambda i, s: (0, 0))
    return pl.pallas_call(
        turn_kernel,
        grid_spec=pltpu.PrefetchScalarGridSpec(
            num_scalar_prefetch=1,
            grid=(1,),
            in_specs=[pl.BlockSpec(order.shape, lambda i, s: (0, 0)), whole, whole],
            out_specs=[result, result],
        ),
        out_shape=[jax.ShapeDtypeStruct((width // CORES, 2 * tokens), BF16)] * 2,
        compiler_params=pltpu.CompilerParams(vmem_limit_bytes=40 * 2**20),
        cost_estimate=pl.CostEstimate(
            flops=4 * tokens * width * width // Y, bytes_accessed=8 * tokens * width, transcendentals=0
        ),
        name="turn",
    )(jnp.reshape(core, (1,)), order, normed, cotangent)


def attend(begin, length, q, k2, v2, do):
    lane = lax.broadcasted_iota(jnp.int32, (CONTEXT, PAIR), 1)
    heads = (lane < HEAD_DIM, lane >= HEAD_DIM)
    keys = lax.broadcasted_iota(jnp.int32, (2 * CONTEXT, 2 * CONTEXT), 0)
    queries = lax.broadcasted_iota(jnp.int32, (2 * CONTEXT, 2 * CONTEXT), 1)
    key_block = keys // GROUP
    query_block = (queries % CONTEXT) // GROUP
    key_place = begin - CONTEXT + keys
    seen = (key_block >= query_block) & (key_block <= query_block + LEFT) & (key_place >= 0) & (key_place < length)
    zero = jnp.zeros((CONTEXT, PAIR), BF16)
    scale = HEAD_DIM ** (-0.5)
    row_valid = begin + lax.broadcasted_iota(jnp.int32, (CONTEXT, PAIR), 0) < length
    do = jnp.where(row_valid, do, zero)
    q = q * jnp.asarray(scale, BF16)
    q2 = jnp.concatenate([jnp.where(h, q, zero) for h in heads], axis=0)
    do2 = jnp.concatenate([jnp.where(h, do, zero) for h in heads], axis=0)
    scores = jnp.where(seen, dot(k2, q2, NT), -1e30)
    highest = jnp.max(scores, axis=0, keepdims=True)
    raised = jnp.exp(scores - highest)
    prob = raised * (1.0 / jnp.sum(raised, axis=0, keepdims=True))
    rounded = prob.astype(BF16)

    def unstack(both):
        return jnp.concatenate([both[:HEAD_DIM, :CONTEXT], both[HEAD_DIM:, CONTEXT:]], axis=0)

    col_valid = begin + lax.broadcasted_iota(jnp.int32, (PAIR, CONTEXT), 1) < length
    mixed = jnp.where(col_valid, unstack(dot(v2.T, rounded)), 0.0).T.astype(BF16)
    dprob = dot(v2, do2, NT)
    inner = jnp.sum(prob * dprob, axis=0, keepdims=True)
    dscores = (prob * (dprob - inner)).astype(BF16)
    dq = (unstack(dot(k2.T, dscores)) * scale).T.astype(BF16)
    return mixed, dq, dot(dscores, q2), dot(rounded, do2)


def late_kernel(places, q_ref, k_ref, v_ref, do_ref, out_ref, head_ref, tail_ref):
    begin = places[1] + CONTEXT
    out_ref[0], out_ref[1], dk, dv = attend(begin, places[0], q_ref[...], k_ref[...], v_ref[...], do_ref[...])
    for n, grad in enumerate((dk, dv)):
        head_ref[n] = grad[:CONTEXT]
        tail_ref[n] = grad[CONTEXT:]


def early_kernel(places, q_ref, k_ref, v_ref, kh_ref, vh_ref, do_ref, add_ref, out_ref, head_ref, halo_ref):
    k2 = jnp.concatenate([kh_ref[...], k_ref[...]], axis=0)
    v2 = jnp.concatenate([vh_ref[...], v_ref[...]], axis=0)
    out_ref[0], out_ref[1], dk, dv = attend(places[1], places[0], q_ref[...], k2, v2, do_ref[...])
    for n, grad in enumerate((dk, dv)):
        halo_ref[n] = grad[:CONTEXT].astype(BF16)
        head_ref[n] = (grad[CONTEXT:] + add_ref[n]).astype(BF16)


def attention(kernel, places, operands, in_specs, inner, types, name):
    both = pl.BlockSpec((2, CONTEXT, PAIR), lambda p, s: (0, 0, p))
    return pl.pallas_call(
        kernel,
        grid_spec=pltpu.PrefetchScalarGridSpec(
            num_scalar_prefetch=1,
            grid=(inner // PAIR,),
            in_specs=[both if spec is None else pl.BlockSpec((spec[0], PAIR), lambda p, s, spec=spec: (spec[1], spec[2] + p)) for spec in in_specs],
            out_specs=[both] * len(types),
        ),
        out_shape=[jax.ShapeDtypeStruct((2, CONTEXT, inner), dtype) for dtype in types],
        compiler_params=pltpu.CompilerParams(vmem_limit_bytes=40 * 2**20),
        cost_estimate=pl.CostEstimate(
            flops=28 * CONTEXT * 2 * CONTEXT * inner, bytes_accessed=16 * CONTEXT * inner, transcendentals=CONTEXT * 4 * inner
        ),
        name=name,
    )(places, *operands)


def weight_kernel(chunks, left_ref, left_other_ref, right_ref, right_other_ref, keep_ref, send_ref, held):
    total = dot(left_ref[...], right_ref[0]) + dot(left_other_ref[...], right_other_ref[0])
    held[...] = total.reshape(held.shape)
    half = CHUNKS // 2
    route = pl.program_id(0)
    for slot in range(CHUNKS):
        ref = keep_ref if slot < half else send_ref
        ref[0, slot % half] = held[chunks[route, slot]].astype(BF16)


def weight_sections(chunks, left, left_other, left_block, right, right_other):
    rows = left.shape[0]
    tokens = right.shape[1]
    columns = right.shape[2] // 2
    routes = len(ROUTES)
    lefts = pl.BlockSpec((rows, tokens), lambda r, s: (0, left_block(r)))
    rights = pl.BlockSpec((1, tokens, columns), lambda r, s: (r // 2, 0, r % 2))
    size = (CHUNKS // 2, rows // CHUNKS, columns)
    result = pl.BlockSpec((1, *size), lambda r, s: (r, 0, 0, 0))
    return pl.pallas_call(
        weight_kernel,
        grid_spec=pltpu.PrefetchScalarGridSpec(
            num_scalar_prefetch=1,
            grid=(routes,),
            in_specs=[lefts, lefts, rights, rights],
            out_specs=[result, result],
            scratch_shapes=[pltpu.VMEM((CHUNKS, rows // CHUNKS, columns), F32)],
        ),
        out_shape=[jax.ShapeDtypeStruct((routes, *size), BF16)] * 2,
        compiler_params=pltpu.CompilerParams(vmem_limit_bytes=40 * 2**20),
        cost_estimate=pl.CostEstimate(
            flops=4 * rows * tokens * columns * routes,
            bytes_accessed=4 * rows * (tokens + columns * routes),
            transcendentals=0,
        ),
        name="weight_sections",
    )(chunks, left, left_other, right, right_other)


def plus(a, b):
    return (a.astype(F32) + b.astype(F32)).astype(BF16)


def pieces_kernel(*refs):
    ins, out_ref, held = refs[:-2], refs[-2], refs[-1]
    share = out_ref.shape[1] // held.shape[1]
    for n, ref in enumerate(ins):
        block = ref[...].astype(F32)
        width = block.shape[1] // PAIR // 2
        bases = (((n + 2) % 4) * width + (0 if n > 1 else 4 * width), (2 + n) * width)
        for wave, base in enumerate(bases):
            for t in range(width):
                column = (wave * width + t) * PAIR
                for z in range(Z):
                    held[z, base + t] = block[z * share : (z + 1) * share, column : column + PAIR]
    for z in range(Z):
        for t in range(held.shape[1]):
            out_ref[z, t * share : (t + 1) * share, :] = held[z, t].astype(BF16)


def total_kernel(in_ref, out_ref):
    total = in_ref[0].astype(F32)
    for z in range(1, Z):
        total += in_ref[z].astype(F32)
    share = out_ref.shape[0]
    for t in range(out_ref.shape[1] // PAIR):
        out_ref[:, t * PAIR : (t + 1) * PAIR] = total[t * share : (t + 1) * share]


def on_device(frames, cotangent, lengths, w_qkv, w_out):
    frame_rows = frames[0]
    grad_rows = cotangent[0]
    row_count, width = frame_rows.shape
    inner = w_out.shape[0]
    pairs = inner // PAIR
    seq_index = lax.axis_index("seq")
    dp_index = lax.axis_index("dp")
    xl = seq_index % XL
    core, xh, y = dp_index % CORES, dp_index // CORES % XH, dp_index // (CORES * XH)
    places = jnp.stack([lengths[0], seq_index * row_count])
    routes = range(len(ROUTES))
    chunks = jnp.stack([jnp.stack([chunk_at(r, slot, y, xh, xl) for slot in range(CHUNKS)]) for r in routes])

    normed, projected, tail = project(frame_rows, w_qkv)
    received = from_behind(tail, "seq", 1)
    attended_grad = dot(grad_rows, w_out, NT).astype(BF16)
    late, late_head, late_tail = attention(
        late_kernel,
        places,
        (projected, projected, projected, attended_grad),
        ((CONTEXT, 1, 0), (2 * CONTEXT, 0, pairs), (2 * CONTEXT, 0, 2 * pairs), (CONTEXT, 1, 0)),
        inner,
        (BF16, F32, F32),
        "attention_late",
    )
    left, left_out = turn(normed, grad_rows, core)
    left_other = to_device(left_out, to_core)
    early, kv_head, halo = attention(
        early_kernel,
        places,
        (projected, projected, projected, received, received, attended_grad, late_head),
        ((CONTEXT, 0, 0), (CONTEXT, 0, pairs), (CONTEXT, 0, 2 * pairs), (CONTEXT, 0, 0), (CONTEXT, 0, pairs), (CONTEXT, 0, 0), None),
        inner,
        (BF16, BF16, BF16),
        "attention_early",
    )
    returned = from_behind(halo, "seq", -1)
    own = jnp.concatenate([early, late], axis=1)
    own_other = to_device(own, to_core)
    keep_a, send_a = weight_sections(chunks, left, left_other, lambda r: 1 - r // 2, own, own_other)
    got_a = [to_device(send_a[r], ROUTES[r][0]) for r in routes]

    kv_total = jnp.concatenate([kv_head, (late_tail + returned.astype(F32)).astype(BF16)], axis=1)
    kv_other = to_device(kv_total, to_core)
    keep_b, send_b = weight_sections(chunks, left, left_other, lambda r: 0, kv_total, kv_other)
    got_b = [to_device(send_b[r], ROUTES[r][0]) for r in routes]

    attended, send_a = lax.optimization_barrier((own[0], send_a))
    block_out = dot(attended, w_out).astype(BF16)
    projected_grad = jnp.concatenate([own[1], kv_total[0], kv_total[1]], axis=1)
    projected_grad, send_b = lax.optimization_barrier((projected_grad, send_b))
    normed_grad = dot(projected_grad, w_qkv, NT).astype(BF16)
    _, norm_back = jax.vjp(normalize, frame_rows.astype(F32))
    (frame_grad,) = norm_back(normed_grad.astype(F32))

    totals = [
        jnp.concatenate([plus(keep_a[r], got_a[r]), plus(keep_b[r], got_b[r])], axis=-1) for r in routes
    ]
    for step in range(1, 4):
        count = totals[0].shape[0] // 2
        sends = lax.optimization_barrier([t[count:] for t in totals])
        gots = lax.optimization_barrier([to_device(sends[r], ROUTES[r][step]) for r in routes])
        totals = [plus(totals[r][:count], gots[r]) for r in routes]
    share = width // (CHUNKS * CORES * Z)
    tiles = 4 * inner // PAIR
    shares = pl.pallas_call(
        pieces_kernel,
        out_shape=jax.ShapeDtypeStruct((Z, tiles * share, PAIR), BF16),
        scratch_shapes=[pltpu.VMEM((Z, tiles, share, PAIR), F32)],
        compiler_params=pltpu.CompilerParams(vmem_limit_bytes=40 * 2**20),
        name="pieces",
    )(*[t[0] for t in totals])
    rings = [[place * XL + x for place in range(Z)] for x in range(XL)]
    shares = lax.all_to_all(shares, "seq", 0, 0, axis_index_groups=rings, tiled=True)
    total = pl.pallas_call(
        total_kernel,
        out_shape=jax.ShapeDtypeStruct((share, 4 * inner), F32),
        name="total",
    )(shares)
    return block_out[None], frame_grad.astype(BF16)[None], total


def solution(mesh):
    placed = (P("dp", "seq", None), P("dp", "seq", None), P("dp"), P(), P())
    return jax.shard_map(
        on_device,
        mesh=mesh,
        in_specs=placed,
        out_specs=(P("dp", "seq", None), P("dp", "seq", None), P(("dp", "seq"), None)),
        check_vma=False,
    )
```

```python
import jax
import jax.numpy as jnp
import numpy as np
from jax import lax
from jax.experimental import pallas as pl
from jax.experimental.pallas import tpu as pltpu
from jax.sharding import PartitionSpec as P

HEAD_DIM = 64
GROUP = 32
LEFT = 4
CONTEXT = LEFT * GROUP
PAIR = 2 * HEAD_DIM
F32 = jnp.float32
BF16 = jnp.bfloat16
NT = (((1,), (1,)), ((), ()))
NN = (((1,), (0,)), ((), ()))

Y, XH, CORES, Z, XL = 4, 2, 2, 8, 2
CHUNKS = Y * XH * XL

epsilon = 1e-05


def dot(a, b, dims=NN):
    return lax.dot_general(a, b, dims, preferred_element_type=F32)


def from_behind(value, axis, by):
    peers = lax.axis_size(axis)
    pairs = [(i, i + by) for i in range(peers) if 0 <= i + by < peers]
    return lax.ppermute(value, axis, pairs)


def flat(y, xh, core, z, xl):
    return ((y * XH + xh) * CORES + core) * (Z * XL) + z * XL + xl


def to_device(value, where):
    pairs = []
    for place in np.ndindex(Y, XH, CORES, Z, XL):
        pairs.append((flat(*place), flat(*where(*place))))
    return lax.ppermute(value, ("dp", "seq"), pairs)


def to_core(y, xh, core, z, xl):
    return y, xh, 1 - core, z, xl


def to_x_near(y, xh, core, z, xl):
    return y, xh, core, z, 1 - xl


def to_x_mirror(y, xh, core, z, xl):
    return y, 1 - xh, core, z, 1 - xl


def to_y_near(y, xh, core, z, xl):
    return y ^ 1, xh, core, z, xl


def to_y_mirror(y, xh, core, z, xl):
    return 3 - y, xh, core, z, xl


def to_x_far(y, xh, core, z, xl):
    return y, 1 - xh, core, z, xl


def to_y_far(y, xh, core, z, xl):
    return y ^ 2, xh, core, z, xl


ROUTES = (
    (to_x_near, to_x_mirror),
    (to_x_mirror, to_x_near),
    (to_y_near, to_y_mirror),
    (to_y_mirror, to_y_near),
)
OWNERS = (
    (to_y_mirror, to_y_near, to_y_far),
    (to_x_mirror, to_x_near, to_x_far),
)


def halves(route, hi, lo):
    return (hi ^ lo, hi) if route % 2 == 0 else (hi, hi ^ lo)


def chunk_at(route, slot, y, xh, xl):
    bits = [(slot >> (3 - i)) & 1 for i in range(4)]
    x_first = route < 2
    x_bits, y_bits = (bits[:2], bits[2:]) if x_first else (bits[2:], bits[:2])
    found = []
    for hi, lo, pair, order in ((y >> 1, y & 1, y_bits, 0 if x_first else route), (xh, xl, x_bits, route if x_first else 0)):
        first, second = halves(order, hi, lo)
        first, second = first ^ pair[0], second ^ pair[1]
        found.append((second, first ^ second) if order % 2 == 0 else (first, first ^ second))
    (yh, yl), (xh_to, xl_to) = found
    return ((yh * 2 + yl) * XH + xh_to) * XL + xl_to


def row_order(width):
    share = width // (CHUNKS * CORES * Z)
    order = np.arange(width // Y).reshape(XH, CORES, Z, XL, share).transpose(1, 0, 3, 2, 4).reshape(-1)
    return jnp.asarray(np.eye(width // Y, dtype=np.float32)[order], BF16)


def normalize(rows_in):
    average = jnp.mean(rows_in, axis=-1, keepdims=True)
    centered = rows_in - average
    variance = jnp.mean(centered * centered, axis=-1, keepdims=True)
    return centered * lax.rsqrt(variance + epsilon)


SMEM_SPEC = pl.BlockSpec(memory_space=pltpu.SMEM)
VMEM_SPEC = pl.BlockSpec(memory_space=pltpu.VMEM)
HBM_SPEC = pl.BlockSpec(memory_space=pltpu.HBM)


def in_vmem(value):
    return pltpu.with_memory_space_constraint(value, pltpu.VMEM)


def in_hbm(value):
    return pltpu.with_memory_space_constraint(value, pltpu.HBM)


def cost(flops, nbytes, transcendentals=0):
    return pl.CostEstimate(flops=flops, bytes_accessed=nbytes, transcendentals=transcendentals)


def params(mebibytes):
    return pltpu.CompilerParams(vmem_limit_bytes=mebibytes * 2**20)


def fetch(source, target, sems, block, base=0):
    copies = []
    for i in range(target.shape[1] // block):
        there = source.at[:, pl.ds(base + i * block, block)]
        copies.append(pltpu.make_async_copy(there, target.at[:, pl.ds(i * block, block)], sems.at[i]))
        copies[-1].start()
    return copies


BLOCK = 384


def project_kernel(frames_ref, weight_ref, normed_ref, keys_ref, tail_ref, rows, weight, row_sem, sems):
    whole = pltpu.make_async_copy(frames_ref, rows, row_sem)
    whole.start()
    copies = fetch(weight_ref, weight, sems, BLOCK, weight_ref.shape[1] - weight.shape[1])
    whole.wait()
    normed_ref[...] = normalize(rows[...].astype(F32)).astype(BF16)
    for i, copy in enumerate(copies):
        copy.wait()
        here = slice(i * BLOCK, (i + 1) * BLOCK)
        out = dot(normed_ref[...], weight[:, here]).astype(BF16)
        keys_ref[:, here] = out
        tail_ref[:, here] = out[out.shape[0] - CONTEXT :]


def project(frames, weight):
    rows, width = frames.shape
    columns = weight.shape[1] // 3 * 2
    return pl.pallas_call(
        project_kernel,
        in_specs=[HBM_SPEC, HBM_SPEC],
        out_specs=[VMEM_SPEC] * 3,
        out_shape=[pltpu.VMEM((rows, width), BF16), pltpu.VMEM((rows, columns), BF16), pltpu.VMEM((CONTEXT, columns), BF16)],
        scratch_shapes=[
            pltpu.VMEM((rows, width), BF16),
            pltpu.VMEM((width, columns), BF16),
            pltpu.SemaphoreType.DMA,
            pltpu.SemaphoreType.DMA((columns // BLOCK,)),
        ],
        compiler_params=params(24),
        cost_estimate=cost(2 * rows * width * columns, 2 * width * columns),
        name="project",
    )(in_hbm(frames), in_hbm(weight))


def second_kernel(places, order_ref, normed_ref, cotangent_ref, weight_ref, out_ref,
                  query_ref, grad_ref, keep_ref, send_ref, cotangent, weight, outer, sem, sems, out_sem):
    whole = pltpu.make_async_copy(cotangent_ref, cotangent, sem)
    whole.start()
    copies = fetch(weight_ref, weight, sems, BLOCK)
    last = pltpu.make_async_copy(out_ref, outer, out_sem)
    last.start()
    rows = order_ref.shape[0]
    half = rows // CORES
    tokens = normed_ref.shape[0]

    def turn(ref, columns):
        for y in range(Y):
            turned = dot(order_ref[...], ref[:, y * rows : (y + 1) * rows].T).astype(BF16)
            there = slice(y * half, (y + 1) * half)

            @pl.when(places[0] == 0)
            def _():
                keep_ref[there, columns] = turned[:half]
                send_ref[there, columns] = turned[half:]

            @pl.when(places[0] == 1)
            def _():
                keep_ref[there, columns] = turned[half:]
                send_ref[there, columns] = turned[:half]

    turn(normed_ref, slice(0, tokens))
    for i, copy in enumerate(copies):
        copy.wait()
        here = slice(i * BLOCK, (i + 1) * BLOCK)
        query_ref[:, here] = dot(normed_ref[...], weight[:, here]).astype(BF16)
    whole.wait()
    turn(cotangent, slice(tokens, 2 * tokens))
    last.wait()
    grad_ref[...] = dot(cotangent[...], outer[...], NT).astype(BF16)


def second(normed, cotangent, w_qkv, w_out, core):
    tokens, width = normed.shape
    inner = w_out.shape[0]
    order = row_order(width)
    turned = pltpu.VMEM((width // CORES, 2 * tokens), BF16)
    return pl.pallas_call(
        second_kernel,
        in_specs=[SMEM_SPEC, VMEM_SPEC, VMEM_SPEC, HBM_SPEC, HBM_SPEC, HBM_SPEC],
        out_specs=[VMEM_SPEC] * 4,
        out_shape=[pltpu.VMEM((tokens, inner), BF16), pltpu.VMEM((tokens, inner), BF16), turned, turned],
        scratch_shapes=[
            pltpu.VMEM((tokens, width), BF16),
            pltpu.VMEM((width, inner), BF16),
            pltpu.VMEM((inner, width), BF16),
            pltpu.SemaphoreType.DMA,
            pltpu.SemaphoreType.DMA((inner // BLOCK,)),
            pltpu.SemaphoreType.DMA,
        ],
        compiler_params=params(24),
        cost_estimate=cost(8 * tokens * width * inner, 8 * inner * width),
        name="second",
    )(jnp.reshape(core, (1,)), in_vmem(order), normed, in_hbm(cotangent), in_hbm(w_qkv), in_hbm(w_out))


def attend(begin, length, inner, operands, results):
    lane = lax.broadcasted_iota(jnp.int32, (CONTEXT, PAIR), 1)
    heads = (lane < HEAD_DIM, lane >= HEAD_DIM)
    row_valid = begin + lax.broadcasted_iota(jnp.int32, (CONTEXT, PAIR), 0) < length
    col_valid = begin + lane < length
    keys = lax.broadcasted_iota(jnp.int32, (2 * CONTEXT, 2 * CONTEXT), 0)
    queries = lax.broadcasted_iota(jnp.int32, (2 * CONTEXT, 2 * CONTEXT), 1)
    key_block = keys // GROUP
    query_block = (queries % CONTEXT) // GROUP
    key_place = begin - CONTEXT + keys
    seen = (key_block >= query_block) & (key_block <= query_block + LEFT) & (key_place >= 0) & (key_place < length)
    zero = jnp.zeros((CONTEXT, PAIR), BF16)
    scale = HEAD_DIM ** (-0.5)

    def unstack(both):
        return jnp.concatenate([both[:HEAD_DIM, :CONTEXT], both[HEAD_DIM:, CONTEXT:]], axis=0)

    for pair in range(inner // PAIR):
        q, k2, v2, do = operands(pair)
        do = jnp.where(row_valid, do, zero)
        q = q * jnp.asarray(scale, BF16)
        q2 = jnp.concatenate([jnp.where(h, q, zero) for h in heads], axis=0)
        do2 = jnp.concatenate([jnp.where(h, do, zero) for h in heads], axis=0)
        scores = jnp.where(seen, dot(k2, q2, NT), -1e30)
        dprob = dot(v2, do2, NT)
        highest = jnp.max(scores, axis=0, keepdims=True)
        raised = jnp.exp(scores - highest)
        prob = raised * (1.0 / jnp.sum(raised, axis=0, keepdims=True))
        rounded = prob.astype(BF16)
        mixed = jnp.where(col_valid, unstack(dot(v2.T, rounded)), 0.0).T.astype(BF16)
        weighed = prob * dprob
        dscores = (weighed - prob * jnp.sum(weighed, axis=0, keepdims=True)).astype(BF16)
        dq = (unstack(dot(k2.T, dscores)) * scale).T.astype(BF16)
        results(pair, mixed, dq, dot(dscores, q2), dot(rounded, do2))


def late_kernel(places, q_ref, kv_ref, do_ref, out_ref, head_ref, tail_ref):
    inner = q_ref.shape[1]

    def operands(pair):
        at = slice(pair * PAIR, (pair + 1) * PAIR)
        return q_ref[CONTEXT:, at], kv_ref[:, at], kv_ref[:, slice(inner + at.start, inner + at.stop)], do_ref[CONTEXT:, at]

    def results(pair, mixed, dq, dk, dv):
        at = slice(pair * PAIR, (pair + 1) * PAIR)
        out_ref[0, :, at] = mixed
        out_ref[1, :, at] = dq
        for n, grad in enumerate((dk, dv)):
            head_ref[n, :, at] = grad[:CONTEXT]
            tail_ref[n, :, at] = grad[CONTEXT:]

    attend(places[1] + CONTEXT, places[0], inner, operands, results)


def early_kernel(places, q_ref, kv_ref, halo_ref, do_ref, add_ref, out_ref, head_ref, back_ref):
    inner = q_ref.shape[1]

    def operands(pair):
        at = slice(pair * PAIR, (pair + 1) * PAIR)
        v_at = slice(inner + at.start, inner + at.stop)
        k2 = jnp.concatenate([halo_ref[:, at], kv_ref[:CONTEXT, at]], axis=0)
        v2 = jnp.concatenate([halo_ref[:, v_at], kv_ref[:CONTEXT, v_at]], axis=0)
        return q_ref[:CONTEXT, at], k2, v2, do_ref[:CONTEXT, at]

    def results(pair, mixed, dq, dk, dv):
        at = slice(pair * PAIR, (pair + 1) * PAIR)
        out_ref[0, :, at] = mixed
        out_ref[1, :, at] = dq
        for n, grad in enumerate((dk, dv)):
            back_ref[n, :, at] = grad[:CONTEXT].astype(BF16)
            head_ref[n, :, at] = (grad[CONTEXT:] + add_ref[n, :, at]).astype(BF16)

    attend(places[1], places[0], inner, operands, results)


def attention(kernel, places, operands, inner, types, name):
    return pl.pallas_call(
        kernel,
        in_specs=[SMEM_SPEC] + [VMEM_SPEC] * len(operands),
        out_specs=[VMEM_SPEC] * len(types),
        out_shape=[pltpu.VMEM((2, CONTEXT, inner), dtype) for dtype in types],
        compiler_params=params(24),
        cost_estimate=cost(28 * CONTEXT * 2 * CONTEXT * inner, 16 * CONTEXT * inner, CONTEXT * 4 * inner),
        name=name,
    )(places, *[in_vmem(o) for o in operands])


def weight_kernel(lefts, chunks, left_ref, left_other_ref, right_ref, right_other_ref, *refs):
    outs, held = refs[:-1], refs[-1]
    tokens = right_ref.shape[1]
    columns = right_ref.shape[2] // 2
    half = CHUNKS // 2
    for n, left in enumerate(lefts):
        at = slice(left * tokens, (left + 1) * tokens)
        total = dot(left_ref[:, at], right_ref[n]) + dot(left_other_ref[:, at], right_other_ref[n])
        for part in range(2):
            route = 2 * n + part
            held[route] = total[:, part * columns : (part + 1) * columns].reshape(held.shape[1:])
            for slot in range(CHUNKS):
                ref = outs[route] if slot < half else outs[len(ROUTES) + route]
                ref[slot % half] = held[route, chunks[route, slot]].astype(BF16)


def weight_sections(chunks, left, left_other, lefts, right, right_other):
    rows = left.shape[0]
    tokens = right.shape[1]
    columns = right.shape[2] // 2
    routes = len(ROUTES)
    out = pltpu.VMEM((CHUNKS // 2, rows // CHUNKS, columns), BF16)
    outs = pl.pallas_call(
        lambda *refs: weight_kernel(lefts, *refs),
        in_specs=[SMEM_SPEC] + [VMEM_SPEC] * 4,
        out_specs=[VMEM_SPEC] * (2 * routes),
        out_shape=[out] * (2 * routes),
        scratch_shapes=[pltpu.VMEM((routes, CHUNKS, rows // CHUNKS, columns), F32)],
        compiler_params=params(24),
        cost_estimate=cost(4 * rows * tokens * columns * routes, 4 * rows * (tokens + columns * routes)),
        name="weight_sections",
    )(chunks, *[in_vmem(o) for o in (left, left_other, right, right_other)])
    return outs[:routes], outs[routes:]


def plus(*terms):
    return sum(t.astype(F32) for t in terms).astype(BF16)


def pieces_kernel(*refs):
    ins, out_ref, held = refs[:-2], refs[-2], refs[-1]
    for group, ref in enumerate(ins):
        block = ref[...].astype(F32)
        width = block.shape[1] // PAIR // 4
        share = block.shape[0] // Z
        for n in (2 * group, 2 * group + 1):
            bases = (((n + 2) % 4) * width + (0 if n > 1 else 4 * width), (2 + n) * width)
            for wave, base in enumerate(bases):
                for t in range(width):
                    column = (((n % 2) * 2 + wave) * width + t) * PAIR
                    for z in range(Z):
                        rows = slice((base + t) * share, (base + t + 1) * share)
                        held[z, rows, :] = block[z * share : (z + 1) * share, column : column + PAIR]
    out_ref[...] = held[...].astype(BF16)


def total_kernel(in_ref, out_ref):
    total = in_ref[0].astype(F32)
    for z in range(1, Z):
        total += in_ref[z].astype(F32)
    share = out_ref.shape[0]
    for t in range(out_ref.shape[1] // PAIR):
        out_ref[:, t * PAIR : (t + 1) * PAIR] = total[t * share : (t + 1) * share]


def on_device(frames, cotangent, lengths, w_qkv, w_out):
    frame_rows = frames[0]
    grad_rows = cotangent[0]
    row_count, width = frame_rows.shape
    inner = w_out.shape[0]
    seq_index = lax.axis_index("seq")
    dp_index = lax.axis_index("dp")
    xl = seq_index % XL
    core, xh, y = dp_index % CORES, dp_index // CORES % XH, dp_index // (CORES * XH)
    places = jnp.stack([lengths[0], seq_index * row_count])
    routes = range(len(ROUTES))
    chunks = jnp.stack([jnp.stack([chunk_at(r, slot, y, xh, xl) for slot in range(CHUNKS)]) for r in routes])

    normed, keys, tail = project(frame_rows, w_qkv)
    received = from_behind(tail, "seq", 1)
    queries, attended_grad, left, left_out = second(normed, grad_rows, w_qkv, w_out, core)
    left_other = to_device(left_out, to_core)
    late, late_head, late_tail = attention(
        late_kernel, places, (queries, keys, attended_grad), inner, (BF16, F32, F32), "attention_late"
    )
    early, kv_head, halo = attention(
        early_kernel, places, (queries, keys, received, attended_grad, late_head), inner, (BF16,) * 3, "attention_early"
    )
    returned = from_behind(halo, "seq", -1)
    own = jnp.concatenate([early, late], axis=1)
    own_other = to_device(own, to_core)
    keep_a, send_a = weight_sections(chunks, left, left_other, (1, 0), own, own_other)
    attended, late_tail, send_a = lax.optimization_barrier((own[0], late_tail, send_a))
    got_a = [to_device(send_a[r], ROUTES[r][0]) for r in routes]

    kv_total = jnp.concatenate([kv_head, plus(late_tail, returned)], axis=1)
    kv_other = to_device(kv_total, to_core)
    keep_b, send_b = weight_sections(chunks, left, left_other, (0, 0), kv_total, kv_other)
    projected_grad = jnp.concatenate([own[1], kv_total[0], kv_total[1]], axis=1)
    projected_grad, send_b = lax.optimization_barrier((projected_grad, send_b))
    got_b = [to_device(send_b[r], ROUTES[r][0]) for r in routes]

    block_out = dot(attended, w_out).astype(BF16)
    normed_grad = dot(projected_grad, w_qkv, NT).astype(BF16)
    _, norm_back = jax.vjp(normalize, frame_rows.astype(F32))
    (frame_grad,) = norm_back(normed_grad.astype(F32))

    totals = [
        jnp.concatenate([plus(keep_a[r], got_a[r]), plus(keep_b[r], got_b[r])], axis=-1) for r in routes
    ]
    count = totals[0].shape[0] // 2
    sends = lax.optimization_barrier([t[count:] for t in totals])
    gots = lax.optimization_barrier([to_device(sends[r], ROUTES[r][1]) for r in routes])
    totals = [plus(totals[r][:count], gots[r]) for r in routes]
    groups = [jnp.concatenate(totals[:2], axis=-1), jnp.concatenate(totals[2:], axis=-1)]
    slots = lax.optimization_barrier([[g[slot] for slot in range(1, 4)] for g in groups])
    gots = [[to_device(slots[n][i], OWNERS[n][i]) for n in range(2)] for i in range(3)]
    groups = [plus(groups[n][0], *[gots[i][n] for i in range(3)]) for n in range(2)]
    share = width // (CHUNKS * CORES * Z)
    tiles = 4 * inner // PAIR
    shares = pl.pallas_call(
        pieces_kernel,
        in_specs=[VMEM_SPEC] * 2,
        out_shape=jax.ShapeDtypeStruct((Z, tiles * share, PAIR), BF16),
        scratch_shapes=[pltpu.VMEM((Z, tiles * share, PAIR), F32)],
        compiler_params=params(24),
        name="pieces",
    )(*[in_vmem(g) for g in groups])
    rings = [[place * XL + x for place in range(Z)] for x in range(XL)]
    shares = lax.all_to_all(shares, "seq", 0, 0, axis_index_groups=rings, tiled=True)
    total = pl.pallas_call(
        total_kernel,
        in_specs=[VMEM_SPEC],
        out_shape=jax.ShapeDtypeStruct((share, 4 * inner), F32),
        compiler_params=params(24),
        name="total",
    )(in_vmem(shares))
    return block_out[None], frame_grad.astype(BF16)[None], total


def solution(mesh):
    placed = (P("dp", "seq", None), P("dp", "seq", None), P("dp"), P(), P())
    return jax.shard_map(
        on_device,
        mesh=mesh,
        in_specs=placed,
        out_specs=(P("dp", "seq", None), P("dp", "seq", None), P(("dp", "seq"), None)),
        check_vma=False,
    )
```

```python
import jax
import jax.numpy as jnp
import numpy as np
from jax import lax
from jax.experimental import pallas as pl
from jax.experimental.pallas import tpu as pltpu
from jax.sharding import PartitionSpec as P

HEAD_DIM = 64
GROUP = 32
LEFT = 4
CONTEXT = LEFT * GROUP
PAIR = 2 * HEAD_DIM
F32 = jnp.float32
BF16 = jnp.bfloat16
NT = (((1,), (1,)), ((), ()))
NN = (((1,), (0,)), ((), ()))

Y, XH, CORES, Z, XL = 4, 2, 2, 8, 2
CHUNKS = Y * XH * XL

epsilon = 1e-05


def dot(a, b, dims=NN):
    return lax.dot_general(a, b, dims, preferred_element_type=F32)


def from_behind(value, axis, by):
    peers = lax.axis_size(axis)
    return lax.ppermute(value, axis, [(i, (i + by) % peers) for i in range(peers)])


def flat(y, xh, core, z, xl):
    return ((y * XH + xh) * CORES + core) * (Z * XL) + z * XL + xl


def to_device(value, where):
    pairs = []
    for place in np.ndindex(Y, XH, CORES, Z, XL):
        pairs.append((flat(*place), flat(*where(*place))))
    return lax.ppermute(value, ("dp", "seq"), pairs)


def to_core(y, xh, core, z, xl):
    return y, xh, 1 - core, z, xl


def to_x_near(y, xh, core, z, xl):
    return y, xh, core, z, 1 - xl


def to_x_mirror(y, xh, core, z, xl):
    return y, 1 - xh, core, z, 1 - xl


def to_y_near(y, xh, core, z, xl):
    return y ^ 1, xh, core, z, xl


def to_y_mirror(y, xh, core, z, xl):
    return 3 - y, xh, core, z, xl


def to_x_far(y, xh, core, z, xl):
    return y, 1 - xh, core, z, xl


def to_y_far(y, xh, core, z, xl):
    return y ^ 2, xh, core, z, xl


ROUTES = (
    (to_x_near, to_x_mirror),
    (to_x_mirror, to_x_near),
    (to_y_near, to_y_mirror),
    (to_y_mirror, to_y_near),
)
OWNERS = (
    (to_y_mirror, to_y_near, to_y_far),
    (to_x_mirror, to_x_near, to_x_far),
)


def halves(route, hi, lo):
    return (hi ^ lo, hi) if route % 2 == 0 else (hi, hi ^ lo)


def chunk_at(route, slot, y, xh, xl):
    bits = [(slot >> (3 - i)) & 1 for i in range(4)]
    x_first = route < 2
    x_bits, y_bits = (bits[:2], bits[2:]) if x_first else (bits[2:], bits[:2])
    found = []
    for hi, lo, pair, order in ((y >> 1, y & 1, y_bits, 0 if x_first else route), (xh, xl, x_bits, route if x_first else 0)):
        first, second = halves(order, hi, lo)
        first, second = first ^ pair[0], second ^ pair[1]
        found.append((second, first ^ second) if order % 2 == 0 else (first, first ^ second))
    (yh, yl), (xh_to, xl_to) = found
    return ((yh * 2 + yl) * XH + xh_to) * XL + xl_to


def row_order(width):
    share = width // (CHUNKS * CORES * Z)
    order = np.arange(width // Y).reshape(XH, CORES, Z, XL, share).transpose(1, 0, 3, 2, 4).reshape(-1)
    return jnp.asarray(np.eye(width // Y, dtype=np.float32)[order], BF16)


def statistics(rows_in):
    average = jnp.mean(rows_in, axis=-1, keepdims=True)
    centered = rows_in - average
    variance = jnp.mean(centered * centered, axis=-1, keepdims=True)
    return average, lax.rsqrt(variance + epsilon)


def normalize_grad(rows_in, average, inverse, grad):
    normed = (rows_in - average) * inverse
    along = jnp.mean(grad * normed, axis=-1, keepdims=True)
    return inverse * (grad - jnp.mean(grad, axis=-1, keepdims=True) - normed * along)


SMEM_SPEC = pl.BlockSpec(memory_space=pltpu.SMEM)
VMEM_SPEC = pl.BlockSpec(memory_space=pltpu.VMEM)
HBM_SPEC = pl.BlockSpec(memory_space=pltpu.HBM)


def in_vmem(value):
    return pltpu.with_memory_space_constraint(value, pltpu.VMEM)


def in_hbm(value):
    return pltpu.with_memory_space_constraint(value, pltpu.HBM)


def cost(flops, nbytes, transcendentals=0):
    return pl.CostEstimate(flops=flops, bytes_accessed=nbytes, transcendentals=transcendentals)


def params(mebibytes):
    return pltpu.CompilerParams(vmem_limit_bytes=mebibytes * 2**20)


def fetch(source, target, sems, block, base=0):
    copies = []
    for i in range(target.shape[1] // block):
        there = source.at[:, pl.ds(base + i * block, block)]
        copies.append(pltpu.make_async_copy(there, target.at[:, pl.ds(i * block, block)], sems.at[i]))
        copies[-1].start()
    return copies


BLOCK = 768


def project_kernel(frames_ref, weight_ref, normed_ref, keys_ref, tail_ref, stats_ref, rows, weight, row_sem, sems):
    whole = pltpu.make_async_copy(frames_ref, rows, row_sem)
    whole.start()
    copies = fetch(weight_ref, weight, sems, BLOCK, weight_ref.shape[1] - weight.shape[1])
    whole.wait()
    values = rows[...].astype(F32)
    average, inverse = statistics(values)
    for n, column in enumerate((average, inverse)):
        stats_ref[n : n + 1, :] = jnp.broadcast_to(column, (column.shape[0], PAIR)).T[:1]
    normed_ref[...] = ((values - average) * inverse).astype(BF16)
    for i, copy in enumerate(copies):
        copy.wait()
        here = slice(i * BLOCK, (i + 1) * BLOCK)
        out = dot(normed_ref[...], weight[:, here]).astype(BF16)
        keys_ref[:, here] = out
        tail_ref[:, here] = out[out.shape[0] - CONTEXT :]


def project(frames, weight):
    rows, width = frames.shape
    columns = weight.shape[1] // 3 * 2
    return pl.pallas_call(
        project_kernel,
        in_specs=[HBM_SPEC, HBM_SPEC],
        out_specs=[VMEM_SPEC] * 4,
        out_shape=[
            pltpu.VMEM((rows, width), BF16),
            pltpu.VMEM((rows, columns), BF16),
            pltpu.VMEM((CONTEXT, columns), BF16),
            pltpu.VMEM((2, rows), F32),
        ],
        scratch_shapes=[
            pltpu.VMEM((rows, width), BF16),
            pltpu.VMEM((width, columns), BF16),
            pltpu.SemaphoreType.DMA,
            pltpu.SemaphoreType.DMA((columns // BLOCK,)),
        ],
        compiler_params=params(24),
        cost_estimate=cost(2 * rows * width * columns, 2 * width * columns),
        name="project",
    )(in_hbm(frames), in_hbm(weight))


def second_kernel(places, order_ref, normed_ref, cotangent_ref, weight_ref, out_ref,
                  query_ref, grad_ref, keep_ref, send_ref, cotangent, weight, outer, sem, sems, out_sem):
    whole = pltpu.make_async_copy(cotangent_ref, cotangent, sem)
    whole.start()
    first = pltpu.make_async_copy(out_ref, outer, out_sem)
    first.start()
    copies = fetch(weight_ref, weight, sems, BLOCK)
    rows = order_ref.shape[0]
    half = rows // CORES
    tokens = normed_ref.shape[0]

    def turn(ref, columns):
        for y in range(Y):
            turned = dot(order_ref[...], ref[:, y * rows : (y + 1) * rows].T).astype(BF16)
            there = slice(y * half, (y + 1) * half)

            @pl.when(places[0] == 0)
            def _():
                keep_ref[there, columns] = turned[:half]
                send_ref[there, columns] = turned[half:]

            @pl.when(places[0] == 1)
            def _():
                keep_ref[there, columns] = turned[half:]
                send_ref[there, columns] = turned[:half]

    turn(normed_ref, slice(0, tokens))
    whole.wait()
    turn(cotangent, slice(tokens, 2 * tokens))
    first.wait()
    grad_ref[...] = dot(cotangent[...], outer[...], NT).astype(BF16)
    for i, copy in enumerate(copies):
        copy.wait()
        here = slice(i * BLOCK, (i + 1) * BLOCK)
        query_ref[:, here] = dot(normed_ref[...], weight[:, here]).astype(BF16)


def second(normed, cotangent, w_qkv, w_out, core):
    tokens, width = normed.shape
    inner = w_out.shape[0]
    order = row_order(width)
    turned = pltpu.VMEM((width // CORES, 2 * tokens), BF16)
    return pl.pallas_call(
        second_kernel,
        in_specs=[SMEM_SPEC, VMEM_SPEC, VMEM_SPEC, HBM_SPEC, HBM_SPEC, HBM_SPEC],
        out_specs=[VMEM_SPEC] * 4,
        out_shape=[pltpu.VMEM((tokens, inner), BF16), pltpu.VMEM((tokens, inner), BF16), turned, turned],
        scratch_shapes=[
            pltpu.VMEM((tokens, width), BF16),
            pltpu.VMEM((width, inner), BF16),
            pltpu.VMEM((inner, width), BF16),
            pltpu.SemaphoreType.DMA,
            pltpu.SemaphoreType.DMA((inner // BLOCK,)),
            pltpu.SemaphoreType.DMA,
        ],
        compiler_params=params(24),
        cost_estimate=cost(8 * tokens * width * inner, 8 * inner * width),
        name="second",
    )(jnp.reshape(core, (1,)), in_vmem(order), normed, in_hbm(cotangent), in_hbm(w_qkv), in_hbm(w_out))


def attend(begin, length, inner, operands, results):
    lane = lax.broadcasted_iota(jnp.int32, (CONTEXT, PAIR), 1)
    heads = (lane < HEAD_DIM, lane >= HEAD_DIM)
    row_valid = begin + lax.broadcasted_iota(jnp.int32, (CONTEXT, PAIR), 0) < length
    col_valid = begin + lane < length
    keys = lax.broadcasted_iota(jnp.int32, (2 * CONTEXT, 2 * CONTEXT), 0)
    queries = lax.broadcasted_iota(jnp.int32, (2 * CONTEXT, 2 * CONTEXT), 1)
    key_block = keys // GROUP
    query_block = (queries % CONTEXT) // GROUP
    key_place = begin - CONTEXT + keys
    seen = (key_block >= query_block) & (key_block <= query_block + LEFT) & (key_place >= 0) & (key_place < length)
    zero = jnp.zeros((CONTEXT, PAIR), BF16)
    scale = HEAD_DIM ** (-0.5)

    def unstack(both):
        return jnp.concatenate([both[:HEAD_DIM, :CONTEXT], both[HEAD_DIM:, CONTEXT:]], axis=0)

    for pair in range(inner // PAIR):
        q, k2, v2, do = operands(pair)
        do = jnp.where(row_valid, do, zero)
        q = q * jnp.asarray(scale, BF16)
        q2 = jnp.concatenate([jnp.where(h, q, zero) for h in heads], axis=0)
        do2 = jnp.concatenate([jnp.where(h, do, zero) for h in heads], axis=0)
        scores = jnp.where(seen, dot(k2, q2, NT), -1e30)
        dprob = dot(v2, do2, NT)
        highest = jnp.max(scores, axis=0, keepdims=True)
        raised = jnp.exp(scores - highest)
        prob = raised * (1.0 / jnp.sum(raised, axis=0, keepdims=True))
        rounded = prob.astype(BF16)
        mixed = jnp.where(col_valid, unstack(dot(v2.T, rounded)), 0.0).T.astype(BF16)
        weighed = prob * dprob
        dscores = (weighed - prob * jnp.sum(weighed, axis=0, keepdims=True)).astype(BF16)
        dq = (unstack(dot(k2.T, dscores)) * scale).T.astype(BF16)
        results(pair, mixed, dq, dot(dscores, q2), dot(rounded, do2))


def late_kernel(places, q_ref, kv_ref, do_ref, out_ref, head_ref, tail_ref):
    inner = q_ref.shape[1]

    def operands(pair):
        at = slice(pair * PAIR, (pair + 1) * PAIR)
        return q_ref[CONTEXT:, at], kv_ref[:, at], kv_ref[:, slice(inner + at.start, inner + at.stop)], do_ref[CONTEXT:, at]

    def results(pair, mixed, dq, dk, dv):
        at = slice(pair * PAIR, (pair + 1) * PAIR)
        out_ref[0, :, at] = mixed
        out_ref[1, :, at] = dq
        for n, grad in enumerate((dk, dv)):
            head_ref[n, :, at] = grad[:CONTEXT]
            tail_ref[n, :, at] = grad[CONTEXT:]

    attend(places[1] + CONTEXT, places[0], inner, operands, results)


def early_kernel(places, q_ref, kv_ref, halo_ref, do_ref, late_ref, add_ref, out_ref, head_ref, back_ref):
    inner = q_ref.shape[1]
    out_ref[:, CONTEXT:, :] = late_ref[...]

    def operands(pair):
        at = slice(pair * PAIR, (pair + 1) * PAIR)
        v_at = slice(inner + at.start, inner + at.stop)
        k2 = jnp.concatenate([halo_ref[:, at], kv_ref[:CONTEXT, at]], axis=0)
        v2 = jnp.concatenate([halo_ref[:, v_at], kv_ref[:CONTEXT, v_at]], axis=0)
        return q_ref[:CONTEXT, at], k2, v2, do_ref[:CONTEXT, at]

    def results(pair, mixed, dq, dk, dv):
        at = slice(pair * PAIR, (pair + 1) * PAIR)
        out_ref[0, :CONTEXT, at] = mixed
        out_ref[1, :CONTEXT, at] = dq
        for n, grad in enumerate((dk, dv)):
            back_ref[n, :, at] = grad[:CONTEXT].astype(BF16)
            head_ref[n, :, at] = (grad[CONTEXT:] + add_ref[n, :, at]).astype(BF16)

    attend(places[1], places[0], inner, operands, results)


def join_kernel(head_ref, tail_ref, back_ref, out_ref):
    out_ref[:, :CONTEXT, :] = head_ref[...]
    out_ref[:, CONTEXT:, :] = (tail_ref[...] + back_ref[...].astype(F32)).astype(BF16)


def join(head, tail, back):
    return pl.pallas_call(
        join_kernel,
        in_specs=[VMEM_SPEC] * 3,
        out_specs=VMEM_SPEC,
        out_shape=pltpu.VMEM((2, 2 * CONTEXT, head.shape[2]), BF16),
        compiler_params=params(8),
        cost_estimate=cost(1, 1),
        name="join",
    )(*[in_vmem(o) for o in (head, tail, back)])


def attention(kernel, places, operands, inner, rows, types, name):
    return pl.pallas_call(
        kernel,
        in_specs=[SMEM_SPEC] + [VMEM_SPEC] * len(operands),
        out_specs=[VMEM_SPEC] * len(types),
        out_shape=[pltpu.VMEM((2, n, inner), dtype) for n, dtype in zip(rows, types)],
        compiler_params=params(24),
        cost_estimate=cost(28 * CONTEXT * 2 * CONTEXT * inner, 16 * CONTEXT * inner, CONTEXT * 4 * inner),
        name=name,
    )(places, *[in_vmem(o) for o in operands])


def weight_kernel(lefts, chunks, left_ref, left_other_ref, right_ref, right_other_ref, *refs):
    outs, held = refs[:-1], refs[-1]
    tokens = right_ref.shape[1]
    columns = right_ref.shape[2] // 2
    half = CHUNKS // 2
    for n, left in enumerate(lefts):
        at = slice(left * tokens, (left + 1) * tokens)
        total = dot(left_ref[:, at], right_ref[n]) + dot(left_other_ref[:, at], right_other_ref[n])
        for part in range(2):
            route = 2 * n + part
            held[route] = total[:, part * columns : (part + 1) * columns].reshape(held.shape[1:])
            for slot in range(CHUNKS):
                ref = outs[route] if slot < half else outs[len(ROUTES) + route]
                ref[slot % half] = held[route, chunks[route, slot]].astype(BF16)


def weight_sections(chunks, left, left_other, lefts, right, right_other):
    rows = left.shape[0]
    tokens = right.shape[1]
    columns = right.shape[2] // 2
    routes = len(ROUTES)
    out = pltpu.VMEM((CHUNKS // 2, rows // CHUNKS, columns), BF16)
    outs = pl.pallas_call(
        lambda *refs: weight_kernel(lefts, *refs),
        in_specs=[SMEM_SPEC] + [VMEM_SPEC] * 4,
        out_specs=[VMEM_SPEC] * (2 * routes),
        out_shape=[out] * (2 * routes),
        scratch_shapes=[pltpu.VMEM((routes, CHUNKS, rows // CHUNKS, columns), F32)],
        compiler_params=params(24),
        cost_estimate=cost(1, 1),
        name="weight_sections",
    )(chunks, *[in_vmem(o) for o in (left, left_other, right, right_other)])
    return outs[:routes], outs[routes:]


def plus(*terms):
    return sum(t.astype(F32) for t in terms).astype(BF16)


def pieces_kernel(*refs):
    ins, out_ref, held = refs[:-2], refs[-2], refs[-1]
    for group, ref in enumerate(ins):
        block = ref[...].astype(F32)
        width = block.shape[1] // PAIR // 4
        share = block.shape[0] // Z
        for n in (2 * group, 2 * group + 1):
            bases = (((n + 2) % 4) * width + (0 if n > 1 else 4 * width), (2 + n) * width)
            for wave, base in enumerate(bases):
                for t in range(width):
                    column = (((n % 2) * 2 + wave) * width + t) * PAIR
                    for z in range(Z):
                        rows = slice((base + t) * share, (base + t + 1) * share)
                        held[z, rows, :] = block[z * share : (z + 1) * share, column : column + PAIR]
    out_ref[...] = held[...].astype(BF16)


def total_kernel(in_ref, out_ref):
    total = in_ref[0].astype(F32)
    for z in range(1, Z):
        total += in_ref[z].astype(F32)
    share = out_ref.shape[0]
    for t in range(out_ref.shape[1] // PAIR):
        out_ref[:, t * PAIR : (t + 1) * PAIR] = total[t * share : (t + 1) * share]


def on_device(frames, cotangent, lengths, w_qkv, w_out):
    frame_rows = frames[0]
    grad_rows = cotangent[0]
    row_count, width = frame_rows.shape
    inner = w_out.shape[0]
    seq_index = lax.axis_index("seq")
    dp_index = lax.axis_index("dp")
    xl = seq_index % XL
    core, xh, y = dp_index % CORES, dp_index // CORES % XH, dp_index // (CORES * XH)
    places = jnp.stack([lengths[0], seq_index * row_count])
    routes = range(len(ROUTES))
    chunks = jnp.stack([jnp.stack([chunk_at(r, slot, y, xh, xl) for slot in range(CHUNKS)]) for r in routes])

    frame_rows, places, chunks = lax.optimization_barrier((frame_rows, places, chunks))
    normed, keys, tail, stats = project(frame_rows, w_qkv)
    received = from_behind(tail, "seq", 1)
    queries, attended_grad, left, left_out = second(normed, grad_rows, w_qkv, w_out, core)
    left_other = to_device(left_out, to_core)
    late, late_head, late_tail = attention(
        late_kernel, places, (queries, keys, attended_grad), inner, (CONTEXT,) * 3, (BF16, F32, F32), "attention_late"
    )
    own, kv_head, halo = attention(
        early_kernel,
        places,
        (queries, keys, received, attended_grad, late, late_head),
        inner,
        (row_count, CONTEXT, CONTEXT),
        (BF16,) * 3,
        "attention_early",
    )
    returned = from_behind(halo, "seq", -1)
    own_other = to_device(own, to_core)
    keep_a, send_a = weight_sections(chunks, left, left_other, (1, 0), own, own_other)
    attended, send_a = lax.optimization_barrier((own[0], send_a))
    block_out = dot(attended, w_out).astype(BF16)
    block_out, late_tail = lax.optimization_barrier((block_out, late_tail))
    got_a = [None] + [to_device(send_a[r], ROUTES[r][0]) for r in routes[1:]]
    got_a[1], got_a[2], late_tail = lax.optimization_barrier((got_a[1], got_a[2], late_tail))

    kv_total, send_first = lax.optimization_barrier((join(kv_head, late_tail, returned), send_a[0]))
    got_a[0] = to_device(send_first, ROUTES[0][0])
    kv_other = to_device(kv_total, to_core)
    keep_b, send_b = weight_sections(chunks, left, left_other, (0, 0), kv_total, kv_other)
    projected_grad = jnp.concatenate([own[1], kv_total[0], kv_total[1]], axis=1)
    got_b = [to_device(send_b[r], ROUTES[r][0]) for r in routes]

    totals = [
        jnp.concatenate([plus(keep_a[r], got_a[r]), plus(keep_b[r], got_b[r])], axis=-1) for r in routes
    ]
    count = totals[0].shape[0] // 2
    sends = [t[count:] for t in totals]
    projected_grad, frame_rows, stats, sends = lax.optimization_barrier((projected_grad, frame_rows, stats, sends))
    normed_grad = dot(projected_grad, w_qkv, NT).astype(BF16)
    frame_grad = normalize_grad(frame_rows.astype(F32), stats[0][:, None], stats[1][:, None], normed_grad.astype(F32))
    gots = lax.optimization_barrier([to_device(sends[r], ROUTES[r][1]) for r in routes])
    totals = [plus(totals[r][:count], gots[r]) for r in routes]
    groups = [jnp.concatenate(totals[:2], axis=-1), jnp.concatenate(totals[2:], axis=-1)]
    slots = lax.optimization_barrier([[g[slot] for slot in range(1, 4)] for g in groups])
    gots = [[to_device(slots[n][i], OWNERS[n][i]) for n in range(2)] for i in range(3)]
    groups = [plus(groups[n][0], *[gots[i][n] for i in range(3)]) for n in range(2)]
    share = width // (CHUNKS * CORES * Z)
    tiles = 4 * inner // PAIR
    shares = pl.pallas_call(
        pieces_kernel,
        in_specs=[VMEM_SPEC] * 2,
        out_shape=jax.ShapeDtypeStruct((Z, tiles * share, PAIR), BF16),
        scratch_shapes=[pltpu.VMEM((Z, tiles * share, PAIR), F32)],
        compiler_params=params(24),
        name="pieces",
    )(*[in_vmem(g) for g in groups])
    rings = [[place * XL + x for place in range(Z)] for x in range(XL)]
    shares = lax.all_to_all(shares, "seq", 0, 0, axis_index_groups=rings, tiled=True)
    total = pl.pallas_call(
        total_kernel,
        in_specs=[VMEM_SPEC],
        out_shape=jax.ShapeDtypeStruct((share, 4 * inner), F32),
        compiler_params=params(24),
        name="total",
    )(in_vmem(shares))
    return block_out[None], frame_grad.astype(BF16)[None], total


def solution(mesh):
    placed = (P("dp", "seq", None), P("dp", "seq", None), P("dp"), P(), P())
    return jax.shard_map(
        on_device,
        mesh=mesh,
        in_specs=placed,
        out_specs=(P("dp", "seq", None), P("dp", "seq", None), P(("dp", "seq"), None)),
        check_vma=False,
    )
```

```python
import jax
import jax.numpy as jnp
import numpy as np
from jax import lax
from jax.experimental import pallas as pl
from jax.experimental.pallas import tpu as pltpu
from jax.sharding import PartitionSpec as P

HEAD_DIM = 64
GROUP = 32
LEFT = 4
CONTEXT = LEFT * GROUP
PAIR = 2 * HEAD_DIM
F32 = jnp.float32
BF16 = jnp.bfloat16
NT = (((1,), (1,)), ((), ()))
NN = (((1,), (0,)), ((), ()))

Y, XH, CORES, Z, XL = 4, 2, 2, 8, 2
CHUNKS = Y * XH * XL

epsilon = 1e-05


def dot(a, b, dims=NN):
    return lax.dot_general(a, b, dims, preferred_element_type=F32)


def from_behind(value, axis, by):
    peers = lax.axis_size(axis)
    return lax.ppermute(value, axis, [(i, (i + by) % peers) for i in range(peers)])


def flat(y, xh, core, z, xl):
    return ((y * XH + xh) * CORES + core) * (Z * XL) + z * XL + xl


def to_device(value, where):
    pairs = []
    for place in np.ndindex(Y, XH, CORES, Z, XL):
        pairs.append((flat(*place), flat(*where(*place))))
    return lax.ppermute(value, ("dp", "seq"), pairs)


def to_core(y, xh, core, z, xl):
    return y, xh, 1 - core, z, xl


def to_x_near(y, xh, core, z, xl):
    return y, xh, core, z, 1 - xl


def to_x_mirror(y, xh, core, z, xl):
    return y, 1 - xh, core, z, 1 - xl


def to_y_near(y, xh, core, z, xl):
    return y ^ 1, xh, core, z, xl


def to_y_mirror(y, xh, core, z, xl):
    return 3 - y, xh, core, z, xl


def to_x_far(y, xh, core, z, xl):
    return y, 1 - xh, core, z, xl


def to_y_far(y, xh, core, z, xl):
    return y ^ 2, xh, core, z, xl


ROUTES = (
    (to_x_near, to_x_mirror),
    (to_x_mirror, to_x_near),
    (to_y_near, to_y_mirror),
    (to_y_mirror, to_y_near),
)
OWNERS = (
    (to_y_mirror, to_y_near, to_y_far),
    (to_x_mirror, to_x_near, to_x_far),
)


def halves(route, hi, lo):
    return (hi ^ lo, hi) if route % 2 == 0 else (hi, hi ^ lo)


def chunk_at(route, slot, y, xh, xl):
    bits = [(slot >> (3 - i)) & 1 for i in range(4)]
    x_first = route < 2
    x_bits, y_bits = (bits[:2], bits[2:]) if x_first else (bits[2:], bits[:2])
    found = []
    for hi, lo, pair, order in ((y >> 1, y & 1, y_bits, 0 if x_first else route), (xh, xl, x_bits, route if x_first else 0)):
        first, second = halves(order, hi, lo)
        first, second = first ^ pair[0], second ^ pair[1]
        found.append((second, first ^ second) if order % 2 == 0 else (first, first ^ second))
    (yh, yl), (xh_to, xl_to) = found
    return ((yh * 2 + yl) * XH + xh_to) * XL + xl_to


def row_order(width):
    share = width // (CHUNKS * CORES * Z)
    order = np.arange(width // Y).reshape(XH, CORES, Z, XL, share).transpose(1, 0, 3, 2, 4).reshape(-1)
    return jnp.asarray(np.eye(width // Y, dtype=np.float32)[order], BF16)


def statistics(rows_in):
    average = jnp.mean(rows_in, axis=-1, keepdims=True)
    centered = rows_in - average
    variance = jnp.mean(centered * centered, axis=-1, keepdims=True)
    return average, lax.rsqrt(variance + epsilon)


def normalize_grad(rows_in, average, inverse, grad):
    normed = (rows_in - average) * inverse
    along = jnp.mean(grad * normed, axis=-1, keepdims=True)
    return inverse * (grad - jnp.mean(grad, axis=-1, keepdims=True) - normed * along)


SMEM_SPEC = pl.BlockSpec(memory_space=pltpu.SMEM)
VMEM_SPEC = pl.BlockSpec(memory_space=pltpu.VMEM)
HBM_SPEC = pl.BlockSpec(memory_space=pltpu.HBM)


def in_vmem(value):
    return pltpu.with_memory_space_constraint(value, pltpu.VMEM)


def in_hbm(value):
    return pltpu.with_memory_space_constraint(value, pltpu.HBM)


def cost(flops, nbytes, transcendentals=0):
    return pl.CostEstimate(flops=flops, bytes_accessed=nbytes, transcendentals=transcendentals)


def params(mebibytes):
    return pltpu.CompilerParams(vmem_limit_bytes=mebibytes * 2**20)


def turn(ref, order_ref, store):
    rows = order_ref.shape[0]
    half = rows // CORES
    for y in range(Y):
        turned = dot(order_ref[...], ref[:, y * rows : (y + 1) * rows].T).astype(BF16)
        for core in range(CORES):
            store(core, slice(y * half, (y + 1) * half), turned[core * half : (core + 1) * half])


def front_kernel(
    places, order_ref, frames_ref, cotangent_ref, weight_ref, out_ref,
    qkv_ref, grad_ref, keep_ref, send_ref, stats_ref, weight, late_ref, dkv_ref,
    rows, cotangent, outer, normed, sems,
):
    here = places[2]
    tokens = rows.shape[0]
    thirds = weight.shape[1] // 3
    block = [slice(n * thirds, (n + 1) * thirds) for n in range(3)]
    copies = [
        pltpu.make_async_copy(frames_ref, rows, sems.at[0]),
        pltpu.make_async_copy(cotangent_ref, cotangent, sems.at[1]),
        pltpu.make_async_copy(out_ref, outer, sems.at[2]),
    ] + [
        pltpu.make_async_copy(weight_ref.at[:, pl.ds(n * thirds, thirds)], weight.at[:, pl.ds(n * thirds, thirds)], sems.at[3 + n])
        for n in range(3)
    ]
    for copy in copies:
        copy.start()

    def put(columns):
        def store(core, at, values):
            @pl.when(here == core)
            def _():
                keep_ref[at, columns] = values

            @pl.when(here != core)
            def _():
                send_ref[at, columns] = values

        return store

    copies[0].wait()
    values = rows[...].astype(F32)
    average, inverse = statistics(values)
    for n, column in enumerate((average, inverse)):
        stats_ref[n : n + 1, :] = jnp.broadcast_to(column, (tokens, PAIR)).T[:1]
    normed[...] = ((values - average) * inverse).astype(BF16)
    turn(normed, order_ref, put(slice(0, tokens)))
    copies[1].wait()
    turn(cotangent, order_ref, put(slice(tokens, 2 * tokens)))
    copies[2].wait()
    grad_ref[...] = dot(cotangent[...], outer[...], NT).astype(BF16)
    for n in range(3):
        copies[3 + n].wait()
        qkv_ref[:, block[n]] = dot(normed[...], weight[:, block[n]]).astype(BF16)

    inner = thirds

    def operands(pair):
        q, k, v = pair_columns(pair, inner)
        return qkv_ref[CONTEXT:, q], qkv_ref[:, k], qkv_ref[:, v], grad_ref[CONTEXT:, q]

    def results(pair, mixed, dq, dk, dv):
        at = pair_columns(pair, inner)[0]
        late_ref[0, :, at] = mixed
        late_ref[1, :, at] = dq
        dkv_ref[0, :, at] = dk
        dkv_ref[1, :, at] = dv

    attend(places[1] + CONTEXT, places[0], inner, operands, results)


def front(places, frames, cotangent, w_qkv, w_out):
    tokens, width = frames.shape
    inner = w_out.shape[0]
    turned = pltpu.VMEM((width // CORES, 2 * tokens), BF16)
    return pl.pallas_call(
        front_kernel,
        in_specs=[SMEM_SPEC, VMEM_SPEC] + [HBM_SPEC] * 4,
        out_specs=[VMEM_SPEC] * 8,
        out_shape=[
            pltpu.VMEM((tokens, 3 * inner), BF16),
            pltpu.VMEM((tokens, inner), BF16),
            turned,
            turned,
            pltpu.VMEM((2, tokens), F32),
            pltpu.VMEM((width, 3 * inner), BF16),
            pltpu.VMEM((2, CONTEXT, inner), BF16),
            pltpu.VMEM((2, tokens, inner), F32),
        ],
        scratch_shapes=[
            pltpu.VMEM((tokens, width), BF16),
            pltpu.VMEM((tokens, width), BF16),
            pltpu.VMEM((inner, width), BF16),
            pltpu.VMEM((tokens, width), BF16),
            pltpu.SemaphoreType.DMA((6,)),
        ],
        compiler_params=params(24),
        cost_estimate=cost(12 * tokens * width * inner, 10 * inner * width),
        name="front",
    )(places, in_vmem(row_order(width)), *[in_hbm(o) for o in (frames, cotangent, w_qkv, w_out)])


def pair_columns(pair, inner):
    return [slice(n * inner + pair * PAIR, n * inner + (pair + 1) * PAIR) for n in range(3)]


def attend(begin, length, inner, operands, results):
    lane = lax.broadcasted_iota(jnp.int32, (CONTEXT, PAIR), 1)
    heads = (lane < HEAD_DIM, lane >= HEAD_DIM)
    row_valid = begin + lax.broadcasted_iota(jnp.int32, (CONTEXT, PAIR), 0) < length
    col_valid = begin + lane < length
    keys = lax.broadcasted_iota(jnp.int32, (2 * CONTEXT, 2 * CONTEXT), 0)
    queries = lax.broadcasted_iota(jnp.int32, (2 * CONTEXT, 2 * CONTEXT), 1)
    key_block = keys // GROUP
    query_block = (queries % CONTEXT) // GROUP
    key_place = begin - CONTEXT + keys
    seen = (key_block >= query_block) & (key_block <= query_block + LEFT) & (key_place >= 0) & (key_place < length)
    zero = jnp.zeros((CONTEXT, PAIR), BF16)
    scale = HEAD_DIM ** (-0.5)

    def unstack(both):
        return jnp.concatenate([both[:HEAD_DIM, :CONTEXT], both[HEAD_DIM:, CONTEXT:]], axis=0)

    for pair in range(inner // PAIR):
        q, k2, v2, do = operands(pair)
        do = jnp.where(row_valid, do, zero)
        q = q * jnp.asarray(scale, BF16)
        q2 = jnp.concatenate([jnp.where(h, q, zero) for h in heads], axis=0)
        do2 = jnp.concatenate([jnp.where(h, do, zero) for h in heads], axis=0)
        scores = jnp.where(seen, dot(k2, q2, NT), -1e30)
        dprob = dot(v2, do2, NT)
        highest = jnp.max(scores, axis=0, keepdims=True)
        raised = jnp.exp(scores - highest)
        prob = raised * (1.0 / jnp.sum(raised, axis=0, keepdims=True))
        rounded = prob.astype(BF16)
        mixed = jnp.where(col_valid, unstack(dot(v2.T, rounded)), 0.0).T.astype(BF16)
        weighed = prob * dprob
        dscores = (weighed - prob * jnp.sum(weighed, axis=0, keepdims=True)).astype(BF16)
        dq = (unstack(dot(k2.T, dscores)) * scale).T.astype(BF16)
        results(pair, mixed, dq, dot(dscores, q2), dot(rounded, do2))


def early_kernel(places, order_ref, frames_ref, weight_ref, qkv_ref, do_ref, late_ref, add_ref,
                 out_ref, dkv_ref, turned_ref, normed, halo):
    inner = do_ref.shape[1]
    rows = qkv_ref.shape[0]
    here = places[2]
    values = frames_ref[...].astype(F32)
    average, inverse = statistics(values)
    normed[...] = ((values - average) * inverse).astype(BF16)
    halo[...] = dot(normed[...], weight_ref[:, inner:]).astype(BF16)
    out_ref[:, CONTEXT:, :] = late_ref[...]
    dkv_ref[:, CONTEXT:rows, :inner] = add_ref[:, CONTEXT:, :].astype(BF16)

    def store(core, at, values):
        @pl.when(here == core)
        def _():
            turned_ref[at, :] = values

        @pl.when(here != core)
        def _():
            half = dkv_ref.shape[1]
            for n in range(2):
                first, last = max(at.start, n * half), min(at.stop, (n + 1) * half)
                if first < last:
                    dkv_ref[n, first - n * half : last - n * half, inner:] = values[first - at.start : last - at.start]

    turn(normed, order_ref, store)

    def operands(pair):
        q, k, v = pair_columns(pair, inner)
        k2 = jnp.concatenate([halo[:, q], qkv_ref[:CONTEXT, k]], axis=0)
        v2 = jnp.concatenate([halo[:, k], qkv_ref[:CONTEXT, v]], axis=0)
        return qkv_ref[:CONTEXT, q], k2, v2, do_ref[:CONTEXT, q]

    def results(pair, mixed, dq, dk, dv):
        at = pair_columns(pair, inner)[0]
        out_ref[0, :CONTEXT, at] = mixed
        out_ref[1, :CONTEXT, at] = dq
        for n, grad in enumerate((dk, dv)):
            dkv_ref[n, rows:, at] = grad[:CONTEXT].astype(BF16)
            dkv_ref[n, :CONTEXT, at] = (grad[CONTEXT:] + add_ref[n, :CONTEXT, at]).astype(BF16)

    attend(places[1], places[0], inner, operands, results)


def early_tile(places, frames, weight, qkv, attended_grad, late, late_grad):
    rows, inner = attended_grad.shape
    width = frames.shape[1]
    return pl.pallas_call(
        early_kernel,
        in_specs=[SMEM_SPEC] + [VMEM_SPEC] * 7,
        out_specs=[VMEM_SPEC] * 3,
        out_shape=[
            pltpu.VMEM((2, rows, inner), BF16),
            pltpu.VMEM((2, rows + CONTEXT, inner + CONTEXT), BF16),
            pltpu.VMEM((width // CORES, CONTEXT), BF16),
        ],
        scratch_shapes=[pltpu.VMEM((CONTEXT, width), BF16), pltpu.VMEM((CONTEXT, 2 * inner), BF16)],
        compiler_params=params(16),
        cost_estimate=cost(28 * CONTEXT * 2 * CONTEXT * inner, 16 * CONTEXT * inner, CONTEXT * 4 * inner),
        name="attention_early",
    )(places, in_vmem(row_order(width)), *[in_vmem(o) for o in (frames, weight, qkv, attended_grad, late, late_grad)])


def store_sections(chunks, n, total, outs, held):
    columns = total.shape[1] // 2
    half = CHUNKS // 2
    for part in range(2):
        route = 2 * n + part
        held[route] = total[:, part * columns : (part + 1) * columns].reshape(held.shape[1:])
        for slot in range(CHUNKS):
            ref = outs[route] if slot < half else outs[len(ROUTES) + route]
            ref[slot % half] = held[route, chunks[route, slot]].astype(BF16)


def first_wave_kernel(chunks, left_ref, left_other_ref, right_ref, right_other_ref, *refs):
    tokens = right_ref.shape[1]
    for n, at in enumerate((slice(tokens, 2 * tokens), slice(0, tokens))):
        total = dot(left_ref[:, at], right_ref[n]) + dot(left_other_ref[:, at], right_other_ref[n])
        store_sections(chunks, n, total, refs[:-1], refs[-1])


def second_wave_kernel(chunks, left_ref, left_other_ref, behind_ref, right_ref, right_other_ref, *refs):
    tokens = left_ref.shape[1] // 2
    inner = right_ref.shape[2] - CONTEXT
    behind_other = jnp.concatenate([right_other_ref[n, :, inner:] for n in range(2)], axis=0)
    for n in range(2):
        total = dot(left_ref[:, :tokens], right_ref[n, :tokens, :inner])
        total += dot(left_other_ref[:, :tokens], right_other_ref[n, :tokens, :inner])
        total += dot(behind_ref[...], right_ref[n, tokens:, :inner])
        total += dot(behind_other, right_other_ref[n, tokens:, :inner])
        store_sections(chunks, n, total, refs[:-1], refs[-1])


def weight_sections(kernel, chunks, operands, inner, flops, name):
    size = (operands[0].shape[0] // CHUNKS, inner // 2)
    routes = len(ROUTES)
    outs = pl.pallas_call(
        kernel,
        in_specs=[SMEM_SPEC] + [VMEM_SPEC] * len(operands),
        out_specs=[VMEM_SPEC] * (2 * routes),
        out_shape=[pltpu.VMEM((CHUNKS // 2, *size), BF16)] * (2 * routes),
        scratch_shapes=[pltpu.VMEM((routes, CHUNKS, *size), F32)],
        compiler_params=params(24),
        cost_estimate=cost(flops, 1),
        name=name,
    )(chunks, *[in_vmem(o) for o in operands])
    return outs[:routes], outs[routes:]


def plus(*terms):
    return sum(t.astype(F32) for t in terms).astype(BF16)


def pieces_kernel(*refs):
    ins, out_ref, held = refs[:-2], refs[-2], refs[-1]
    for group, ref in enumerate(ins):
        block = ref[...].astype(F32)
        width = block.shape[1] // PAIR // 4
        share = block.shape[0] // Z
        for n in (2 * group, 2 * group + 1):
            bases = (((n + 2) % 4) * width + (0 if n > 1 else 4 * width), (2 + n) * width)
            for wave, base in enumerate(bases):
                for t in range(width):
                    column = (((n % 2) * 2 + wave) * width + t) * PAIR
                    for z in range(Z):
                        rows = slice((base + t) * share, (base + t + 1) * share)
                        held[z, rows, :] = block[z * share : (z + 1) * share, column : column + PAIR]
    out_ref[...] = held[...].astype(BF16)


def total_kernel(in_ref, out_ref):
    total = in_ref[0].astype(F32)
    for z in range(1, Z):
        total += in_ref[z].astype(F32)
    share = out_ref.shape[0]
    for t in range(out_ref.shape[1] // PAIR):
        out_ref[:, t * PAIR : (t + 1) * PAIR] = total[t * share : (t + 1) * share]


def on_device(frames, cotangent, lengths, w_qkv, w_out):
    frame_rows = frames[0]
    grad_rows = cotangent[0]
    row_count, width = frame_rows.shape
    inner = w_out.shape[0]
    seq_index = lax.axis_index("seq")
    dp_index = lax.axis_index("dp")
    xl = seq_index % XL
    core, xh, y = dp_index % CORES, dp_index // CORES % XH, dp_index // (CORES * XH)
    places = jnp.stack([lengths[0], seq_index * row_count, core])
    routes = range(len(ROUTES))
    chunks = jnp.stack([chunk_at(r, jnp.arange(CHUNKS), y, xh, xl) for r in routes])

    behind = from_behind(frame_rows[row_count - CONTEXT :], "seq", 1)
    frame_rows, places, chunks = lax.optimization_barrier((frame_rows, places, chunks))
    qkv, attended_grad, left, left_out, stats, weight, late, late_grad = front(
        places, frame_rows, grad_rows, w_qkv, w_out
    )
    left_other = to_device(left_out, to_core)
    own, grads, left_behind = early_tile(places, behind, weight, qkv, attended_grad, late, late_grad)
    own_other, left_other, grads = lax.optimization_barrier((to_device(own, to_core), left_other, grads))
    grads_other = to_device(grads, to_core)
    keep_a, send_a = weight_sections(first_wave_kernel, chunks, (left, left_other, own, own_other), inner, 1, "first_wave")
    got_a = [to_device(send_a[r], ROUTES[r][0]) for r in routes]
    keep_b, send_b = weight_sections(
        second_wave_kernel, chunks, (left, left_other, left_behind, grads, grads_other), inner, 3 * 10**9, "second_wave"
    )
    attended, send_b = lax.optimization_barrier((own[0], send_b))
    block_out = dot(attended, w_out).astype(BF16)
    got_b = [to_device(send_b[r], ROUTES[r][0]) for r in routes]

    got_a, got_b = lax.optimization_barrier((got_a, got_b))
    totals = [
        jnp.concatenate([plus(keep_a[r], got_a[r]), plus(keep_b[r], got_b[r])], axis=-1) for r in routes
    ]
    count = totals[0].shape[0] // 2
    projected_grad = jnp.concatenate([own[1], grads[0, :row_count, :inner], grads[1, :row_count, :inner]], axis=1)
    projected_grad, block_out, sends = lax.optimization_barrier(
        (projected_grad, block_out, [t[count:] for t in totals])
    )
    normed_grad = dot(projected_grad, w_qkv, NT)
    gots = lax.optimization_barrier([to_device(sends[r], ROUTES[r][1]) for r in routes])
    totals = [plus(totals[r][:count], gots[r]) for r in routes]
    groups = [jnp.concatenate(totals[:2], axis=-1), jnp.concatenate(totals[2:], axis=-1)]
    slots, grads, normed_grad = lax.optimization_barrier(
        ([[g[slot] for slot in range(1, 4)] for g in groups], grads, normed_grad)
    )
    returned = from_behind(grads[:, row_count:, :inner], "seq", -1)
    gots = [[to_device(slots[n][i], OWNERS[n][i]) for n in range(2)] for i in range(3)]
    groups = [plus(groups[n][0], *[gots[i][n] for i in range(3)]) for n in range(2)]
    returned = jnp.concatenate([jnp.zeros((CONTEXT, inner), BF16), returned[0], returned[1]], axis=1)
    returned = jnp.concatenate([jnp.zeros((row_count - CONTEXT, width), F32), dot(returned, w_qkv, NT)], axis=0)
    normed_grad = (normed_grad + returned).astype(BF16)
    frame_grad = normalize_grad(frame_rows.astype(F32), stats[0][:, None], stats[1][:, None], normed_grad.astype(F32))
    share = width // (CHUNKS * CORES * Z)
    tiles = 4 * inner // PAIR
    shares = pl.pallas_call(
        pieces_kernel,
        in_specs=[VMEM_SPEC] * 2,
        out_shape=jax.ShapeDtypeStruct((Z, tiles * share, PAIR), BF16),
        scratch_shapes=[pltpu.VMEM((Z, tiles * share, PAIR), F32)],
        compiler_params=params(24),
        name="pieces",
    )(*[in_vmem(g) for g in groups])
    rings = [[place * XL + x for place in range(Z)] for x in range(XL)]
    shares = lax.all_to_all(shares, "seq", 0, 0, axis_index_groups=rings, tiled=True)
    total = pl.pallas_call(
        total_kernel,
        in_specs=[VMEM_SPEC],
        out_shape=jax.ShapeDtypeStruct((share, 4 * inner), F32),
        compiler_params=params(24),
        name="total",
    )(in_vmem(shares))
    return block_out[None], frame_grad.astype(BF16)[None], total


def solution(mesh):
    placed = (P("dp", "seq", None), P("dp", "seq", None), P("dp"), P(), P())
    return jax.shard_map(
        on_device,
        mesh=mesh,
        in_specs=placed,
        out_specs=(P("dp", "seq", None), P("dp", "seq", None), P(("dp", "seq"), None)),
        check_vma=False,
    )
```

```python
import jax
import jax.numpy as jnp
import numpy as np
from jax import lax
from jax.experimental import pallas as pl
from jax.experimental.pallas import tpu as pltpu
from jax.sharding import PartitionSpec as P

HEAD_DIM = 64
GROUP = 32
LEFT = 4
CONTEXT = LEFT * GROUP
PAIR = 2 * HEAD_DIM
F32 = jnp.float32
BF16 = jnp.bfloat16
NT = (((1,), (1,)), ((), ()))
NN = (((1,), (0,)), ((), ()))

Y, XH, CORES, Z, XL = 4, 2, 2, 8, 2
CHUNKS = Y * XH * XL

epsilon = 1e-05


def dot(a, b, dims=NN):
    return lax.dot_general(a, b, dims, preferred_element_type=F32)


def from_behind(value, axis, by):
    peers = lax.axis_size(axis)
    return lax.ppermute(value, axis, [(i, (i + by) % peers) for i in range(peers)])


def flat(y, xh, core, z, xl):
    return ((y * XH + xh) * CORES + core) * (Z * XL) + z * XL + xl


def to_device(value, where):
    pairs = []
    for place in np.ndindex(Y, XH, CORES, Z, XL):
        pairs.append((flat(*place), flat(*where(*place))))
    return lax.ppermute(value, ("dp", "seq"), pairs)


def to_core(y, xh, core, z, xl):
    return y, xh, 1 - core, z, xl


def to_x_near(y, xh, core, z, xl):
    return y, xh, core, z, 1 - xl


def to_x_mirror(y, xh, core, z, xl):
    return y, 1 - xh, core, z, 1 - xl


def to_y_near(y, xh, core, z, xl):
    return y ^ 1, xh, core, z, xl


def to_y_mirror(y, xh, core, z, xl):
    return 3 - y, xh, core, z, xl


def to_x_far(y, xh, core, z, xl):
    return y, 1 - xh, core, z, xl


def to_y_far(y, xh, core, z, xl):
    return y ^ 2, xh, core, z, xl


ROUTES = (
    (to_x_near, to_x_mirror),
    (to_x_mirror, to_x_near),
    (to_y_near, to_y_mirror),
    (to_y_mirror, to_y_near),
)
OWNERS = (
    (to_y_mirror, to_y_near, to_y_far),
    (to_x_mirror, to_x_near, to_x_far),
)


def halves(route, hi, lo):
    return (hi ^ lo, hi) if route % 2 == 0 else (hi, hi ^ lo)


def chunk_at(route, slot, y, xh, xl):
    bits = [(slot >> (3 - i)) & 1 for i in range(4)]
    x_first = route < 2
    x_bits, y_bits = (bits[:2], bits[2:]) if x_first else (bits[2:], bits[:2])
    found = []
    for hi, lo, pair, order in ((y >> 1, y & 1, y_bits, 0 if x_first else route), (xh, xl, x_bits, route if x_first else 0)):
        first, second = halves(order, hi, lo)
        first, second = first ^ pair[0], second ^ pair[1]
        found.append((second, first ^ second) if order % 2 == 0 else (first, first ^ second))
    (yh, yl), (xh_to, xl_to) = found
    return ((yh * 2 + yl) * XH + xh_to) * XL + xl_to


def row_order(width):
    share = width // (CHUNKS * CORES * Z)
    order = np.arange(width // Y).reshape(XH, CORES, Z, XL, share).transpose(1, 0, 3, 2, 4).reshape(-1)
    return jnp.asarray(np.eye(width // Y, dtype=np.float32)[order], BF16)


def statistics(rows_in):
    average = jnp.mean(rows_in, axis=-1, keepdims=True)
    centered = rows_in - average
    variance = jnp.mean(centered * centered, axis=-1, keepdims=True)
    return average, lax.rsqrt(variance + epsilon)


def normalize_grad(rows_in, average, inverse, grad):
    normed = (rows_in - average) * inverse
    along = jnp.mean(grad * normed, axis=-1, keepdims=True)
    return inverse * (grad - jnp.mean(grad, axis=-1, keepdims=True) - normed * along)


SMEM_SPEC = pl.BlockSpec(memory_space=pltpu.SMEM)
VMEM_SPEC = pl.BlockSpec(memory_space=pltpu.VMEM)
HBM_SPEC = pl.BlockSpec(memory_space=pltpu.HBM)


def in_vmem(value):
    return pltpu.with_memory_space_constraint(value, pltpu.VMEM)


def in_hbm(value):
    return pltpu.with_memory_space_constraint(value, pltpu.HBM)


def cost(flops, nbytes, transcendentals=0):
    return pl.CostEstimate(flops=flops, bytes_accessed=nbytes, transcendentals=transcendentals)


def params(mebibytes):
    return pltpu.CompilerParams(vmem_limit_bytes=mebibytes * 2**20)


def turn(ref, order_ref, here, store):
    rows = order_ref.shape[0]
    half = rows // CORES
    for y in range(Y):
        turned = dot(order_ref[...], ref[:, y * rows : (y + 1) * rows].T).astype(BF16)
        first, second = turned[:half], turned[half:]
        at = slice(y * half, (y + 1) * half)
        store(at, jnp.where(here == 0, first, second), jnp.where(here == 0, second, first))


def last_rows(frames):
    rows, width = frames.shape

    def kernel(frames_ref, out_ref, sem):
        copy = pltpu.make_async_copy(frames_ref.at[pl.ds(rows - CONTEXT, CONTEXT)], out_ref, sem)
        copy.start()
        copy.wait()

    return pl.pallas_call(
        kernel,
        in_specs=[HBM_SPEC],
        out_specs=VMEM_SPEC,
        out_shape=pltpu.VMEM((CONTEXT, width), BF16),
        scratch_shapes=[pltpu.SemaphoreType.DMA],
        compiler_params=params(4),
        cost_estimate=cost(1, 1),
        name="last_rows",
    )(in_hbm(frames))


def front_kernel(
    places, lengths_ref, order_ref, frames_ref, cotangent_ref, weight_ref, out_ref,
    qkv_ref, grad_ref, keep_ref, send_ref, stats_ref, weight, late_ref, dkv_ref, order,
    length, rows, cotangent, outer, normed, sems,
):
    here = places[1]
    tokens = rows.shape[0]
    thirds = weight.shape[1] // 3
    block = [slice(n * thirds, (n + 1) * thirds) for n in range(3)]
    small = [
        pltpu.make_async_copy(order_ref, order, sems.at[6]),
        pltpu.make_async_copy(lengths_ref, length, sems.at[7]),
    ]
    copies = [
        pltpu.make_async_copy(frames_ref, rows, sems.at[0]),
        pltpu.make_async_copy(cotangent_ref, cotangent, sems.at[1]),
        pltpu.make_async_copy(out_ref, outer, sems.at[2]),
    ] + [
        pltpu.make_async_copy(weight_ref.at[:, pl.ds(n * thirds, thirds)], weight.at[:, pl.ds(n * thirds, thirds)], sems.at[3 + n])
        for n in range(3)
    ]
    for copy in copies[:1] + small + copies[1:]:
        copy.start()

    def put(columns):
        def store(at, own, other):
            keep_ref[at, columns] = own
            send_ref[at, columns] = other

        return store

    copies[0].wait()
    values = rows[...].astype(F32)
    average, inverse = statistics(values)
    for n, column in enumerate((average, inverse)):
        stats_ref[n : n + 1, :] = jnp.broadcast_to(column, (tokens, PAIR)).T[:1]
    normed[...] = ((values - average) * inverse).astype(BF16)
    small[0].wait()
    turn(normed, order, here, put(slice(0, tokens)))
    copies[1].wait()
    turn(cotangent, order, here, put(slice(tokens, 2 * tokens)))
    copies[2].wait()
    grad_ref[...] = dot(cotangent[...], outer[...], NT).astype(BF16)
    for n in range(3):
        copies[3 + n].wait()
    qkv_ref[...] = dot(normed[...], weight[...]).astype(BF16)

    inner = thirds

    def operands(pair):
        q, k, v = pair_columns(pair, inner)
        return qkv_ref[CONTEXT:, q], qkv_ref[:, k], qkv_ref[:, v], grad_ref[CONTEXT:, q]

    def results(pair, mixed, dq, dk, dv):
        at = pair_columns(pair, inner)[0]
        late_ref[0, :, at] = mixed
        late_ref[1, :, at] = dq
        dkv_ref[0, :, at] = dk
        dkv_ref[1, :, at] = dv

    small[1].wait()
    attend(places[0] + CONTEXT, length[0], inner, operands, results)


def front(places, lengths, frames, cotangent, w_qkv, w_out):
    tokens, width = frames.shape
    inner = w_out.shape[0]
    order = row_order(width)
    turned = pltpu.VMEM((width // CORES, 2 * tokens), BF16)
    return pl.pallas_call(
        front_kernel,
        in_specs=[SMEM_SPEC] + [HBM_SPEC] * 6,
        out_specs=[VMEM_SPEC] * 9,
        out_shape=[
            pltpu.VMEM((tokens, 3 * inner), BF16),
            pltpu.VMEM((tokens, inner), BF16),
            turned,
            turned,
            pltpu.VMEM((2, tokens), F32),
            pltpu.VMEM((width, 3 * inner), BF16),
            pltpu.VMEM((2, CONTEXT, inner), BF16),
            pltpu.VMEM((2, tokens, inner), F32),
            pltpu.VMEM(order.shape, BF16),
        ],
        scratch_shapes=[
            pltpu.SMEM((1,), jnp.int32),
            pltpu.VMEM((tokens, width), BF16),
            pltpu.VMEM((tokens, width), BF16),
            pltpu.VMEM((inner, width), BF16),
            pltpu.VMEM((tokens, width), BF16),
            pltpu.SemaphoreType.DMA((8,)),
        ],
        compiler_params=params(24),
        cost_estimate=cost(12 * tokens * width * inner, 10 * inner * width),
        name="front",
    )(places, lengths, *[in_hbm(o) for o in (order, frames, cotangent, w_qkv, w_out)])


def pair_columns(pair, inner):
    return [slice(n * inner + pair * PAIR, n * inner + (pair + 1) * PAIR) for n in range(3)]


def attend(begin, length, inner, operands, results):
    lane = lax.broadcasted_iota(jnp.int32, (CONTEXT, PAIR), 1)
    heads = (lane < HEAD_DIM, lane >= HEAD_DIM)
    row_valid = begin + lax.broadcasted_iota(jnp.int32, (CONTEXT, PAIR), 0) < length
    col_valid = begin + lane < length
    keys = lax.broadcasted_iota(jnp.int32, (2 * CONTEXT, 2 * CONTEXT), 0)
    queries = lax.broadcasted_iota(jnp.int32, (2 * CONTEXT, 2 * CONTEXT), 1)
    key_block = keys // GROUP
    query_block = (queries % CONTEXT) // GROUP
    key_place = begin - CONTEXT + keys
    seen = (key_block >= query_block) & (key_block <= query_block + LEFT) & (key_place >= 0) & (key_place < length)
    zero = jnp.zeros((CONTEXT, PAIR), BF16)
    scale = HEAD_DIM ** (-0.5)

    def unstack(both):
        return jnp.concatenate([both[:HEAD_DIM, :CONTEXT], both[HEAD_DIM:, CONTEXT:]], axis=0)

    for pair in range(inner // PAIR):
        q, k2, v2, do = operands(pair)
        do = jnp.where(row_valid, do, zero)
        q = q * jnp.asarray(scale, BF16)
        q2 = jnp.concatenate([jnp.where(h, q, zero) for h in heads], axis=0)
        do2 = jnp.concatenate([jnp.where(h, do, zero) for h in heads], axis=0)
        scores = jnp.where(seen, dot(k2, q2, NT), -1e30)
        dprob = dot(v2, do2, NT)
        highest = jnp.max(scores, axis=0, keepdims=True)
        raised = jnp.exp(scores - highest)
        prob = raised * (1.0 / jnp.sum(raised, axis=0, keepdims=True))
        rounded = prob.astype(BF16)
        mixed = jnp.where(col_valid, unstack(dot(v2.T, rounded)), 0.0).T.astype(BF16)
        weighed = prob * dprob
        dscores = (weighed - prob * jnp.sum(weighed, axis=0, keepdims=True)).astype(BF16)
        dq = (unstack(dot(k2.T, dscores)) * scale).T.astype(BF16)
        results(pair, mixed, dq, dot(dscores, q2), dot(rounded, do2))


def early_kernel(
    places, lengths_ref, order_ref, frames_ref, weight_ref, qkv_ref, do_ref, late_ref, add_ref,
    out_ref, dkv_ref, turned_ref, length, normed, halo, sem,
):
    fetch = pltpu.make_async_copy(lengths_ref, length, sem)
    fetch.start()
    inner = do_ref.shape[1]
    rows = qkv_ref.shape[0]
    here = places[1]
    values = frames_ref[...].astype(F32)
    average, inverse = statistics(values)
    normed[...] = ((values - average) * inverse).astype(BF16)
    halo[...] = dot(normed[...], weight_ref[:, inner:]).astype(BF16)
    out_ref[:, CONTEXT:, :] = late_ref[...]
    dkv_ref[:, CONTEXT:rows, :inner] = add_ref[:, CONTEXT:, :].astype(BF16)

    def store(at, own, other):
        turned_ref[at, :] = own
        half = dkv_ref.shape[1]
        for n in range(2):
            first, last = max(at.start, n * half), min(at.stop, (n + 1) * half)
            if first < last:
                dkv_ref[n, first - n * half : last - n * half, inner:] = other[first - at.start : last - at.start]

    turn(normed, order_ref, here, store)

    def operands(pair):
        q, k, v = pair_columns(pair, inner)
        k2 = jnp.concatenate([halo[:, q], qkv_ref[:CONTEXT, k]], axis=0)
        v2 = jnp.concatenate([halo[:, k], qkv_ref[:CONTEXT, v]], axis=0)
        return qkv_ref[:CONTEXT, q], k2, v2, do_ref[:CONTEXT, q]

    def results(pair, mixed, dq, dk, dv):
        at = pair_columns(pair, inner)[0]
        out_ref[0, :CONTEXT, at] = mixed
        out_ref[1, :CONTEXT, at] = dq
        for n, grad in enumerate((dk, dv)):
            dkv_ref[n, rows:, at] = grad[:CONTEXT].astype(BF16)
            dkv_ref[n, :CONTEXT, at] = (grad[CONTEXT:] + add_ref[n, :CONTEXT, at]).astype(BF16)

    fetch.wait()
    attend(places[0], length[0], inner, operands, results)


def early_tile(places, lengths, order, frames, weight, qkv, attended_grad, late, late_grad):
    rows, inner = attended_grad.shape
    width = frames.shape[1]
    return pl.pallas_call(
        early_kernel,
        in_specs=[SMEM_SPEC, HBM_SPEC] + [VMEM_SPEC] * 7,
        out_specs=[VMEM_SPEC] * 3,
        out_shape=[
            pltpu.VMEM((2, rows, inner), BF16),
            pltpu.VMEM((2, rows + CONTEXT, inner + CONTEXT), BF16),
            pltpu.VMEM((width // CORES, CONTEXT), BF16),
        ],
        scratch_shapes=[
            pltpu.SMEM((1,), jnp.int32),
            pltpu.VMEM((CONTEXT, width), BF16),
            pltpu.VMEM((CONTEXT, 2 * inner), BF16),
            pltpu.SemaphoreType.DMA,
        ],
        compiler_params=params(16),
        cost_estimate=cost(28 * CONTEXT * 2 * CONTEXT * inner, 16 * CONTEXT * inner, CONTEXT * 4 * inner),
        name="attention_early",
    )(places, lengths, *[in_vmem(o) for o in (order, frames, weight, qkv, attended_grad, late, late_grad)])


def store_sections(chunks, n, total, outs, held):
    columns = total.shape[1] // 2
    half = CHUNKS // 2
    for part in range(2):
        route = 2 * n + part
        held[route] = total[:, part * columns : (part + 1) * columns].reshape(held.shape[1:])
        for slot in range(CHUNKS):
            ref = outs[route] if slot < half else outs[len(ROUTES) + route]
            ref[slot % half] = held[route, chunks[route, slot]].astype(BF16)


def first_own_kernel(left_ref, right_ref, out_ref):
    tokens = right_ref.shape[1]
    out_ref[0] = dot(left_ref[:, tokens:], right_ref[0])
    out_ref[1] = dot(left_ref[:, :tokens], right_ref[1])


def first_own(left, right):
    return pl.pallas_call(
        first_own_kernel,
        in_specs=[VMEM_SPEC] * 2,
        out_specs=VMEM_SPEC,
        out_shape=pltpu.VMEM((2, left.shape[0], right.shape[2]), F32),
        compiler_params=params(8),
        cost_estimate=cost(2 * 10**9, 1),
        name="first_own",
    )(in_vmem(left), in_vmem(right))


def first_wave_kernel(chunks, left_other_ref, right_other_ref, own_ref, *refs):
    tokens = right_other_ref.shape[1]
    for n, at in enumerate((slice(tokens, 2 * tokens), slice(0, tokens))):
        total = own_ref[n] + dot(left_other_ref[:, at], right_other_ref[n])
        store_sections(chunks, n, total, refs[:-1], refs[-1])


def second_wave_kernel(chunks, left_ref, left_other_ref, behind_ref, right_ref, right_other_ref, *refs):
    tokens = left_ref.shape[1] // 2
    inner = right_ref.shape[2] - CONTEXT
    behind_other = jnp.concatenate([right_other_ref[n, :, inner:] for n in range(2)], axis=0)
    left = jnp.concatenate([left_ref[:, :tokens], behind_ref[...], left_other_ref[:, :tokens], behind_other], axis=1)
    for n in range(2):
        total = dot(left, jnp.concatenate([right_ref[n, :, :inner], right_other_ref[n, :, :inner]], axis=0))
        store_sections(chunks, n, total, refs[:-1], refs[-1])


def weight_sections(kernel, chunks, operands, inner, flops, name):
    size = (operands[0].shape[0] // CHUNKS, inner // 2)
    routes = len(ROUTES)
    outs = pl.pallas_call(
        kernel,
        in_specs=[SMEM_SPEC] + [VMEM_SPEC] * len(operands),
        out_specs=[VMEM_SPEC] * (2 * routes),
        out_shape=[pltpu.VMEM((CHUNKS // 2, *size), BF16)] * (2 * routes),
        scratch_shapes=[pltpu.VMEM((routes, CHUNKS, *size), F32)],
        compiler_params=params(24),
        cost_estimate=cost(flops, 1),
        name=name,
    )(chunks, *[in_vmem(o) for o in operands])
    return outs[:routes], outs[routes:]


def plus(*terms):
    return sum(t.astype(F32) for t in terms).astype(BF16)


def pieces_kernel(*refs):
    ins, out_ref, held = refs[:-2], refs[-2], refs[-1]
    for group, ref in enumerate(ins):
        block = ref[...].astype(F32)
        width = block.shape[1] // PAIR // 4
        share = block.shape[0] // Z
        for n in (2 * group, 2 * group + 1):
            bases = (((n + 2) % 4) * width + (0 if n > 1 else 4 * width), (2 + n) * width)
            for wave, base in enumerate(bases):
                for t in range(width):
                    column = (((n % 2) * 2 + wave) * width + t) * PAIR
                    for z in range(Z):
                        rows = slice((base + t) * share, (base + t + 1) * share)
                        held[z, rows, :] = block[z * share : (z + 1) * share, column : column + PAIR]
    out_ref[...] = held[...].astype(BF16)


def total_kernel(in_ref, out_ref):
    total = in_ref[0].astype(F32)
    for z in range(1, Z):
        total += in_ref[z].astype(F32)
    share = out_ref.shape[0]
    for t in range(out_ref.shape[1] // PAIR):
        out_ref[:, t * PAIR : (t + 1) * PAIR] = total[t * share : (t + 1) * share]


def on_device(frames, cotangent, lengths, w_qkv, w_out):
    frame_rows = frames[0]
    grad_rows = cotangent[0]
    row_count, width = frame_rows.shape
    inner = w_out.shape[0]
    seq_index = lax.axis_index("seq")
    dp_index = lax.axis_index("dp")
    xl = seq_index % XL
    core, xh, y = dp_index % CORES, dp_index // CORES % XH, dp_index // (CORES * XH)
    places = jnp.stack([seq_index * row_count, core])
    routes = range(len(ROUTES))
    chunks = jnp.stack([chunk_at(r, jnp.arange(CHUNKS), y, xh, xl) for r in routes])

    behind = from_behind(last_rows(frame_rows), "seq", 1)
    frame_rows, places, chunks = lax.optimization_barrier((frame_rows, places, chunks))
    qkv, attended_grad, left, left_out, stats, weight, late, late_grad, order = front(
        places, lengths, frame_rows, grad_rows, w_qkv, w_out
    )
    left_other = to_device(left_out, to_core)
    own, grads, left_behind = early_tile(places, lengths, order, behind, weight, qkv, attended_grad, late, late_grad)
    own_other = to_device(own, to_core)
    own_sum = first_own(left, own)
    own_other, left_other, own_sum, grads = lax.optimization_barrier((own_other, left_other, own_sum, grads))
    grads_other = to_device(grads, to_core)
    keep_a, send_a = weight_sections(first_wave_kernel, chunks, (left_other, own_other, own_sum), inner, 1, "first_wave")
    got_a = [to_device(send_a[r], ROUTES[r][0]) for r in routes]
    keep_b, send_b = weight_sections(
        second_wave_kernel, chunks, (left, left_other, left_behind, grads, grads_other), inner, 3 * 10**9, "second_wave"
    )
    attended, send_b = lax.optimization_barrier((own[0], send_b))
    block_out = dot(attended, w_out).astype(BF16)
    got_b = [to_device(send_b[r], ROUTES[r][0]) for r in routes]

    got_a, got_b = lax.optimization_barrier((got_a, got_b))
    totals = [
        jnp.concatenate([plus(keep_a[r], got_a[r]), plus(keep_b[r], got_b[r])], axis=-1) for r in routes
    ]
    count = totals[0].shape[0] // 2
    query_grad = jnp.concatenate([own[1], jnp.zeros((CONTEXT, inner), BF16)], axis=0)
    projected_grad = jnp.concatenate([query_grad, grads[0, :, :inner], grads[1, :, :inner]], axis=1)
    sends = [t[count:] for t in totals]
    projected_grad, block_out, sends = lax.optimization_barrier((projected_grad, block_out, sends))
    normed_grad = dot(projected_grad, w_qkv, NT)
    gots = [to_device(sends[r], ROUTES[r][1]) for r in routes]
    groups = []
    for n in range(2):
        pair = [plus(totals[r][:count], gots[r]) for r in (2 * n, 2 * n + 1)]
        group = jnp.concatenate(pair, axis=-1)
        slots = lax.optimization_barrier([group[slot] for slot in range(1, 4)])
        if n == 0:
            slots, normed_grad = lax.optimization_barrier((slots, normed_grad))
        others = [to_device(slots[i], OWNERS[n][i]) for i in range(3)]
        groups.append(plus(group[0], *others))
    returned = from_behind(normed_grad[row_count:].astype(BF16), "seq", -1)
    returned = jnp.concatenate([jnp.zeros((row_count - CONTEXT, width), BF16), returned], axis=0)
    normed_grad = (normed_grad[:row_count] + returned.astype(F32)).astype(BF16)
    frame_grad = normalize_grad(frame_rows.astype(F32), stats[0][:, None], stats[1][:, None], normed_grad.astype(F32))
    share = width // (CHUNKS * CORES * Z)
    tiles = 4 * inner // PAIR
    shares = pl.pallas_call(
        pieces_kernel,
        in_specs=[VMEM_SPEC] * 2,
        out_shape=jax.ShapeDtypeStruct((Z, tiles * share, PAIR), BF16),
        scratch_shapes=[pltpu.VMEM((Z, tiles * share, PAIR), F32)],
        compiler_params=params(24),
        name="pieces",
    )(*[in_vmem(g) for g in groups])
    rings = [[place * XL + x for place in range(Z)] for x in range(XL)]
    shares = lax.all_to_all(shares, "seq", 0, 0, axis_index_groups=rings, tiled=True)
    total = pl.pallas_call(
        total_kernel,
        in_specs=[VMEM_SPEC],
        out_shape=jax.ShapeDtypeStruct((share, 4 * inner), F32),
        compiler_params=params(24),
        name="total",
    )(in_vmem(shares))
    return block_out[None], frame_grad.astype(BF16)[None], total


def solution(mesh):
    placed = (P("dp", "seq", None), P("dp", "seq", None), P("dp"), P(), P())
    return jax.shard_map(
        on_device,
        mesh=mesh,
        in_specs=placed,
        out_specs=(P("dp", "seq", None), P("dp", "seq", None), P(("dp", "seq"), None)),
        check_vma=False,
    )
```

```python
import jax
import jax.numpy as jnp
import numpy as np
from jax import lax
from jax.experimental import pallas as pl
from jax.experimental.pallas import tpu as pltpu
from jax.sharding import PartitionSpec as P

HEAD_DIM = 64
GROUP = 32
LEFT = 4
CONTEXT = LEFT * GROUP
PAIR = 2 * HEAD_DIM
F32 = jnp.float32
BF16 = jnp.bfloat16
NT = (((1,), (1,)), ((), ()))
NN = (((1,), (0,)), ((), ()))

Y, XH, CORES, Z, XL = 4, 2, 2, 8, 2
CHUNKS = Y * XH * XL

epsilon = 1e-05


def dot(a, b, dims=NN):
    return lax.dot_general(a, b, dims, preferred_element_type=F32)


def from_behind(value, axis, by):
    peers = lax.axis_size(axis)
    return lax.ppermute(value, axis, [(i, (i + by) % peers) for i in range(peers)])


def flat(y, xh, core, z, xl):
    return ((y * XH + xh) * CORES + core) * (Z * XL) + z * XL + xl


def to_device(value, where):
    pairs = []
    for place in np.ndindex(Y, XH, CORES, Z, XL):
        pairs.append((flat(*place), flat(*where(*place))))
    return lax.ppermute(value, ("dp", "seq"), pairs)


def to_core(y, xh, core, z, xl):
    return y, xh, 1 - core, z, xl


def to_x_near(y, xh, core, z, xl):
    return y, xh, core, z, 1 - xl


def to_x_mirror(y, xh, core, z, xl):
    return y, 1 - xh, core, z, 1 - xl


def to_y_near(y, xh, core, z, xl):
    return y ^ 1, xh, core, z, xl


def to_y_mirror(y, xh, core, z, xl):
    return 3 - y, xh, core, z, xl


def to_x_far(y, xh, core, z, xl):
    return y, 1 - xh, core, z, xl


def to_y_far(y, xh, core, z, xl):
    return y ^ 2, xh, core, z, xl


ROUTES = (
    (to_x_near, to_x_mirror),
    (to_x_mirror, to_x_near),
    (to_y_near, to_y_mirror),
    (to_y_mirror, to_y_near),
)
OWNERS = (
    (to_y_mirror, to_y_near, to_y_far),
    (to_x_mirror, to_x_near, to_x_far),
)


def halves(route, hi, lo):
    return (hi ^ lo, hi) if route % 2 == 0 else (hi, hi ^ lo)


def chunk_at(route, slot, y, xh, xl):
    bits = [(slot >> (3 - i)) & 1 for i in range(4)]
    x_first = route < 2
    x_bits, y_bits = (bits[:2], bits[2:]) if x_first else (bits[2:], bits[:2])
    found = []
    for hi, lo, pair, order in ((y >> 1, y & 1, y_bits, 0 if x_first else route), (xh, xl, x_bits, route if x_first else 0)):
        first, second = halves(order, hi, lo)
        first, second = first ^ pair[0], second ^ pair[1]
        found.append((second, first ^ second) if order % 2 == 0 else (first, first ^ second))
    (yh, yl), (xh_to, xl_to) = found
    return ((yh * 2 + yl) * XH + xh_to) * XL + xl_to


def row_order(width):
    share = width // (CHUNKS * CORES * Z)
    order = np.arange(width // Y).reshape(XH, CORES, Z, XL, share).transpose(1, 0, 3, 2, 4).reshape(-1)
    return jnp.asarray(np.eye(width // Y, dtype=np.float32)[order], BF16)


def statistics(rows_in):
    average = jnp.mean(rows_in, axis=-1, keepdims=True)
    centered = rows_in - average
    variance = jnp.mean(centered * centered, axis=-1, keepdims=True)
    return average, lax.rsqrt(variance + epsilon)


def normalize_grad(rows_in, average, inverse, grad):
    normed = (rows_in - average) * inverse
    along = jnp.mean(grad * normed, axis=-1, keepdims=True)
    return inverse * (grad - jnp.mean(grad, axis=-1, keepdims=True) - normed * along)


SMEM_SPEC = pl.BlockSpec(memory_space=pltpu.SMEM)
VMEM_SPEC = pl.BlockSpec(memory_space=pltpu.VMEM)
HBM_SPEC = pl.BlockSpec(memory_space=pltpu.HBM)


def in_vmem(value):
    return pltpu.with_memory_space_constraint(value, pltpu.VMEM)


def in_hbm(value):
    return pltpu.with_memory_space_constraint(value, pltpu.HBM)


def cost(flops, nbytes, transcendentals=0):
    return pl.CostEstimate(flops=flops, bytes_accessed=nbytes, transcendentals=transcendentals)


def params(mebibytes):
    return pltpu.CompilerParams(vmem_limit_bytes=mebibytes * 2**20)


def turn(ref, order_ref, here, store):
    rows = order_ref.shape[0]
    half = rows // CORES
    for y in range(Y):
        turned = dot(order_ref[...], ref[:, y * rows : (y + 1) * rows].T).astype(BF16)
        first, second = turned[:half], turned[half:]
        at = slice(y * half, (y + 1) * half)
        store(at, jnp.where(here == 0, first, second), jnp.where(here == 0, second, first))


def last_rows(frames):
    rows, width = frames.shape

    pieces = 8

    def kernel(frames_ref, out_ref, sems):
        size = CONTEXT // pieces
        copies = [
            pltpu.make_async_copy(
                frames_ref.at[pl.ds(rows - CONTEXT + i * size, size)], out_ref.at[pl.ds(i * size, size)], sems.at[i]
            )
            for i in range(pieces)
        ]
        for copy in copies:
            copy.start()
        for copy in copies:
            copy.wait()

    return pl.pallas_call(
        kernel,
        in_specs=[HBM_SPEC],
        out_specs=VMEM_SPEC,
        out_shape=pltpu.VMEM((CONTEXT, width), BF16),
        scratch_shapes=[pltpu.SemaphoreType.DMA((pieces,))],
        compiler_params=params(4),
        cost_estimate=cost(1, 1),
        name="last_rows",
    )(in_hbm(frames))


def front_kernel(
    places, lengths_ref, order_ref, frames_ref, cotangent_ref, weight_ref, out_ref,
    qkv_ref, grad_ref, keep_ref, send_ref, stats_ref, weight, late_ref, dkv_ref, order,
    length, rows, cotangent, outer, normed, sems,
):
    here = places[1]
    tokens = rows.shape[0]
    thirds = weight.shape[1] // 3
    block = [slice(n * thirds, (n + 1) * thirds) for n in range(3)]
    small = [
        pltpu.make_async_copy(order_ref, order, sems.at[6]),
        pltpu.make_async_copy(lengths_ref, length, sems.at[7]),
    ]
    copies = [
        pltpu.make_async_copy(frames_ref, rows, sems.at[0]),
        pltpu.make_async_copy(cotangent_ref, cotangent, sems.at[1]),
        pltpu.make_async_copy(out_ref, outer, sems.at[2]),
    ] + [
        pltpu.make_async_copy(weight_ref.at[:, pl.ds(n * thirds, thirds)], weight.at[:, pl.ds(n * thirds, thirds)], sems.at[3 + n])
        for n in range(3)
    ]
    for copy in copies[:1] + small + copies[1:]:
        copy.start()

    def put(columns):
        def store(at, own, other):
            keep_ref[at, columns] = own
            send_ref[at, columns] = other

        return store

    copies[0].wait()
    values = rows[...].astype(F32)
    average, inverse = statistics(values)
    for n, column in enumerate((average, inverse)):
        stats_ref[n : n + 1, :] = jnp.broadcast_to(column, (tokens, PAIR)).T[:1]
    normed[...] = ((values - average) * inverse).astype(BF16)
    small[0].wait()
    turn(normed, order, here, put(slice(0, tokens)))
    copies[1].wait()
    turn(cotangent, order, here, put(slice(tokens, 2 * tokens)))
    copies[2].wait()
    grad_ref[...] = dot(cotangent[...], outer[...], NT).astype(BF16)
    for n in range(3):
        copies[3 + n].wait()
    qkv_ref[...] = dot(normed[...], weight[...]).astype(BF16)

    inner = thirds

    def operands(pair):
        q, k, v = pair_columns(pair, inner)
        return qkv_ref[CONTEXT:, q], qkv_ref[:, k], qkv_ref[:, v], grad_ref[CONTEXT:, q]

    def results(pair, mixed, dq, dk, dv):
        at = pair_columns(pair, inner)[0]
        late_ref[0, :, at] = mixed
        late_ref[1, :, at] = dq
        dkv_ref[0, :, at] = dk
        dkv_ref[1, :, at] = dv

    small[1].wait()
    attend(places[0] + CONTEXT, length[0], inner, operands, results)


def front(places, lengths, frames, cotangent, w_qkv, w_out):
    tokens, width = frames.shape
    inner = w_out.shape[0]
    order = row_order(width)
    turned = pltpu.VMEM((width // CORES, 2 * tokens), BF16)
    return pl.pallas_call(
        front_kernel,
        in_specs=[SMEM_SPEC] + [HBM_SPEC] * 6,
        out_specs=[VMEM_SPEC] * 9,
        out_shape=[
            pltpu.VMEM((tokens, 3 * inner), BF16),
            pltpu.VMEM((tokens, inner), BF16),
            turned,
            turned,
            pltpu.VMEM((2, tokens), F32),
            pltpu.VMEM((width, 3 * inner), BF16),
            pltpu.VMEM((2, CONTEXT, inner), BF16),
            pltpu.VMEM((2, tokens, inner), F32),
            pltpu.VMEM(order.shape, BF16),
        ],
        scratch_shapes=[
            pltpu.SMEM((1,), jnp.int32),
            pltpu.VMEM((tokens, width), BF16),
            pltpu.VMEM((tokens, width), BF16),
            pltpu.VMEM((inner, width), BF16),
            pltpu.VMEM((tokens, width), BF16),
            pltpu.SemaphoreType.DMA((8,)),
        ],
        compiler_params=params(24),
        cost_estimate=cost(12 * tokens * width * inner, 10 * inner * width),
        name="front",
    )(places, lengths, *[in_hbm(o) for o in (order, frames, cotangent, w_qkv, w_out)])


def pair_columns(pair, inner):
    return [slice(n * inner + pair * PAIR, n * inner + (pair + 1) * PAIR) for n in range(3)]


def attend(begin, length, inner, operands, results):
    lane = lax.broadcasted_iota(jnp.int32, (CONTEXT, PAIR), 1)
    heads = (lane < HEAD_DIM, lane >= HEAD_DIM)
    row_valid = begin + lax.broadcasted_iota(jnp.int32, (CONTEXT, PAIR), 0) < length
    col_valid = begin + lane < length
    keys = lax.broadcasted_iota(jnp.int32, (2 * CONTEXT, 2 * CONTEXT), 0)
    queries = lax.broadcasted_iota(jnp.int32, (2 * CONTEXT, 2 * CONTEXT), 1)
    key_block = keys // GROUP
    query_block = (queries % CONTEXT) // GROUP
    key_place = begin - CONTEXT + keys
    seen = (key_block >= query_block) & (key_block <= query_block + LEFT) & (key_place >= 0) & (key_place < length)
    zero = jnp.zeros((CONTEXT, PAIR), BF16)
    scale = HEAD_DIM ** (-0.5)

    def unstack(both):
        return jnp.concatenate([both[:HEAD_DIM, :CONTEXT], both[HEAD_DIM:, CONTEXT:]], axis=0)

    for pair in range(inner // PAIR):
        q, k2, v2, do = operands(pair)
        do = jnp.where(row_valid, do, zero)
        q = q * jnp.asarray(scale, BF16)
        q2 = jnp.concatenate([jnp.where(h, q, zero) for h in heads], axis=0)
        do2 = jnp.concatenate([jnp.where(h, do, zero) for h in heads], axis=0)
        scores = jnp.where(seen, dot(k2, q2, NT), -1e30)
        dprob = dot(v2, do2, NT)
        highest = jnp.max(scores, axis=0, keepdims=True)
        raised = jnp.exp(scores - highest)
        prob = raised * (1.0 / jnp.sum(raised, axis=0, keepdims=True))
        rounded = prob.astype(BF16)
        mixed = jnp.where(col_valid, unstack(dot(v2.T, rounded)), 0.0).T.astype(BF16)
        weighed = prob * dprob
        dscores = (weighed - prob * jnp.sum(weighed, axis=0, keepdims=True)).astype(BF16)
        dq = (unstack(dot(k2.T, dscores)) * scale).T.astype(BF16)
        results(pair, mixed, dq, dot(dscores, q2), dot(rounded, do2))


def early_kernel(
    places, lengths_ref, order_ref, frames_ref, weight_ref, qkv_ref, do_ref, late_ref, add_ref,
    out_ref, dkv_ref, turned_ref, length, normed, halo, sem,
):
    fetch = pltpu.make_async_copy(lengths_ref, length, sem)
    fetch.start()
    inner = do_ref.shape[1]
    rows = qkv_ref.shape[0]
    here = places[1]
    values = frames_ref[...].astype(F32)
    average, inverse = statistics(values)
    normed[...] = ((values - average) * inverse).astype(BF16)
    halo[...] = dot(normed[...], weight_ref[:, inner:]).astype(BF16)
    out_ref[:, CONTEXT:, :] = late_ref[...]
    dkv_ref[:, CONTEXT:rows, :inner] = add_ref[:, CONTEXT:, :].astype(BF16)

    def store(at, own, other):
        turned_ref[at, :] = own
        half = dkv_ref.shape[1]
        for n in range(2):
            first, last = max(at.start, n * half), min(at.stop, (n + 1) * half)
            if first < last:
                dkv_ref[n, first - n * half : last - n * half, inner:] = other[first - at.start : last - at.start]

    turn(normed, order_ref, here, store)

    def operands(pair):
        q, k, v = pair_columns(pair, inner)
        k2 = jnp.concatenate([halo[:, q], qkv_ref[:CONTEXT, k]], axis=0)
        v2 = jnp.concatenate([halo[:, k], qkv_ref[:CONTEXT, v]], axis=0)
        return qkv_ref[:CONTEXT, q], k2, v2, do_ref[:CONTEXT, q]

    def results(pair, mixed, dq, dk, dv):
        at = pair_columns(pair, inner)[0]
        out_ref[0, :CONTEXT, at] = mixed
        out_ref[1, :CONTEXT, at] = dq
        for n, grad in enumerate((dk, dv)):
            dkv_ref[n, rows:, at] = grad[:CONTEXT].astype(BF16)
            dkv_ref[n, :CONTEXT, at] = (grad[CONTEXT:] + add_ref[n, :CONTEXT, at]).astype(BF16)

    fetch.wait()
    attend(places[0], length[0], inner, operands, results)


def early_tile(places, lengths, order, frames, weight, qkv, attended_grad, late, late_grad):
    rows, inner = attended_grad.shape
    width = frames.shape[1]
    return pl.pallas_call(
        early_kernel,
        in_specs=[SMEM_SPEC, HBM_SPEC] + [VMEM_SPEC] * 7,
        out_specs=[VMEM_SPEC] * 3,
        out_shape=[
            pltpu.VMEM((2, rows, inner), BF16),
            pltpu.VMEM((2, rows + CONTEXT, inner + CONTEXT), BF16),
            pltpu.VMEM((width // CORES, CONTEXT), BF16),
        ],
        scratch_shapes=[
            pltpu.SMEM((1,), jnp.int32),
            pltpu.VMEM((CONTEXT, width), BF16),
            pltpu.VMEM((CONTEXT, 2 * inner), BF16),
            pltpu.SemaphoreType.DMA,
        ],
        compiler_params=params(16),
        cost_estimate=cost(28 * CONTEXT * 2 * CONTEXT * inner, 16 * CONTEXT * inner, CONTEXT * 4 * inner),
        name="attention_early",
    )(places, lengths, *[in_vmem(o) for o in (order, frames, weight, qkv, attended_grad, late, late_grad)])


def store_section(chunks, route, n, total, outs, held):
    half = CHUNKS // 2
    held[n] = total.reshape(held.shape[1:])
    for slot in range(CHUNKS):
        outs[n if slot < half else 2 + n][slot % half] = held[n, chunks[route, slot]].astype(BF16)


def first_own_kernel(left_ref, right_ref, out_ref):
    tokens = right_ref.shape[1]
    out_ref[0] = dot(left_ref[:, tokens:], right_ref[0])
    out_ref[1] = dot(left_ref[:, :tokens], right_ref[1])


def first_own(left, right):
    return pl.pallas_call(
        first_own_kernel,
        in_specs=[VMEM_SPEC] * 2,
        out_specs=VMEM_SPEC,
        out_shape=pltpu.VMEM((2, left.shape[0], right.shape[2]), F32),
        compiler_params=params(8),
        cost_estimate=cost(2 * 10**9, 1),
        name="first_own",
    )(in_vmem(left), in_vmem(right))


def first_wave_kernel(chunks, left_other_ref, right_other_ref, own_ref, *refs):
    tokens = right_other_ref.shape[1]
    for n, at in enumerate((slice(tokens, 2 * tokens), slice(0, tokens))):
        total = own_ref[n] + dot(left_other_ref[:, at], right_other_ref[n])
        store_section(chunks, n, n, total, refs[:-1], refs[-1])


def second_wave_kernel(chunks, left_ref, left_other_ref, behind_ref, right_ref, right_other_ref, *refs):
    tokens = left_ref.shape[1] // 2
    inner = right_ref.shape[2] - CONTEXT
    behind_other = jnp.concatenate([right_other_ref[n, :, inner:] for n in range(2)], axis=0)
    left = jnp.concatenate([left_ref[:, :tokens], behind_ref[...], left_other_ref[:, :tokens], behind_other], axis=1)
    for n in range(2):
        total = dot(left, jnp.concatenate([right_ref[n, :, :inner], right_other_ref[n, :, :inner]], axis=0))
        store_section(chunks, 2 + n, n, total, refs[:-1], refs[-1])


def weight_sections(kernel, chunks, operands, inner, flops, name):
    size = (operands[0].shape[0] // CHUNKS, inner)
    routes = 2
    outs = pl.pallas_call(
        kernel,
        in_specs=[SMEM_SPEC] + [VMEM_SPEC] * len(operands),
        out_specs=[VMEM_SPEC] * (2 * routes),
        out_shape=[pltpu.VMEM((CHUNKS // 2, *size), BF16)] * (2 * routes),
        scratch_shapes=[pltpu.VMEM((routes, CHUNKS, *size), F32)],
        compiler_params=params(24),
        cost_estimate=cost(flops, 1),
        name=name,
    )(chunks, *[in_vmem(o) for o in operands])
    return outs[:routes], outs[routes:]


def plus(*terms):
    return sum(t.astype(F32) for t in terms).astype(BF16)


def halve_kernel(*refs):
    for route in range(2):
        keep, got, kept, sent = refs[route::2]
        count = kept.shape[0]
        for ref, at in ((kept, slice(0, count)), (sent, slice(count, 2 * count))):
            ref[...] = (keep[at].astype(F32) + got[at].astype(F32)).astype(BF16)


def halve(keep, gots):
    count, *size = keep[0].shape
    outs = pl.pallas_call(
        halve_kernel,
        in_specs=[VMEM_SPEC] * 4,
        out_specs=[VMEM_SPEC] * 4,
        out_shape=[pltpu.VMEM((count // 2, *size), BF16)] * 4,
        compiler_params=params(8),
        cost_estimate=cost(1, 1),
        name="halve",
    )(*[in_vmem(o) for o in (*keep, *gots)])
    return outs[:2], outs[2:]


def pieces_kernel(*refs):
    ins, out_ref, held = refs[:-2], refs[-2], refs[-1]
    for ref, places in zip(ins, ((3, 0), (1, 2))):
        block = ref[...].astype(F32)
        tiles = block.shape[1] // PAIR // 2
        share = block.shape[0] // Z
        for n, place in enumerate(places):
            for t in range(tiles):
                rows = slice((place * tiles + t) * share, (place * tiles + t + 1) * share)
                column = (n * tiles + t) * PAIR
                for z in range(Z):
                    held[z, rows, :] = block[z * share : (z + 1) * share, column : column + PAIR]
    out_ref[...] = held[...].astype(BF16)


def total_kernel(in_ref, out_ref):
    total = in_ref[0].astype(F32)
    for z in range(1, Z):
        total += in_ref[z].astype(F32)
    share = out_ref.shape[0]
    for t in range(out_ref.shape[1] // PAIR):
        out_ref[:, t * PAIR : (t + 1) * PAIR] = total[t * share : (t + 1) * share]


def on_device(frames, cotangent, lengths, w_qkv, w_out):
    frame_rows = frames[0]
    grad_rows = cotangent[0]
    row_count, width = frame_rows.shape
    inner = w_out.shape[0]
    seq_index = lax.axis_index("seq")
    dp_index = lax.axis_index("dp")
    xl = seq_index % XL
    core, xh, y = dp_index % CORES, dp_index // CORES % XH, dp_index // (CORES * XH)
    places = jnp.stack([seq_index * row_count, core])
    chunks = jnp.stack([chunk_at(r, jnp.arange(CHUNKS), y, xh, xl) for r in range(len(ROUTES))])

    behind = from_behind(last_rows(frame_rows), "seq", 1)
    frame_rows, places, chunks = lax.optimization_barrier((frame_rows, places, chunks))
    qkv, attended_grad, left, left_out, stats, weight, late, late_grad, order = front(
        places, lengths, frame_rows, grad_rows, w_qkv, w_out
    )
    left_other = to_device(left_out, to_core)
    own, grads, left_behind = early_tile(places, lengths, order, behind, weight, qkv, attended_grad, late, late_grad)
    own_other = to_device(own, to_core)
    own_sum = first_own(left, own)
    own_other, left_other, own_sum, grads = lax.optimization_barrier((own_other, left_other, own_sum, grads))
    grads_other = to_device(grads, to_core)
    keep_a, send_a = weight_sections(first_wave_kernel, chunks, (left_other, own_other, own_sum), inner, 1, "first_wave")
    keep_b, send_b = weight_sections(
        second_wave_kernel, chunks, (left, left_other, left_behind, grads, grads_other), inner, 3 * 10**9, "second_wave"
    )
    query_grad = jnp.concatenate([own[1], jnp.zeros((CONTEXT, inner), BF16)], axis=0)
    projected_grad = jnp.concatenate([query_grad, grads[0, :, :inner], grads[1, :, :inner]], axis=1)
    attended, projected_grad, send_b = lax.optimization_barrier((own[0], projected_grad, send_b))
    block_out = dot(attended, w_out).astype(BF16)
    def second_ring(kept, gots, n, *after):
        group = jnp.concatenate([plus(kept[r], gots[r]) for r in range(2)], axis=-1)
        slots, *after = lax.optimization_barrier(([group[slot] for slot in range(1, 4)], *after))
        others = [to_device(slots[i], OWNERS[n][i]) for i in range(3)]
        return plus(group[0], *others), *after

    gots_a = [to_device(send_a[r], ROUTES[r][0]) for r in range(2)]
    gots_b = [to_device(send_b[r], ROUTES[2 + r][0]) for r in range(2)]
    gots_a, block_out = lax.optimization_barrier((gots_a, block_out))
    kept_a, sent_a = halve(keep_a, gots_a)
    gots_a = [to_device(sent_a[r], ROUTES[r][1]) for r in range(2)]
    kept_b, sent_b = halve(keep_b, gots_b)
    projected_grad, sent_b = lax.optimization_barrier((projected_grad, sent_b))
    gots_b = [to_device(sent_b[r], ROUTES[2 + r][1]) for r in range(2)]
    normed_grad = dot(projected_grad, w_qkv, NT)
    gots_a, normed_grad = lax.optimization_barrier((gots_a, normed_grad))
    first_group, = second_ring(kept_a, gots_a, 0)
    second_group, normed_grad = second_ring(kept_b, gots_b, 1, normed_grad)
    groups = [first_group, second_group]
    returned = from_behind(normed_grad[row_count:].astype(BF16), "seq", -1)
    returned = jnp.concatenate([jnp.zeros((row_count - CONTEXT, width), BF16), returned], axis=0)
    normed_grad = (normed_grad[:row_count] + returned.astype(F32)).astype(BF16)
    frame_grad = normalize_grad(frame_rows.astype(F32), stats[0][:, None], stats[1][:, None], normed_grad.astype(F32))
    share = width // (CHUNKS * CORES * Z)
    tiles = 4 * inner // PAIR
    shares = pl.pallas_call(
        pieces_kernel,
        in_specs=[VMEM_SPEC] * 2,
        out_shape=jax.ShapeDtypeStruct((Z, tiles * share, PAIR), BF16),
        scratch_shapes=[pltpu.VMEM((Z, tiles * share, PAIR), F32)],
        compiler_params=params(24),
        name="pieces",
    )(*[in_vmem(g) for g in groups])
    rings = [[place * XL + x for place in range(Z)] for x in range(XL)]
    shares = lax.all_to_all(shares, "seq", 0, 0, axis_index_groups=rings, tiled=True)
    total = pl.pallas_call(
        total_kernel,
        in_specs=[VMEM_SPEC],
        out_shape=jax.ShapeDtypeStruct((share, 4 * inner), F32),
        compiler_params=params(24),
        name="total",
    )(in_vmem(shares))
    return block_out[None], frame_grad.astype(BF16)[None], total


def solution(mesh):
    placed = (P("dp", "seq", None), P("dp", "seq", None), P("dp"), P(), P())
    return jax.shard_map(
        on_device,
        mesh=mesh,
        in_specs=placed,
        out_specs=(P("dp", "seq", None), P("dp", "seq", None), P(("dp", "seq"), None)),
        check_vma=False,
    )
```

```python
import jax
import jax.numpy as jnp
import numpy as np
from jax import lax
from jax.experimental import pallas as pl
from jax.experimental.pallas import tpu as pltpu
from jax.sharding import PartitionSpec as P

HEAD_DIM = 64
GROUP = 32
LEFT = 4
CONTEXT = LEFT * GROUP
PAIR = 2 * HEAD_DIM
F32 = jnp.float32
BF16 = jnp.bfloat16
NT = (((1,), (1,)), ((), ()))
NN = (((1,), (0,)), ((), ()))

Y, XH, CORES, Z, XL = 4, 2, 2, 8, 2
CHUNKS = Y * XH * XL

epsilon = 1e-05


def dot(a, b, dims=NN):
    return lax.dot_general(a, b, dims, preferred_element_type=F32)


def from_behind(value, axis, by):
    peers = lax.axis_size(axis)
    return lax.ppermute(value, axis, [(i, (i + by) % peers) for i in range(peers)])


def flat(y, xh, core, z, xl):
    return ((y * XH + xh) * CORES + core) * (Z * XL) + z * XL + xl


def to_device(value, where):
    pairs = []
    for place in np.ndindex(Y, XH, CORES, Z, XL):
        pairs.append((flat(*place), flat(*where(*place))))
    return lax.ppermute(value, ("dp", "seq"), pairs)


def to_core(y, xh, core, z, xl):
    return y, xh, 1 - core, z, xl


def to_x_near(y, xh, core, z, xl):
    return y, xh, core, z, 1 - xl


def to_x_mirror(y, xh, core, z, xl):
    return y, 1 - xh, core, z, 1 - xl


def to_y_near(y, xh, core, z, xl):
    return y ^ 1, xh, core, z, xl


def to_y_mirror(y, xh, core, z, xl):
    return 3 - y, xh, core, z, xl


def to_x_far(y, xh, core, z, xl):
    return y, 1 - xh, core, z, xl


def to_y_far(y, xh, core, z, xl):
    return y ^ 2, xh, core, z, xl


def along_z(step):
    return lambda y, xh, core, z, xl: (y, xh, core, (z + step) % Z, xl)


ROUTES = (
    (to_y_near, to_y_mirror),
    (to_y_mirror, to_y_near),
    (to_x_near, to_x_mirror),
    (to_x_mirror, to_x_near),
)
OWNERS = (
    (to_x_mirror, to_x_near, to_x_far),
    (to_y_mirror, to_y_near, to_y_far),
)


def halves(route, hi, lo):
    return (hi ^ lo, hi) if route % 2 == 0 else (hi, hi ^ lo)


def chunk_at(route, slot, y, xh, xl):
    bits = [(slot >> (3 - i)) & 1 for i in range(4)]
    x_first = route >= 2
    x_bits, y_bits = (bits[:2], bits[2:]) if x_first else (bits[2:], bits[:2])
    found = []
    for hi, lo, pair, order in ((y >> 1, y & 1, y_bits, 0 if x_first else route), (xh, xl, x_bits, route if x_first else 0)):
        first, second = halves(order, hi, lo)
        first, second = first ^ pair[0], second ^ pair[1]
        found.append((second, first ^ second) if order % 2 == 0 else (first, first ^ second))
    (yh, yl), (xh_to, xl_to) = found
    return ((yh * 2 + yl) * XH + xh_to) * XL + xl_to


def row_order(width):
    share = width // (CHUNKS * CORES * Z)
    order = np.arange(width // Y).reshape(XH, CORES, Z, XL, share).transpose(1, 0, 3, 2, 4).reshape(-1)
    return jnp.asarray(np.eye(width // Y, dtype=np.float32)[order], BF16)


def statistics(rows_in):
    average = jnp.mean(rows_in, axis=-1, keepdims=True)
    centered = rows_in - average
    variance = jnp.mean(centered * centered, axis=-1, keepdims=True)
    return average, lax.rsqrt(variance + epsilon)


SMEM_SPEC = pl.BlockSpec(memory_space=pltpu.SMEM)
VMEM_SPEC = pl.BlockSpec(memory_space=pltpu.VMEM)
HBM_SPEC = pl.BlockSpec(memory_space=pltpu.HBM)


def in_vmem(value):
    return pltpu.with_memory_space_constraint(value, pltpu.VMEM)


def in_hbm(value):
    return pltpu.with_memory_space_constraint(value, pltpu.HBM)


def cost(flops, nbytes, transcendentals=0):
    return pl.CostEstimate(flops=flops, bytes_accessed=nbytes, transcendentals=transcendentals)


def params(mebibytes):
    return pltpu.CompilerParams(vmem_limit_bytes=mebibytes * 2**20)


def turn(ref, order_ref, here, store):
    rows = order_ref.shape[0]
    half = rows // CORES
    for y in range(Y):
        turned = dot(order_ref[...], ref[:, y * rows : (y + 1) * rows].T).astype(BF16)
        first, second = turned[:half], turned[half:]
        at = slice(y * half, (y + 1) * half)
        store(at, jnp.where(here == 0, first, second), jnp.where(here == 0, second, first))


def last_rows(frames):
    rows, width = frames.shape

    pieces = 8

    def kernel(frames_ref, out_ref, sems):
        size = CONTEXT // pieces
        copies = [
            pltpu.make_async_copy(
                frames_ref.at[pl.ds(rows - CONTEXT + i * size, size)], out_ref.at[pl.ds(i * size, size)], sems.at[i]
            )
            for i in range(pieces)
        ]
        for copy in copies:
            copy.start()
        for copy in copies:
            copy.wait()

    return pl.pallas_call(
        kernel,
        in_specs=[HBM_SPEC],
        out_specs=VMEM_SPEC,
        out_shape=pltpu.VMEM((CONTEXT, width), BF16),
        scratch_shapes=[pltpu.SemaphoreType.DMA((pieces,))],
        compiler_params=params(4),
        cost_estimate=cost(1, 1),
        name="last_rows",
    )(in_hbm(frames))


def front_kernel(
    places, lengths_ref, order_ref, frames_ref, cotangent_ref, weight_ref, out_ref,
    qkv_ref, grad_ref, keep_ref, send_ref, stats_ref, weight, late_ref, dkv_ref, order,
    length, rows, cotangent, outer, normed, sems,
):
    here = places[1]
    tokens = rows.shape[0]
    thirds = weight.shape[1] // 3
    block = [slice(n * thirds, (n + 1) * thirds) for n in range(3)]
    small = [
        pltpu.make_async_copy(order_ref, order, sems.at[6]),
        pltpu.make_async_copy(lengths_ref, length, sems.at[7]),
    ]
    copies = [
        pltpu.make_async_copy(frames_ref, rows, sems.at[0]),
        pltpu.make_async_copy(cotangent_ref, cotangent, sems.at[1]),
        pltpu.make_async_copy(out_ref, outer, sems.at[2]),
    ] + [
        pltpu.make_async_copy(weight_ref.at[:, pl.ds(n * thirds, thirds)], weight.at[:, pl.ds(n * thirds, thirds)], sems.at[3 + n])
        for n in range(3)
    ]
    for copy in copies[:1] + small + copies[1:]:
        copy.start()

    def put(columns):
        def store(at, own, other):
            keep_ref[at, columns] = own
            send_ref[at, columns] = other

        return store

    copies[0].wait()
    values = rows[...].astype(F32)
    average, inverse = statistics(values)
    for n, column in enumerate((average, inverse)):
        stats_ref[n : n + 1, :] = jnp.broadcast_to(column, (tokens, PAIR)).T[:1]
    normed[...] = ((values - average) * inverse).astype(BF16)
    small[0].wait()
    turn(normed, order, here, put(slice(0, tokens)))
    copies[1].wait()
    turn(cotangent, order, here, put(slice(tokens, 2 * tokens)))
    copies[2].wait()
    grad_ref[...] = dot(cotangent[...], outer[...], NT).astype(BF16)
    for n in range(3):
        copies[3 + n].wait()
    qkv_ref[...] = dot(normed[...], weight[...]).astype(BF16)

    inner = thirds

    def operands(pair):
        q, k, v = pair_columns(pair, inner)
        return qkv_ref[CONTEXT:, q], qkv_ref[:, k], qkv_ref[:, v], grad_ref[CONTEXT:, q]

    def results(pair, mixed, dq, dk, dv):
        at = pair_columns(pair, inner)[0]
        late_ref[0, :, at] = mixed
        late_ref[1, :, at] = dq
        dkv_ref[0, :, at] = dk
        dkv_ref[1, :, at] = dv

    small[1].wait()
    attend(places[0] + CONTEXT, length[0], inner, operands, results)


def front(places, lengths, frames, cotangent, w_qkv, w_out):
    tokens, width = frames.shape
    inner = w_out.shape[0]
    order = row_order(width)
    turned = pltpu.VMEM((width // CORES, 2 * tokens), BF16)
    return pl.pallas_call(
        front_kernel,
        in_specs=[SMEM_SPEC] + [HBM_SPEC] * 6,
        out_specs=[VMEM_SPEC] * 9,
        out_shape=[
            pltpu.VMEM((tokens, 3 * inner), BF16),
            pltpu.VMEM((tokens, inner), BF16),
            turned,
            turned,
            pltpu.VMEM((2, tokens), F32),
            pltpu.VMEM((width, 3 * inner), BF16),
            pltpu.VMEM((2, CONTEXT, inner), BF16),
            pltpu.VMEM((2, tokens, inner), F32),
            pltpu.VMEM(order.shape, BF16),
        ],
        scratch_shapes=[
            pltpu.SMEM((1,), jnp.int32),
            pltpu.VMEM((tokens, width), BF16),
            pltpu.VMEM((tokens, width), BF16),
            pltpu.VMEM((inner, width), BF16),
            pltpu.VMEM((tokens, width), BF16),
            pltpu.SemaphoreType.DMA((8,)),
        ],
        compiler_params=params(24),
        cost_estimate=cost(12 * tokens * width * inner, 10 * inner * width),
        name="front",
    )(places, lengths, *[in_hbm(o) for o in (order, frames, cotangent, w_qkv, w_out)])


def pair_columns(pair, inner):
    return [slice(n * inner + pair * PAIR, n * inner + (pair + 1) * PAIR) for n in range(3)]


def attend(begin, length, inner, operands, results):
    lane = lax.broadcasted_iota(jnp.int32, (CONTEXT, PAIR), 1)
    heads = (lane < HEAD_DIM, lane >= HEAD_DIM)
    row_valid = begin + lax.broadcasted_iota(jnp.int32, (CONTEXT, PAIR), 0) < length
    col_valid = begin + lane < length
    keys = lax.broadcasted_iota(jnp.int32, (2 * CONTEXT, 2 * CONTEXT), 0)
    queries = lax.broadcasted_iota(jnp.int32, (2 * CONTEXT, 2 * CONTEXT), 1)
    key_block = keys // GROUP
    query_block = (queries % CONTEXT) // GROUP
    key_place = begin - CONTEXT + keys
    seen = (key_block >= query_block) & (key_block <= query_block + LEFT) & (key_place >= 0) & (key_place < length)
    zero = jnp.zeros((CONTEXT, PAIR), BF16)
    scale = HEAD_DIM ** (-0.5)

    def unstack(both):
        return jnp.concatenate([both[:HEAD_DIM, :CONTEXT], both[HEAD_DIM:, CONTEXT:]], axis=0)

    for pair in range(inner // PAIR):
        q, k2, v2, do = operands(pair)
        do = jnp.where(row_valid, do, zero)
        q = q * jnp.asarray(scale, BF16)
        q2 = jnp.concatenate([jnp.where(h, q, zero) for h in heads], axis=0)
        do2 = jnp.concatenate([jnp.where(h, do, zero) for h in heads], axis=0)
        scores = jnp.where(seen, dot(k2, q2, NT), -1e30)
        dprob = dot(v2, do2, NT)
        highest = jnp.max(scores, axis=0, keepdims=True)
        raised = jnp.exp(scores - highest)
        prob = raised * (1.0 / jnp.sum(raised, axis=0, keepdims=True))
        rounded = prob.astype(BF16)
        mixed = jnp.where(col_valid, unstack(dot(v2.T, rounded)), 0.0).T.astype(BF16)
        weighed = prob * dprob
        dscores = (weighed - prob * jnp.sum(weighed, axis=0, keepdims=True)).astype(BF16)
        dq = (unstack(dot(k2.T, dscores)) * scale).T.astype(BF16)
        results(pair, mixed, dq, dot(dscores, q2), dot(rounded, do2))


def early_kernel(
    places, lengths_ref, order_ref, frames_ref, weight_ref, qkv_ref, do_ref, late_ref, add_ref,
    out_ref, dkv_ref, turned_ref, length, normed, halo, sem,
):
    fetch = pltpu.make_async_copy(lengths_ref, length, sem)
    fetch.start()
    inner = do_ref.shape[1]
    rows = qkv_ref.shape[0]
    here = places[1]
    values = frames_ref[...].astype(F32)
    average, inverse = statistics(values)
    normed[...] = ((values - average) * inverse).astype(BF16)
    halo[...] = dot(normed[...], weight_ref[:, inner:]).astype(BF16)
    out_ref[:, CONTEXT:, :] = late_ref[...]
    dkv_ref[:, CONTEXT:rows, :inner] = add_ref[:, CONTEXT:, :].astype(BF16)

    def store(at, own, other):
        turned_ref[at, :] = own
        half = dkv_ref.shape[1]
        for n in range(2):
            first, last = max(at.start, n * half), min(at.stop, (n + 1) * half)
            if first < last:
                dkv_ref[n, first - n * half : last - n * half, inner:] = other[first - at.start : last - at.start]

    turn(normed, order_ref, here, store)

    def operands(pair):
        q, k, v = pair_columns(pair, inner)
        k2 = jnp.concatenate([halo[:, q], qkv_ref[:CONTEXT, k]], axis=0)
        v2 = jnp.concatenate([halo[:, k], qkv_ref[:CONTEXT, v]], axis=0)
        return qkv_ref[:CONTEXT, q], k2, v2, do_ref[:CONTEXT, q]

    def results(pair, mixed, dq, dk, dv):
        at = pair_columns(pair, inner)[0]
        out_ref[0, :CONTEXT, at] = mixed
        out_ref[1, :CONTEXT, at] = dq
        for n, grad in enumerate((dk, dv)):
            dkv_ref[n, rows:, at] = grad[:CONTEXT].astype(BF16)
            dkv_ref[n, :CONTEXT, at] = (grad[CONTEXT:] + add_ref[n, :CONTEXT, at]).astype(BF16)

    fetch.wait()
    attend(places[0], length[0], inner, operands, results)


def early_tile(places, lengths, order, frames, weight, qkv, attended_grad, late, late_grad):
    rows, inner = attended_grad.shape
    width = frames.shape[1]
    return pl.pallas_call(
        early_kernel,
        in_specs=[SMEM_SPEC, HBM_SPEC] + [VMEM_SPEC] * 7,
        out_specs=[VMEM_SPEC] * 3,
        out_shape=[
            pltpu.VMEM((2, rows, inner), BF16),
            pltpu.VMEM((2, rows + CONTEXT, inner + CONTEXT), BF16),
            pltpu.VMEM((width // CORES, CONTEXT), BF16),
        ],
        scratch_shapes=[
            pltpu.SMEM((1,), jnp.int32),
            pltpu.VMEM((CONTEXT, width), BF16),
            pltpu.VMEM((CONTEXT, 2 * inner), BF16),
            pltpu.SemaphoreType.DMA,
        ],
        compiler_params=params(16),
        cost_estimate=cost(28 * CONTEXT * 2 * CONTEXT * inner, 16 * CONTEXT * inner, CONTEXT * 4 * inner),
        name="attention_early",
    )(places, lengths, *[in_vmem(o) for o in (order, frames, weight, qkv, attended_grad, late, late_grad)])


def store_section(chunks, route, n, total, outs, held):
    half = CHUNKS // 2
    held[n] = total.reshape(held.shape[1:])
    for slot in range(CHUNKS):
        outs[n if slot < half else 2 + n][slot % half] = held[n, chunks[route, slot]].astype(BF16)


def first_own_kernel(left_ref, right_ref, out_ref):
    tokens = right_ref.shape[1]
    out_ref[0] = dot(left_ref[:, tokens:], right_ref[0])
    out_ref[1] = dot(left_ref[:, :tokens], right_ref[1])


def first_own(left, right):
    return pl.pallas_call(
        first_own_kernel,
        in_specs=[VMEM_SPEC] * 2,
        out_specs=VMEM_SPEC,
        out_shape=pltpu.VMEM((2, left.shape[0], right.shape[2]), F32),
        compiler_params=params(8),
        cost_estimate=cost(2 * 10**9, 1),
        name="first_own",
    )(in_vmem(left), in_vmem(right))


def first_wave_kernel(chunks, left_other_ref, right_other_ref, own_ref, *refs):
    tokens = right_other_ref.shape[1]
    for n, at in enumerate((slice(tokens, 2 * tokens), slice(0, tokens))):
        total = own_ref[n] + dot(left_other_ref[:, at], right_other_ref[n])
        store_section(chunks, n, n, total, refs[:-1], refs[-1])


def second_wave_kernel(chunks, left_ref, left_other_ref, behind_ref, right_ref, right_other_ref, *refs):
    tokens = left_ref.shape[1] // 2
    inner = right_ref.shape[2] - CONTEXT
    behind_other = jnp.concatenate([right_other_ref[n, :, inner:] for n in range(2)], axis=0)
    left = jnp.concatenate([left_ref[:, :tokens], behind_ref[...], left_other_ref[:, :tokens], behind_other], axis=1)
    for n in range(2):
        total = dot(left, jnp.concatenate([right_ref[n, :, :inner], right_other_ref[n, :, :inner]], axis=0))
        store_section(chunks, 2 + n, n, total, refs[:-1], refs[-1])


def weight_sections(kernel, chunks, operands, inner, flops, name):
    size = (operands[0].shape[0] // CHUNKS, inner)
    routes = 2
    outs = pl.pallas_call(
        kernel,
        in_specs=[SMEM_SPEC] + [VMEM_SPEC] * len(operands),
        out_specs=[VMEM_SPEC] * (2 * routes),
        out_shape=[pltpu.VMEM((CHUNKS // 2, *size), BF16)] * (2 * routes),
        scratch_shapes=[pltpu.VMEM((routes, CHUNKS, *size), F32)],
        compiler_params=params(24),
        cost_estimate=cost(flops, 1),
        name=name,
    )(chunks, *[in_vmem(o) for o in operands])
    return outs[:routes], outs[routes:]


def finish_kernel(back_ref, grad_ref, frames_ref, stats_ref, out_ref, rows, grads, sems):
    tiles = rows.shape[0] // CONTEXT
    copies = []
    for i in range(tiles):
        here = pl.ds(i * CONTEXT, CONTEXT)
        copies.append(pltpu.make_async_copy(frames_ref.at[here], rows.at[here], sems.at[i]))
        copies.append(pltpu.make_async_copy(grad_ref.at[here], grads.at[here], sems.at[tiles + i]))
    for copy in copies:
        copy.start()
    columns = jnp.concatenate([stats_ref[...]] * 4, axis=0).T
    for i in range(tiles):
        here = slice(i * CONTEXT, (i + 1) * CONTEXT)
        copies[2 * i].wait()
        copies[2 * i + 1].wait()
        grad = grads[here]
        if (i + 1) * CONTEXT == rows.shape[0]:
            grad += back_ref[...].astype(F32)
        grad = grad.astype(BF16).astype(F32)
        inverse = columns[here, 1:2]
        normed = (rows[here].astype(F32) - columns[here, 0:1]) * inverse
        along = jnp.mean(grad * normed, axis=-1, keepdims=True)
        out_ref[here] = (inverse * (grad - jnp.mean(grad, axis=-1, keepdims=True) - normed * along)).astype(BF16)


def finish(back, grad, frames, stats):
    return pl.pallas_call(
        finish_kernel,
        in_specs=[VMEM_SPEC, HBM_SPEC, HBM_SPEC, VMEM_SPEC],
        out_specs=VMEM_SPEC,
        out_shape=jax.ShapeDtypeStruct(frames.shape, BF16),
        scratch_shapes=[
            pltpu.VMEM(frames.shape, BF16),
            pltpu.VMEM(frames.shape, F32),
            pltpu.SemaphoreType.DMA((2 * frames.shape[0] // CONTEXT,)),
        ],
        compiler_params=params(12),
        cost_estimate=cost(1, 1),
        name="finish",
    )(in_vmem(back), in_hbm(grad), in_hbm(frames), in_vmem(stats))


def plus(*terms):
    return sum(t.astype(F32) for t in terms).astype(BF16)


def halve_kernel(*refs):
    for route in range(2):
        keep, got, kept, sent = refs[route::2]
        count = kept.shape[0]
        for ref, at in ((kept, slice(0, count)), (sent, slice(count, 2 * count))):
            ref[...] = (keep[at].astype(F32) + got[at].astype(F32)).astype(BF16)


def halve(keep, gots):
    count, *size = keep[0].shape
    outs = pl.pallas_call(
        halve_kernel,
        in_specs=[VMEM_SPEC] * 4,
        out_specs=[VMEM_SPEC] * 4,
        out_shape=[pltpu.VMEM((count // 2, *size), BF16)] * 4,
        compiler_params=params(8),
        cost_estimate=cost(1, 1),
        name="halve",
    )(*[in_vmem(o) for o in (*keep, *gots)])
    return outs[:2], outs[2:]


def pieces_kernel(place, first_ref, second_ref, *refs):
    outs, held = refs[:-1], refs[-1]
    for ref, places in ((first_ref, (3, 0)), (second_ref, (1, 2))):
        block = ref[...].astype(F32)
        tiles = block.shape[1] // PAIR // 2
        share = block.shape[0] // Z
        for n, at in enumerate(places):
            for t in range(tiles):
                rows = slice((at * tiles + t) * share, (at * tiles + t + 1) * share)
                column = (n * tiles + t) * PAIR
                for z in range(Z):
                    held[z, rows, :] = block[z * share : (z + 1) * share, column : column + PAIR]
    for step, ref in enumerate(outs):
        ref[...] = held[lax.rem(place[0] + step, Z)].astype(BF16)


def pieces(place, groups):
    rows, columns = groups[0].shape
    size = (rows // Z * 2 * columns // PAIR, PAIR)
    return pl.pallas_call(
        pieces_kernel,
        in_specs=[SMEM_SPEC] + [VMEM_SPEC] * 2,
        out_specs=[VMEM_SPEC] * Z,
        out_shape=[pltpu.VMEM(size, BF16)] * Z,
        scratch_shapes=[pltpu.VMEM((Z, *size), F32)],
        compiler_params=params(16),
        cost_estimate=cost(1, 1),
        name="pieces",
    )(jnp.reshape(place, (1,)), *[in_vmem(g) for g in groups])


def total_kernel(*refs):
    ins, out_ref = refs[:-1], refs[-1]
    total = ins[0][...].astype(F32)
    for ref in ins[1:]:
        total += ref[...].astype(F32)
    share = out_ref.shape[0]
    for t in range(out_ref.shape[1] // PAIR):
        out_ref[:, t * PAIR : (t + 1) * PAIR] = total[t * share : (t + 1) * share]


def on_device(frames, cotangent, lengths, w_qkv, w_out):
    frame_rows = frames[0]
    grad_rows = cotangent[0]
    row_count, width = frame_rows.shape
    inner = w_out.shape[0]
    seq_index = lax.axis_index("seq")
    dp_index = lax.axis_index("dp")
    xl = seq_index % XL
    core, xh, y = dp_index % CORES, dp_index // CORES % XH, dp_index // (CORES * XH)
    places = jnp.stack([seq_index * row_count, core])
    chunks = jnp.stack([chunk_at(r, jnp.arange(CHUNKS), y, xh, xl) for r in range(len(ROUTES))])

    behind = from_behind(last_rows(frame_rows), "seq", 1)
    frame_rows, places, chunks = lax.optimization_barrier((frame_rows, places, chunks))
    qkv, attended_grad, left, left_out, stats, weight, late, late_grad, order = front(
        places, lengths, frame_rows, grad_rows, w_qkv, w_out
    )
    left_other = to_device(left_out, to_core)
    own, grads, left_behind = early_tile(places, lengths, order, behind, weight, qkv, attended_grad, late, late_grad)
    own_other = to_device(own, to_core)
    own_sum = first_own(left, own)
    own_other, left_other, own_sum, grads = lax.optimization_barrier((own_other, left_other, own_sum, grads))
    grads_other = to_device(grads, to_core)
    keep_a, send_a = weight_sections(first_wave_kernel, chunks, (left_other, own_other, own_sum), inner, 1, "first_wave")
    keep_b, send_b = weight_sections(
        second_wave_kernel, chunks, (left, left_other, left_behind, grads, grads_other), inner, 3 * 10**9, "second_wave"
    )
    query_grad = jnp.concatenate([own[1], jnp.zeros((CONTEXT, inner), BF16)], axis=0)
    projected_grad = jnp.concatenate([query_grad, grads[0, :, :inner], grads[1, :, :inner]], axis=1)
    attended, projected_grad, send_b = lax.optimization_barrier((own[0], projected_grad, send_b))
    block_out = dot(attended, w_out).astype(BF16)
    def second_ring(kept, gots, n, *after):
        group = jnp.concatenate([plus(kept[r], gots[r]) for r in range(2)], axis=-1)
        slots, *after = lax.optimization_barrier(([group[slot] for slot in range(1, 4)], *after))
        others = [to_device(slots[i], OWNERS[n][i]) for i in range(3)]
        return plus(group[0], *others), *after

    gots_a = [to_device(send_a[r], ROUTES[r][0]) for r in range(2)]
    gots_b = [to_device(send_b[r], ROUTES[2 + r][0]) for r in range(2)]
    gots_a, block_out = lax.optimization_barrier((gots_a, block_out))
    kept_a, sent_a = halve(keep_a, gots_a)
    gots_a = [to_device(sent_a[r], ROUTES[r][1]) for r in range(2)]
    kept_b, sent_b = halve(keep_b, gots_b)
    projected_grad, sent_b = lax.optimization_barrier((projected_grad, sent_b))
    gots_b = [to_device(sent_b[r], ROUTES[2 + r][1]) for r in range(2)]
    normed_grad = dot(projected_grad, w_qkv, NT)
    gots_a, normed_grad = lax.optimization_barrier((gots_a, normed_grad))
    first_group, = second_ring(kept_a, gots_a, 0)
    second_group, normed_grad = second_ring(kept_b, gots_b, 1, normed_grad)
    groups = [first_group, second_group]
    returned = from_behind(normed_grad[row_count:].astype(BF16), "seq", -1)
    frame_grad = finish(returned, normed_grad, frame_rows, stats)
    shares = pieces(seq_index // XL, groups)
    shares = [shares[0]] + [to_device(shares[step], along_z(step)) for step in (4, 3, 5, 2, 6, 1, 7)]
    shares, frame_grad = lax.optimization_barrier((shares, frame_grad))
    share = width // (CHUNKS * CORES * Z)
    total = pl.pallas_call(
        total_kernel,
        in_specs=[VMEM_SPEC] * Z,
        out_shape=jax.ShapeDtypeStruct((share, 4 * inner), F32),
        compiler_params=params(8),
        cost_estimate=cost(1, 1),
        name="total",
    )(*[in_vmem(o) for o in shares])
    return block_out[None], frame_grad[None], total


def solution(mesh):
    placed = (P("dp", "seq", None), P("dp", "seq", None), P("dp"), P(), P())
    return jax.shard_map(
        on_device,
        mesh=mesh,
        in_specs=placed,
        out_specs=(P("dp", "seq", None), P("dp", "seq", None), P(("dp", "seq"), None)),
        check_vma=False,
    )
```

```python
import jax
import jax.numpy as jnp
import numpy as np
from jax import lax
from jax.experimental import pallas as pl
from jax.experimental.pallas import tpu as pltpu
from jax.sharding import PartitionSpec as P

HEAD_DIM = 64
GROUP = 32
LEFT = 4
CONTEXT = LEFT * GROUP
PAIR = 2 * HEAD_DIM
F32 = jnp.float32
BF16 = jnp.bfloat16
NT = (((1,), (1,)), ((), ()))
NN = (((1,), (0,)), ((), ()))

Y, XH, CORES, Z, XL = 4, 2, 2, 8, 2
CHUNKS = Y * XH * XL

epsilon = 1e-05


def dot(a, b, dims=NN):
    return lax.dot_general(a, b, dims, preferred_element_type=F32)


def from_behind(value, axis, by):
    peers = lax.axis_size(axis)
    return lax.ppermute(value, axis, [(i, (i + by) % peers) for i in range(peers)])


def flat(y, xh, core, z, xl):
    return ((y * XH + xh) * CORES + core) * (Z * XL) + z * XL + xl


def to_device(value, where):
    pairs = []
    for place in np.ndindex(Y, XH, CORES, Z, XL):
        pairs.append((flat(*place), flat(*where(*place))))
    return lax.ppermute(value, ("dp", "seq"), pairs)


def to_core(y, xh, core, z, xl):
    return y, xh, 1 - core, z, xl


def to_x_near(y, xh, core, z, xl):
    return y, xh, core, z, 1 - xl


def to_x_mirror(y, xh, core, z, xl):
    return y, 1 - xh, core, z, 1 - xl


def to_y_near(y, xh, core, z, xl):
    return y ^ 1, xh, core, z, xl


def to_y_mirror(y, xh, core, z, xl):
    return 3 - y, xh, core, z, xl


def to_x_far(y, xh, core, z, xl):
    return y, 1 - xh, core, z, xl


def to_y_far(y, xh, core, z, xl):
    return y ^ 2, xh, core, z, xl


def to_z_near(y, xh, core, z, xl):
    return y, xh, core, z ^ 1, xl


ROUTES = (
    (to_y_near, to_y_mirror),
    (to_y_mirror, to_y_near),
    (to_x_near, to_x_mirror),
    (to_x_mirror, to_x_near),
)
OWNERS = (
    (to_x_mirror, to_x_near, to_x_far),
    (to_y_mirror, to_y_near, to_y_far),
)


def halves(route, hi, lo):
    return (hi ^ lo, hi) if route % 2 == 0 else (hi, hi ^ lo)


def chunk_at(route, slot, y, xh, xl):
    bits = [(slot >> (3 - i)) & 1 for i in range(4)]
    x_first = route >= 2
    x_bits, y_bits = (bits[:2], bits[2:]) if x_first else (bits[2:], bits[:2])
    found = []
    for hi, lo, pair, order in ((y >> 1, y & 1, y_bits, 0 if x_first else route), (xh, xl, x_bits, route if x_first else 0)):
        first, second = halves(order, hi, lo)
        first, second = first ^ pair[0], second ^ pair[1]
        found.append((second, first ^ second) if order % 2 == 0 else (first, first ^ second))
    (yh, yl), (xh_to, xl_to) = found
    return ((yh * 2 + yl) * XH + xh_to) * XL + xl_to


def row_order(width):
    share = width // (CHUNKS * CORES * Z)
    order = np.arange(width // Y).reshape(XH, CORES, Z, XL, share).transpose(1, 0, 3, 2, 4).reshape(-1)
    return jnp.asarray(np.eye(width // Y, dtype=np.float32)[order], BF16)


def statistics(rows_in):
    average = jnp.mean(rows_in, axis=-1, keepdims=True)
    centered = rows_in - average
    variance = jnp.mean(centered * centered, axis=-1, keepdims=True)
    return average, lax.rsqrt(variance + epsilon)


def normalize_grad(rows_in, average, inverse, grad):
    normed = (rows_in - average) * inverse
    along = jnp.mean(grad * normed, axis=-1, keepdims=True)
    return inverse * (grad - jnp.mean(grad, axis=-1, keepdims=True) - normed * along)


SMEM_SPEC = pl.BlockSpec(memory_space=pltpu.SMEM)
VMEM_SPEC = pl.BlockSpec(memory_space=pltpu.VMEM)
HBM_SPEC = pl.BlockSpec(memory_space=pltpu.HBM)


def in_vmem(value):
    return pltpu.with_memory_space_constraint(value, pltpu.VMEM)


def in_hbm(value):
    return pltpu.with_memory_space_constraint(value, pltpu.HBM)


def cost(flops, nbytes, transcendentals=0):
    return pl.CostEstimate(flops=flops, bytes_accessed=nbytes, transcendentals=transcendentals)


def params(mebibytes):
    return pltpu.CompilerParams(vmem_limit_bytes=mebibytes * 2**20)


def turn(ref, order_ref, here, store):
    rows = order_ref.shape[0]
    half = rows // CORES
    for y in range(Y):
        turned = dot(order_ref[...], ref[:, y * rows : (y + 1) * rows].T).astype(BF16)
        first, second = turned[:half], turned[half:]
        at = slice(y * half, (y + 1) * half)
        store(at, jnp.where(here == 0, first, second), jnp.where(here == 0, second, first))


def last_rows(frames):
    rows, width = frames.shape

    pieces = 8

    def kernel(frames_ref, out_ref, sems):
        size = CONTEXT // pieces
        copies = [
            pltpu.make_async_copy(
                frames_ref.at[pl.ds(rows - CONTEXT + i * size, size)], out_ref.at[pl.ds(i * size, size)], sems.at[i]
            )
            for i in range(pieces)
        ]
        for copy in copies:
            copy.start()
        for copy in copies:
            copy.wait()

    return pl.pallas_call(
        kernel,
        in_specs=[HBM_SPEC],
        out_specs=VMEM_SPEC,
        out_shape=pltpu.VMEM((CONTEXT, width), BF16),
        scratch_shapes=[pltpu.SemaphoreType.DMA((pieces,))],
        compiler_params=params(4),
        cost_estimate=cost(1, 1),
        name="last_rows",
    )(in_hbm(frames))


def front_kernel(
    places, lengths_ref, order_ref, frames_ref, cotangent_ref, weight_ref, out_ref,
    qkv_ref, grad_ref, keep_ref, send_ref, stats_ref, weight, late_ref, dkv_ref, order,
    length, rows, cotangent, outer, normed, sems,
):
    here = places[1]
    tokens = rows.shape[0]
    thirds = weight.shape[1] // 3
    block = [slice(n * thirds, (n + 1) * thirds) for n in range(3)]
    small = [
        pltpu.make_async_copy(order_ref, order, sems.at[6]),
        pltpu.make_async_copy(lengths_ref, length, sems.at[7]),
    ]
    copies = [
        pltpu.make_async_copy(frames_ref, rows, sems.at[0]),
        pltpu.make_async_copy(cotangent_ref, cotangent, sems.at[1]),
        pltpu.make_async_copy(out_ref, outer, sems.at[2]),
    ] + [
        pltpu.make_async_copy(weight_ref.at[:, pl.ds(n * thirds, thirds)], weight.at[:, pl.ds(n * thirds, thirds)], sems.at[3 + n])
        for n in range(3)
    ]
    for copy in copies[:1] + small + copies[1:]:
        copy.start()

    def put(columns):
        def store(at, own, other):
            keep_ref[at, columns] = own
            send_ref[at, columns] = other

        return store

    copies[0].wait()
    values = rows[...].astype(F32)
    average, inverse = statistics(values)
    for n, column in enumerate((average, inverse)):
        stats_ref[n : n + 1, :] = jnp.broadcast_to(column, (tokens, PAIR)).T[:1]
    normed[...] = ((values - average) * inverse).astype(BF16)
    small[0].wait()
    turn(normed, order, here, put(slice(0, tokens)))
    copies[1].wait()
    turn(cotangent, order, here, put(slice(tokens, 2 * tokens)))
    copies[2].wait()
    grad_ref[...] = dot(cotangent[...], outer[...], NT).astype(BF16)
    for n in range(3):
        copies[3 + n].wait()
    qkv_ref[...] = dot(normed[...], weight[...]).astype(BF16)

    inner = thirds

    def operands(pair):
        q, k, v = pair_columns(pair, inner)
        return qkv_ref[CONTEXT:, q], qkv_ref[:, k], qkv_ref[:, v], grad_ref[CONTEXT:, q]

    def results(pair, mixed, dq, dk, dv):
        at = pair_columns(pair, inner)[0]
        late_ref[0, :, at] = mixed
        late_ref[1, :, at] = dq
        dkv_ref[0, :, at] = dk
        dkv_ref[1, :, at] = dv

    small[1].wait()
    attend(places[0] + CONTEXT, length[0], inner, operands, results)


def front(places, lengths, frames, cotangent, w_qkv, w_out):
    tokens, width = frames.shape
    inner = w_out.shape[0]
    order = row_order(width)
    turned = pltpu.VMEM((width // CORES, 2 * tokens), BF16)
    return pl.pallas_call(
        front_kernel,
        in_specs=[SMEM_SPEC] + [HBM_SPEC] * 6,
        out_specs=[VMEM_SPEC] * 9,
        out_shape=[
            pltpu.VMEM((tokens, 3 * inner), BF16),
            pltpu.VMEM((tokens, inner), BF16),
            turned,
            turned,
            pltpu.VMEM((2, tokens), F32),
            pltpu.VMEM((width, 3 * inner), BF16),
            pltpu.VMEM((2, CONTEXT, inner), BF16),
            pltpu.VMEM((2, tokens, inner), F32),
            pltpu.VMEM(order.shape, BF16),
        ],
        scratch_shapes=[
            pltpu.SMEM((1,), jnp.int32),
            pltpu.VMEM((tokens, width), BF16),
            pltpu.VMEM((tokens, width), BF16),
            pltpu.VMEM((inner, width), BF16),
            pltpu.VMEM((tokens, width), BF16),
            pltpu.SemaphoreType.DMA((8,)),
        ],
        compiler_params=params(24),
        cost_estimate=cost(12 * tokens * width * inner, 10 * inner * width),
        name="front",
    )(places, lengths, *[in_hbm(o) for o in (order, frames, cotangent, w_qkv, w_out)])


def pair_columns(pair, inner):
    return [slice(n * inner + pair * PAIR, n * inner + (pair + 1) * PAIR) for n in range(3)]


def attend(begin, length, inner, operands, results):
    lane = lax.broadcasted_iota(jnp.int32, (CONTEXT, PAIR), 1)
    heads = (lane < HEAD_DIM, lane >= HEAD_DIM)
    row_valid = begin + lax.broadcasted_iota(jnp.int32, (CONTEXT, PAIR), 0) < length
    col_valid = begin + lane < length
    keys = lax.broadcasted_iota(jnp.int32, (2 * CONTEXT, 2 * CONTEXT), 0)
    queries = lax.broadcasted_iota(jnp.int32, (2 * CONTEXT, 2 * CONTEXT), 1)
    key_block = keys // GROUP
    query_block = (queries % CONTEXT) // GROUP
    key_place = begin - CONTEXT + keys
    seen = (key_block >= query_block) & (key_block <= query_block + LEFT) & (key_place >= 0) & (key_place < length)
    zero = jnp.zeros((CONTEXT, PAIR), BF16)
    scale = HEAD_DIM ** (-0.5)

    def unstack(both):
        return jnp.concatenate([both[:HEAD_DIM, :CONTEXT], both[HEAD_DIM:, CONTEXT:]], axis=0)

    for pair in range(inner // PAIR):
        q, k2, v2, do = operands(pair)
        do = jnp.where(row_valid, do, zero)
        q = q * jnp.asarray(scale, BF16)
        q2 = jnp.concatenate([jnp.where(h, q, zero) for h in heads], axis=0)
        do2 = jnp.concatenate([jnp.where(h, do, zero) for h in heads], axis=0)
        scores = jnp.where(seen, dot(k2, q2, NT), -1e30)
        dprob = dot(v2, do2, NT)
        highest = jnp.max(scores, axis=0, keepdims=True)
        raised = jnp.exp(scores - highest)
        prob = raised * (1.0 / jnp.sum(raised, axis=0, keepdims=True))
        rounded = prob.astype(BF16)
        mixed = jnp.where(col_valid, unstack(dot(v2.T, rounded)), 0.0).T.astype(BF16)
        weighed = prob * dprob
        dscores = (weighed - prob * jnp.sum(weighed, axis=0, keepdims=True)).astype(BF16)
        dq = (unstack(dot(k2.T, dscores)) * scale).T.astype(BF16)
        results(pair, mixed, dq, dot(dscores, q2), dot(rounded, do2))


def early_kernel(
    places, lengths_ref, order_ref, frames_ref, weight_ref, qkv_ref, do_ref, late_ref, add_ref,
    out_ref, dkv_ref, turned_ref, length, normed, halo, sem,
):
    fetch = pltpu.make_async_copy(lengths_ref, length, sem)
    fetch.start()
    inner = do_ref.shape[1]
    rows = qkv_ref.shape[0]
    here = places[1]
    values = frames_ref[...].astype(F32)
    average, inverse = statistics(values)
    normed[...] = ((values - average) * inverse).astype(BF16)
    halo[...] = dot(normed[...], weight_ref[:, inner:]).astype(BF16)
    out_ref[:, CONTEXT:, :] = late_ref[...]
    dkv_ref[:, CONTEXT:rows, :inner] = add_ref[:, CONTEXT:, :].astype(BF16)

    def store(at, own, other):
        turned_ref[at, :] = own
        half = dkv_ref.shape[1]
        for n in range(2):
            first, last = max(at.start, n * half), min(at.stop, (n + 1) * half)
            if first < last:
                dkv_ref[n, first - n * half : last - n * half, inner:] = other[first - at.start : last - at.start]

    turn(normed, order_ref, here, store)

    def operands(pair):
        q, k, v = pair_columns(pair, inner)
        k2 = jnp.concatenate([halo[:, q], qkv_ref[:CONTEXT, k]], axis=0)
        v2 = jnp.concatenate([halo[:, k], qkv_ref[:CONTEXT, v]], axis=0)
        return qkv_ref[:CONTEXT, q], k2, v2, do_ref[:CONTEXT, q]

    def results(pair, mixed, dq, dk, dv):
        at = pair_columns(pair, inner)[0]
        out_ref[0, :CONTEXT, at] = mixed
        out_ref[1, :CONTEXT, at] = dq
        for n, grad in enumerate((dk, dv)):
            dkv_ref[n, rows:, at] = grad[:CONTEXT].astype(BF16)
            dkv_ref[n, :CONTEXT, at] = (grad[CONTEXT:] + add_ref[n, :CONTEXT, at]).astype(BF16)

    fetch.wait()
    attend(places[0], length[0], inner, operands, results)


def early_tile(places, lengths, order, frames, weight, qkv, attended_grad, late, late_grad):
    rows, inner = attended_grad.shape
    width = frames.shape[1]
    return pl.pallas_call(
        early_kernel,
        in_specs=[SMEM_SPEC, HBM_SPEC] + [VMEM_SPEC] * 7,
        out_specs=[VMEM_SPEC] * 3,
        out_shape=[
            pltpu.VMEM((2, rows, inner), BF16),
            pltpu.VMEM((2, rows + CONTEXT, inner + CONTEXT), BF16),
            pltpu.VMEM((width // CORES, CONTEXT), BF16),
        ],
        scratch_shapes=[
            pltpu.SMEM((1,), jnp.int32),
            pltpu.VMEM((CONTEXT, width), BF16),
            pltpu.VMEM((CONTEXT, 2 * inner), BF16),
            pltpu.SemaphoreType.DMA,
        ],
        compiler_params=params(16),
        cost_estimate=cost(28 * CONTEXT * 2 * CONTEXT * inner, 16 * CONTEXT * inner, CONTEXT * 4 * inner),
        name="attention_early",
    )(places, lengths, *[in_vmem(o) for o in (order, frames, weight, qkv, attended_grad, late, late_grad)])


def store_section(chunks, route, n, total, outs, held):
    half = CHUNKS // 2
    held[n] = total.reshape(held.shape[1:])
    for slot in range(CHUNKS):
        outs[n if slot < half else 2 + n][slot % half] = held[n, chunks[route, slot]].astype(BF16)


def first_own_kernel(left_ref, right_ref, out_ref):
    tokens = right_ref.shape[1]
    out_ref[0] = dot(left_ref[:, tokens:], right_ref[0])
    out_ref[1] = dot(left_ref[:, :tokens], right_ref[1])


def first_own(left, right):
    return pl.pallas_call(
        first_own_kernel,
        in_specs=[VMEM_SPEC] * 2,
        out_specs=VMEM_SPEC,
        out_shape=pltpu.VMEM((2, left.shape[0], right.shape[2]), F32),
        compiler_params=params(8),
        cost_estimate=cost(2 * 10**9, 1),
        name="first_own",
    )(in_vmem(left), in_vmem(right))


def first_wave_kernel(chunks, left_other_ref, right_other_ref, own_ref, *refs):
    tokens = right_other_ref.shape[1]
    for n, at in enumerate((slice(tokens, 2 * tokens), slice(0, tokens))):
        total = own_ref[n] + dot(left_other_ref[:, at], right_other_ref[n])
        store_section(chunks, n, n, total, refs[:-1], refs[-1])


def second_wave_kernel(chunks, left_ref, left_other_ref, behind_ref, right_ref, right_other_ref, *refs):
    tokens = left_ref.shape[1] // 2
    inner = right_ref.shape[2] - CONTEXT
    behind_other = jnp.concatenate([right_other_ref[n, :, inner:] for n in range(2)], axis=0)
    left = jnp.concatenate([left_ref[:, :tokens], behind_ref[...], left_other_ref[:, :tokens], behind_other], axis=1)
    for n in range(2):
        total = dot(left, jnp.concatenate([right_ref[n, :, :inner], right_other_ref[n, :, :inner]], axis=0))
        store_section(chunks, 2 + n, n, total, refs[:-1], refs[-1])


def weight_sections(kernel, chunks, operands, inner, flops, name):
    size = (operands[0].shape[0] // CHUNKS, inner)
    routes = 2
    outs = pl.pallas_call(
        kernel,
        in_specs=[SMEM_SPEC] + [VMEM_SPEC] * len(operands),
        out_specs=[VMEM_SPEC] * (2 * routes),
        out_shape=[pltpu.VMEM((CHUNKS // 2, *size), BF16)] * (2 * routes),
        scratch_shapes=[pltpu.VMEM((routes, CHUNKS, *size), F32)],
        compiler_params=params(24),
        cost_estimate=cost(flops, 1),
        name=name,
    )(chunks, *[in_vmem(o) for o in operands])
    return outs[:routes], outs[routes:]


def plus(*terms):
    return sum(t.astype(F32) for t in terms).astype(BF16)


def halve_kernel(*refs):
    for route in range(2):
        keep, got, kept, sent = refs[route::2]
        count = kept.shape[0]
        for ref, at in ((kept, slice(0, count)), (sent, slice(count, 2 * count))):
            ref[...] = (keep[at].astype(F32) + got[at].astype(F32)).astype(BF16)


def halve(keep, gots):
    count, *size = keep[0].shape
    outs = pl.pallas_call(
        halve_kernel,
        in_specs=[VMEM_SPEC] * 4,
        out_specs=[VMEM_SPEC] * 4,
        out_shape=[pltpu.VMEM((count // 2, *size), BF16)] * 4,
        compiler_params=params(8),
        cost_estimate=cost(1, 1),
        name="halve",
    )(*[in_vmem(o) for o in (*keep, *gots)])
    return outs[:2], outs[2:]


def pieces_kernel(place, first_ref, second_ref, keep_ref, send_ref, held):
    for ref, places in ((first_ref, (3, 0)), (second_ref, (1, 2))):
        block = ref[...].astype(F32)
        tiles = block.shape[1] // PAIR // 2
        share = block.shape[0] // Z
        for n, at in enumerate(places):
            for t in range(tiles):
                rows = slice((at * tiles + t) * share, (at * tiles + t + 1) * share)
                column = (n * tiles + t) * PAIR
                for z in range(Z):
                    held[z, rows, :] = block[z * share : (z + 1) * share, column : column + PAIR]
    parity = lax.rem(place[2], 2)
    for step in range(Z // 2):
        keep_ref[step] = held[2 * step + parity].astype(BF16)
        send_ref[step] = held[2 * step + 1 - parity].astype(BF16)


def pieces(place, groups):
    rows, columns = groups[0].shape
    size = (rows // Z * 2 * columns // PAIR, PAIR)
    return pl.pallas_call(
        pieces_kernel,
        in_specs=[SMEM_SPEC] + [VMEM_SPEC] * 2,
        out_specs=[VMEM_SPEC] * 2,
        out_shape=[pltpu.VMEM((Z // 2, *size), BF16)] * 2,
        scratch_shapes=[pltpu.VMEM((Z, *size), F32)],
        compiler_params=params(16),
        cost_estimate=cost(1, 1),
        name="pieces",
    )(place, *[in_vmem(g) for g in groups])


def total_kernel(in_ref, out_ref):
    total = in_ref[0].astype(F32)
    for z in range(1, Z // 2):
        total += in_ref[z].astype(F32)
    share = out_ref.shape[0]
    for t in range(out_ref.shape[1] // PAIR):
        out_ref[:, t * PAIR : (t + 1) * PAIR] = total[t * share : (t + 1) * share]


def on_device(frames, cotangent, lengths, w_qkv, w_out):
    frame_rows = frames[0]
    grad_rows = cotangent[0]
    row_count, width = frame_rows.shape
    inner = w_out.shape[0]
    seq_index = lax.axis_index("seq")
    dp_index = lax.axis_index("dp")
    xl = seq_index % XL
    core, xh, y = dp_index % CORES, dp_index // CORES % XH, dp_index // (CORES * XH)
    places = jnp.stack([seq_index * row_count, core, seq_index // XL])
    chunks = jnp.stack([chunk_at(r, jnp.arange(CHUNKS), y, xh, xl) for r in range(len(ROUTES))])

    behind = from_behind(last_rows(frame_rows), "seq", 1)
    frame_rows, places, chunks = lax.optimization_barrier((frame_rows, places, chunks))
    qkv, attended_grad, left, left_out, stats, weight, late, late_grad, order = front(
        places, lengths, frame_rows, grad_rows, w_qkv, w_out
    )
    left_other = to_device(left_out, to_core)
    own, grads, left_behind = early_tile(places, lengths, order, behind, weight, qkv, attended_grad, late, late_grad)
    own_other = to_device(own, to_core)
    own_sum = first_own(left, own)
    own_other, left_other, own_sum, grads = lax.optimization_barrier((own_other, left_other, own_sum, grads))
    grads_other = to_device(grads, to_core)
    keep_a, send_a = weight_sections(first_wave_kernel, chunks, (left_other, own_other, own_sum), inner, 1, "first_wave")
    keep_b, send_b = weight_sections(
        second_wave_kernel, chunks, (left, left_other, left_behind, grads, grads_other), inner, 3 * 10**9, "second_wave"
    )
    query_grad = jnp.concatenate([own[1], jnp.zeros((CONTEXT, inner), BF16)], axis=0)
    projected_grad = jnp.concatenate([query_grad, grads[0, :, :inner], grads[1, :, :inner]], axis=1)
    attended, projected_grad, send_b = lax.optimization_barrier((own[0], projected_grad, send_b))
    block_out = dot(attended, w_out).astype(BF16)
    def second_ring(kept, gots, n, *after):
        group = jnp.concatenate([plus(kept[r], gots[r]) for r in range(2)], axis=-1)
        slots, *after = lax.optimization_barrier(([group[slot] for slot in range(1, 4)], *after))
        others = [to_device(slots[i], OWNERS[n][i]) for i in range(3)]
        return plus(group[0], *others), *after

    gots_a = [to_device(send_a[r], ROUTES[r][0]) for r in range(2)]
    gots_b = [to_device(send_b[r], ROUTES[2 + r][0]) for r in range(2)]
    gots_a, block_out = lax.optimization_barrier((gots_a, block_out))
    kept_a, sent_a = halve(keep_a, gots_a)
    gots_a = [to_device(sent_a[r], ROUTES[r][1]) for r in range(2)]
    kept_b, sent_b = halve(keep_b, gots_b)
    projected_grad, sent_b = lax.optimization_barrier((projected_grad, sent_b))
    gots_b = [to_device(sent_b[r], ROUTES[2 + r][1]) for r in range(2)]
    normed_grad = dot(projected_grad, w_qkv, NT)
    gots_a, normed_grad = lax.optimization_barrier((gots_a, normed_grad))
    first_group, = second_ring(kept_a, gots_a, 0)
    second_group, normed_grad = second_ring(kept_b, gots_b, 1, normed_grad)
    groups = [first_group, second_group]
    returned = from_behind(normed_grad[row_count:].astype(BF16), "seq", -1)
    returned = jnp.concatenate([jnp.zeros((row_count - CONTEXT, width), BF16), returned], axis=0)
    normed_grad = (normed_grad[:row_count] + returned.astype(F32)).astype(BF16)
    frame_grad = normalize_grad(frame_rows.astype(F32), stats[0][:, None], stats[1][:, None], normed_grad.astype(F32))
    kept, sent = pieces(places, groups)
    shares = plus(kept, to_device(sent, to_z_near))
    rings = [[place * XL + x for place in range(parity, Z, 2)] for parity in range(2) for x in range(XL)]
    shares = lax.all_to_all(shares, "seq", 0, 0, axis_index_groups=rings, tiled=True)
    share = width // (CHUNKS * CORES * Z)
    total = pl.pallas_call(
        total_kernel,
        in_specs=[VMEM_SPEC],
        out_shape=jax.ShapeDtypeStruct((share, 4 * inner), F32),
        compiler_params=params(24),
        name="total",
    )(in_vmem(shares))
    return block_out[None], frame_grad.astype(BF16)[None], total


def solution(mesh):
    placed = (P("dp", "seq", None), P("dp", "seq", None), P("dp"), P(), P())
    return jax.shard_map(
        on_device,
        mesh=mesh,
        in_specs=placed,
        out_specs=(P("dp", "seq", None), P("dp", "seq", None), P(("dp", "seq"), None)),
        check_vma=False,
    )
```

```python
import jax
import jax.numpy as jnp
import numpy as np
from jax import lax
from jax.experimental import pallas as pl
from jax.experimental.pallas import tpu as pltpu
from jax.sharding import PartitionSpec as P

HEAD_DIM = 64
GROUP = 32
LEFT = 4
CONTEXT = LEFT * GROUP
PAIR = 2 * HEAD_DIM
F32 = jnp.float32
BF16 = jnp.bfloat16
NT = (((1,), (1,)), ((), ()))
NN = (((1,), (0,)), ((), ()))

Y, XH, CORES, Z, XL = 4, 2, 2, 8, 2
CHUNKS = Y * XH * XL

epsilon = 1e-05


def dot(a, b, dims=NN):
    return lax.dot_general(a, b, dims, preferred_element_type=F32)


def from_behind(value, axis, by):
    peers = lax.axis_size(axis)
    return lax.ppermute(value, axis, [(i, (i + by) % peers) for i in range(peers)])


def flat(y, xh, core, z, xl):
    return ((y * XH + xh) * CORES + core) * (Z * XL) + z * XL + xl


def to_device(value, where):
    pairs = []
    for place in np.ndindex(Y, XH, CORES, Z, XL):
        pairs.append((flat(*place), flat(*where(*place))))
    return lax.ppermute(value, ("dp", "seq"), pairs)


def to_core(y, xh, core, z, xl):
    return y, xh, 1 - core, z, xl


def to_x_near(y, xh, core, z, xl):
    return y, xh, core, z, 1 - xl


def to_x_mirror(y, xh, core, z, xl):
    return y, 1 - xh, core, z, 1 - xl


def to_y_near(y, xh, core, z, xl):
    return y ^ 1, xh, core, z, xl


def to_y_mirror(y, xh, core, z, xl):
    return 3 - y, xh, core, z, xl


def to_x_far(y, xh, core, z, xl):
    return y, 1 - xh, core, z, xl


def to_y_far(y, xh, core, z, xl):
    return y ^ 2, xh, core, z, xl


ROUTES = (
    (to_y_near, to_y_mirror),
    (to_y_mirror, to_y_near),
    (to_x_near, to_x_mirror),
    (to_x_mirror, to_x_near),
)
OWNERS = (
    (to_x_mirror, to_x_near, to_x_far),
    (to_y_mirror, to_y_near, to_y_far),
)


def halves(route, hi, lo):
    return (hi ^ lo, hi) if route % 2 == 0 else (hi, hi ^ lo)


def chunk_at(route, slot, y, xh, xl):
    bits = [(slot >> (3 - i)) & 1 for i in range(4)]
    x_first = route >= 2
    x_bits, y_bits = (bits[:2], bits[2:]) if x_first else (bits[2:], bits[:2])
    found = []
    for hi, lo, pair, order in ((y >> 1, y & 1, y_bits, 0 if x_first else route), (xh, xl, x_bits, route if x_first else 0)):
        first, second = halves(order, hi, lo)
        first, second = first ^ pair[0], second ^ pair[1]
        found.append((second, first ^ second) if order % 2 == 0 else (first, first ^ second))
    (yh, yl), (xh_to, xl_to) = found
    return ((yh * 2 + yl) * XH + xh_to) * XL + xl_to


def row_order(width):
    share = width // (CHUNKS * CORES * Z)
    order = np.arange(width // Y).reshape(XH, CORES, Z, XL, share).transpose(1, 0, 3, 2, 4).reshape(-1)
    return jnp.asarray(np.eye(width // Y, dtype=np.float32)[order], BF16)


def statistics(rows_in):
    average = jnp.mean(rows_in, axis=-1, keepdims=True)
    centered = rows_in - average
    variance = jnp.mean(centered * centered, axis=-1, keepdims=True)
    return average, lax.rsqrt(variance + epsilon)


def normalize_grad(rows_in, average, inverse, grad):
    normed = (rows_in - average) * inverse
    along = jnp.mean(grad * normed, axis=-1, keepdims=True)
    return inverse * (grad - jnp.mean(grad, axis=-1, keepdims=True) - normed * along)


SMEM_SPEC = pl.BlockSpec(memory_space=pltpu.SMEM)
VMEM_SPEC = pl.BlockSpec(memory_space=pltpu.VMEM)
HBM_SPEC = pl.BlockSpec(memory_space=pltpu.HBM)


def in_vmem(value):
    return pltpu.with_memory_space_constraint(value, pltpu.VMEM)


def in_hbm(value):
    return pltpu.with_memory_space_constraint(value, pltpu.HBM)


def cost(flops, nbytes, transcendentals=0):
    return pl.CostEstimate(flops=flops, bytes_accessed=nbytes, transcendentals=transcendentals)


def params(mebibytes):
    return pltpu.CompilerParams(vmem_limit_bytes=mebibytes * 2**20)


def turn(ref, order_ref, here, store):
    rows = order_ref.shape[0]
    half = rows // CORES
    for y in range(Y):
        turned = dot(order_ref[...], ref[:, y * rows : (y + 1) * rows].T).astype(BF16)
        first, second = turned[:half], turned[half:]
        at = slice(y * half, (y + 1) * half)
        store(at, jnp.where(here == 0, first, second), jnp.where(here == 0, second, first))


def last_rows(frames):
    rows, width = frames.shape

    pieces = 8

    def kernel(frames_ref, out_ref, sems):
        size = CONTEXT // pieces
        copies = [
            pltpu.make_async_copy(
                frames_ref.at[pl.ds(rows - CONTEXT + i * size, size)], out_ref.at[pl.ds(i * size, size)], sems.at[i]
            )
            for i in range(pieces)
        ]
        for copy in copies:
            copy.start()
        for copy in copies:
            copy.wait()

    return pl.pallas_call(
        kernel,
        in_specs=[HBM_SPEC],
        out_specs=VMEM_SPEC,
        out_shape=pltpu.VMEM((CONTEXT, width), BF16),
        scratch_shapes=[pltpu.SemaphoreType.DMA((pieces,))],
        compiler_params=params(4),
        cost_estimate=cost(1, 1),
        name="last_rows",
    )(in_hbm(frames))


def front_kernel(
    places, lengths_ref, order_ref, frames_ref, cotangent_ref, weight_ref, out_ref,
    qkv_ref, grad_ref, keep_ref, send_ref, stats_ref, weight, late_ref, dkv_ref, order,
    length, rows, cotangent, outer, normed, sems,
):
    here = places[1]
    tokens = rows.shape[0]
    thirds = weight.shape[1] // 3
    block = [slice(n * thirds, (n + 1) * thirds) for n in range(3)]
    small = [
        pltpu.make_async_copy(order_ref, order, sems.at[6]),
        pltpu.make_async_copy(lengths_ref, length, sems.at[7]),
    ]
    copies = [
        pltpu.make_async_copy(frames_ref, rows, sems.at[0]),
        pltpu.make_async_copy(cotangent_ref, cotangent, sems.at[1]),
        pltpu.make_async_copy(out_ref, outer, sems.at[2]),
    ] + [
        pltpu.make_async_copy(weight_ref.at[:, pl.ds(n * thirds, thirds)], weight.at[:, pl.ds(n * thirds, thirds)], sems.at[3 + n])
        for n in range(3)
    ]
    for copy in copies[:1] + small + copies[1:]:
        copy.start()

    def put(columns):
        def store(at, own, other):
            keep_ref[at, columns] = own
            send_ref[at, columns] = other

        return store

    copies[0].wait()
    values = rows[...].astype(F32)
    average, inverse = statistics(values)
    for n, column in enumerate((average, inverse)):
        stats_ref[n : n + 1, :] = jnp.broadcast_to(column, (tokens, PAIR)).T[:1]
    normed[...] = ((values - average) * inverse).astype(BF16)
    small[0].wait()
    turn(normed, order, here, put(slice(0, tokens)))
    copies[1].wait()
    turn(cotangent, order, here, put(slice(tokens, 2 * tokens)))
    copies[2].wait()
    grad_ref[...] = dot(cotangent[...], outer[...], NT).astype(BF16)
    for n in range(3):
        copies[3 + n].wait()
    qkv_ref[...] = dot(normed[...], weight[...]).astype(BF16)

    inner = thirds

    def operands(pair):
        q, k, v = pair_columns(pair, inner)
        return qkv_ref[CONTEXT:, q], qkv_ref[:, k], qkv_ref[:, v], grad_ref[CONTEXT:, q]

    def results(pair, mixed, dq, dk, dv):
        at = pair_columns(pair, inner)[0]
        late_ref[0, :, at] = mixed
        late_ref[1, :, at] = dq
        dkv_ref[0, :, at] = dk
        dkv_ref[1, :, at] = dv

    small[1].wait()
    attend(places[0] + CONTEXT, length[0], inner, operands, results)


def front(places, lengths, frames, cotangent, w_qkv, w_out):
    tokens, width = frames.shape
    inner = w_out.shape[0]
    order = row_order(width)
    turned = pltpu.VMEM((width // CORES, 2 * tokens), BF16)
    return pl.pallas_call(
        front_kernel,
        in_specs=[SMEM_SPEC] + [HBM_SPEC] * 6,
        out_specs=[VMEM_SPEC] * 9,
        out_shape=[
            pltpu.VMEM((tokens, 3 * inner), BF16),
            pltpu.VMEM((tokens, inner), BF16),
            turned,
            turned,
            pltpu.VMEM((2, tokens), F32),
            pltpu.VMEM((width, 3 * inner), BF16),
            pltpu.VMEM((2, CONTEXT, inner), BF16),
            pltpu.VMEM((2, tokens, inner), F32),
            pltpu.VMEM(order.shape, BF16),
        ],
        scratch_shapes=[
            pltpu.SMEM((1,), jnp.int32),
            pltpu.VMEM((tokens, width), BF16),
            pltpu.VMEM((tokens, width), BF16),
            pltpu.VMEM((inner, width), BF16),
            pltpu.VMEM((tokens, width), BF16),
            pltpu.SemaphoreType.DMA((8,)),
        ],
        compiler_params=params(24),
        cost_estimate=cost(12 * tokens * width * inner, 10 * inner * width),
        name="front",
    )(places, lengths, *[in_hbm(o) for o in (order, frames, cotangent, w_qkv, w_out)])


def pair_columns(pair, inner):
    return [slice(n * inner + pair * PAIR, n * inner + (pair + 1) * PAIR) for n in range(3)]


def attend(begin, length, inner, operands, results):
    lane = lax.broadcasted_iota(jnp.int32, (CONTEXT, PAIR), 1)
    heads = (lane < HEAD_DIM, lane >= HEAD_DIM)
    row_valid = begin + lax.broadcasted_iota(jnp.int32, (CONTEXT, PAIR), 0) < length
    col_valid = begin + lane < length
    keys = lax.broadcasted_iota(jnp.int32, (2 * CONTEXT, 2 * CONTEXT), 0)
    queries = lax.broadcasted_iota(jnp.int32, (2 * CONTEXT, 2 * CONTEXT), 1)
    key_block = keys // GROUP
    query_block = (queries % CONTEXT) // GROUP
    key_place = begin - CONTEXT + keys
    seen = (key_block >= query_block) & (key_block <= query_block + LEFT) & (key_place >= 0) & (key_place < length)
    zero = jnp.zeros((CONTEXT, PAIR), BF16)
    scale = HEAD_DIM ** (-0.5)

    def unstack(both):
        return jnp.concatenate([both[:HEAD_DIM, :CONTEXT], both[HEAD_DIM:, CONTEXT:]], axis=0)

    for pair in range(inner // PAIR):
        q, k2, v2, do = operands(pair)
        do = jnp.where(row_valid, do, zero)
        q = q * jnp.asarray(scale, BF16)
        q2 = jnp.concatenate([jnp.where(h, q, zero) for h in heads], axis=0)
        do2 = jnp.concatenate([jnp.where(h, do, zero) for h in heads], axis=0)
        scores = jnp.where(seen, dot(k2, q2, NT), -1e30)
        dprob = dot(v2, do2, NT)
        highest = jnp.max(scores, axis=0, keepdims=True)
        raised = jnp.exp(scores - highest)
        prob = raised * (1.0 / jnp.sum(raised, axis=0, keepdims=True))
        rounded = prob.astype(BF16)
        mixed = jnp.where(col_valid, unstack(dot(v2.T, rounded)), 0.0).T.astype(BF16)
        weighed = prob * dprob
        dscores = (weighed - prob * jnp.sum(weighed, axis=0, keepdims=True)).astype(BF16)
        dq = (unstack(dot(k2.T, dscores)) * scale).T.astype(BF16)
        results(pair, mixed, dq, dot(dscores, q2), dot(rounded, do2))


def early_kernel(
    places, lengths_ref, order_ref, frames_ref, weight_ref, qkv_ref, do_ref, late_ref, add_ref,
    out_ref, dkv_ref, turned_ref, length, normed, halo, sem,
):
    fetch = pltpu.make_async_copy(lengths_ref, length, sem)
    fetch.start()
    inner = do_ref.shape[1]
    rows = qkv_ref.shape[0]
    here = places[1]
    values = frames_ref[...].astype(F32)
    average, inverse = statistics(values)
    normed[...] = ((values - average) * inverse).astype(BF16)
    halo[...] = dot(normed[...], weight_ref[:, inner:]).astype(BF16)
    out_ref[:, CONTEXT:, :] = late_ref[...]
    dkv_ref[:, CONTEXT:rows, :inner] = add_ref[:, CONTEXT:, :].astype(BF16)

    def store(at, own, other):
        turned_ref[at, :] = own
        half = dkv_ref.shape[1]
        for n in range(2):
            first, last = max(at.start, n * half), min(at.stop, (n + 1) * half)
            if first < last:
                dkv_ref[n, first - n * half : last - n * half, inner:] = other[first - at.start : last - at.start]

    turn(normed, order_ref, here, store)

    def operands(pair):
        q, k, v = pair_columns(pair, inner)
        k2 = jnp.concatenate([halo[:, q], qkv_ref[:CONTEXT, k]], axis=0)
        v2 = jnp.concatenate([halo[:, k], qkv_ref[:CONTEXT, v]], axis=0)
        return qkv_ref[:CONTEXT, q], k2, v2, do_ref[:CONTEXT, q]

    def results(pair, mixed, dq, dk, dv):
        at = pair_columns(pair, inner)[0]
        out_ref[0, :CONTEXT, at] = mixed
        out_ref[1, :CONTEXT, at] = dq
        for n, grad in enumerate((dk, dv)):
            dkv_ref[n, rows:, at] = grad[:CONTEXT].astype(BF16)
            dkv_ref[n, :CONTEXT, at] = (grad[CONTEXT:] + add_ref[n, :CONTEXT, at]).astype(BF16)

    fetch.wait()
    attend(places[0], length[0], inner, operands, results)


def early_tile(places, lengths, order, frames, weight, qkv, attended_grad, late, late_grad):
    rows, inner = attended_grad.shape
    width = frames.shape[1]
    return pl.pallas_call(
        early_kernel,
        in_specs=[SMEM_SPEC, HBM_SPEC] + [VMEM_SPEC] * 7,
        out_specs=[VMEM_SPEC] * 3,
        out_shape=[
            pltpu.VMEM((2, rows, inner), BF16),
            pltpu.VMEM((2, rows + CONTEXT, inner + CONTEXT), BF16),
            pltpu.VMEM((width // CORES, CONTEXT), BF16),
        ],
        scratch_shapes=[
            pltpu.SMEM((1,), jnp.int32),
            pltpu.VMEM((CONTEXT, width), BF16),
            pltpu.VMEM((CONTEXT, 2 * inner), BF16),
            pltpu.SemaphoreType.DMA,
        ],
        compiler_params=params(16),
        cost_estimate=cost(28 * CONTEXT * 2 * CONTEXT * inner, 16 * CONTEXT * inner, CONTEXT * 4 * inner),
        name="attention_early",
    )(places, lengths, *[in_vmem(o) for o in (order, frames, weight, qkv, attended_grad, late, late_grad)])


def store_section(chunks, route, n, total, outs, held):
    half = CHUNKS // 2
    held[n] = total.reshape(held.shape[1:])
    for slot in range(CHUNKS):
        outs[n if slot < half else 2 + n][slot % half] = held[n, chunks[route, slot]].astype(BF16)


def first_own_kernel(left_ref, right_ref, out_ref):
    tokens = right_ref.shape[1]
    out_ref[0] = dot(left_ref[:, tokens:], right_ref[0])
    out_ref[1] = dot(left_ref[:, :tokens], right_ref[1])


def first_own(left, right):
    return pl.pallas_call(
        first_own_kernel,
        in_specs=[VMEM_SPEC] * 2,
        out_specs=VMEM_SPEC,
        out_shape=pltpu.VMEM((2, left.shape[0], right.shape[2]), F32),
        compiler_params=params(8),
        cost_estimate=cost(2 * 10**9, 1),
        name="first_own",
    )(in_vmem(left), in_vmem(right))


def first_wave_kernel(chunks, left_other_ref, right_other_ref, own_ref, *refs):
    tokens = right_other_ref.shape[1]
    for n, at in enumerate((slice(tokens, 2 * tokens), slice(0, tokens))):
        total = own_ref[n] + dot(left_other_ref[:, at], right_other_ref[n])
        store_section(chunks, n, n, total, refs[:-1], refs[-1])


def second_wave_kernel(chunks, left_ref, left_other_ref, behind_ref, right_ref, right_other_ref, *refs):
    tokens = left_ref.shape[1] // 2
    inner = right_ref.shape[2] - CONTEXT
    behind_other = jnp.concatenate([right_other_ref[n, :, inner:] for n in range(2)], axis=0)
    left = jnp.concatenate([left_ref[:, :tokens], behind_ref[...], left_other_ref[:, :tokens], behind_other], axis=1)
    for n in range(2):
        total = dot(left, jnp.concatenate([right_ref[n, :, :inner], right_other_ref[n, :, :inner]], axis=0))
        store_section(chunks, 2 + n, n, total, refs[:-1], refs[-1])


def weight_sections(kernel, chunks, operands, inner, flops, name):
    size = (operands[0].shape[0] // CHUNKS, inner)
    routes = 2
    outs = pl.pallas_call(
        kernel,
        in_specs=[SMEM_SPEC] + [VMEM_SPEC] * len(operands),
        out_specs=[VMEM_SPEC] * (2 * routes),
        out_shape=[pltpu.VMEM((CHUNKS // 2, *size), BF16)] * (2 * routes),
        scratch_shapes=[pltpu.VMEM((routes, CHUNKS, *size), F32)],
        compiler_params=params(24),
        cost_estimate=cost(flops, 1),
        name=name,
    )(chunks, *[in_vmem(o) for o in operands])
    return outs[:routes], outs[routes:]


def plus(*terms):
    return sum(t.astype(F32) for t in terms).astype(BF16)


def halve_kernel(*refs):
    for route in range(2):
        keep, got, kept, sent = refs[route::2]
        count = kept.shape[0]
        for ref, at in ((kept, slice(0, count)), (sent, slice(count, 2 * count))):
            ref[...] = (keep[at].astype(F32) + got[at].astype(F32)).astype(BF16)


def halve(keep, gots):
    count, *size = keep[0].shape
    outs = pl.pallas_call(
        halve_kernel,
        in_specs=[VMEM_SPEC] * 4,
        out_specs=[VMEM_SPEC] * 4,
        out_shape=[pltpu.VMEM((count // 2, *size), BF16)] * 4,
        compiler_params=params(8),
        cost_estimate=cost(1, 1),
        name="halve",
    )(*[in_vmem(o) for o in (*keep, *gots)])
    return outs[:2], outs[2:]


def pieces_kernel(*refs):
    ins, out_ref, held = refs[:-2], refs[-2], refs[-1]
    for ref, places in zip(ins, ((3, 0), (1, 2))):
        block = ref[...].astype(F32)
        tiles = block.shape[1] // PAIR // 2
        share = block.shape[0] // Z
        for n, place in enumerate(places):
            for t in range(tiles):
                rows = slice((place * tiles + t) * share, (place * tiles + t + 1) * share)
                column = (n * tiles + t) * PAIR
                for z in range(Z):
                    held[z, rows, :] = block[z * share : (z + 1) * share, column : column + PAIR]
    out_ref[...] = held[...].astype(BF16)


def total_kernel(in_ref, out_ref):
    total = in_ref[0].astype(F32)
    for z in range(1, Z):
        total += in_ref[z].astype(F32)
    share = out_ref.shape[0]
    for t in range(out_ref.shape[1] // PAIR):
        out_ref[:, t * PAIR : (t + 1) * PAIR] = total[t * share : (t + 1) * share]


def on_device(frames, cotangent, lengths, w_qkv, w_out):
    frame_rows = frames[0]
    grad_rows = cotangent[0]
    row_count, width = frame_rows.shape
    inner = w_out.shape[0]
    seq_index = lax.axis_index("seq")
    dp_index = lax.axis_index("dp")
    xl = seq_index % XL
    core, xh, y = dp_index % CORES, dp_index // CORES % XH, dp_index // (CORES * XH)
    places = jnp.stack([seq_index * row_count, core])
    chunks = jnp.stack([chunk_at(r, jnp.arange(CHUNKS), y, xh, xl) for r in range(len(ROUTES))])

    behind = from_behind(last_rows(frame_rows), "seq", 1)
    frame_rows, places, chunks = lax.optimization_barrier((frame_rows, places, chunks))
    qkv, attended_grad, left, left_out, stats, weight, late, late_grad, order = front(
        places, lengths, frame_rows, grad_rows, w_qkv, w_out
    )
    left_other = to_device(left_out, to_core)
    own, grads, left_behind = early_tile(places, lengths, order, behind, weight, qkv, attended_grad, late, late_grad)
    own_other = to_device(own, to_core)
    own_sum = first_own(left, own)
    own_other, left_other, own_sum, grads = lax.optimization_barrier((own_other, left_other, own_sum, grads))
    grads_other = to_device(grads, to_core)
    keep_a, send_a = weight_sections(first_wave_kernel, chunks, (left_other, own_other, own_sum), inner, 1, "first_wave")
    keep_b, send_b = weight_sections(
        second_wave_kernel, chunks, (left, left_other, left_behind, grads, grads_other), inner, 3 * 10**9, "second_wave"
    )
    query_grad = jnp.concatenate([own[1], jnp.zeros((CONTEXT, inner), BF16)], axis=0)
    projected_grad = jnp.concatenate([query_grad, grads[0, :, :inner], grads[1, :, :inner]], axis=1)
    attended, projected_grad, send_b = lax.optimization_barrier((own[0], projected_grad, send_b))
    block_out = dot(attended, w_out).astype(BF16)
    def second_ring(kept, gots, n, *after):
        group = jnp.concatenate([plus(kept[r], gots[r]) for r in range(2)], axis=-1)
        slots, *after = lax.optimization_barrier(([group[slot] for slot in range(1, 4)], *after))
        others = [to_device(slots[i], OWNERS[n][i]) for i in range(3)]
        return plus(group[0], *others), *after

    gots_a = [to_device(send_a[r], ROUTES[r][0]) for r in range(2)]
    gots_b = [to_device(send_b[r], ROUTES[2 + r][0]) for r in range(2)]
    gots_a, block_out = lax.optimization_barrier((gots_a, block_out))
    kept_a, sent_a = halve(keep_a, gots_a)
    gots_a = [to_device(sent_a[r], ROUTES[r][1]) for r in range(2)]
    kept_b, sent_b = halve(keep_b, gots_b)
    projected_grad, sent_b = lax.optimization_barrier((projected_grad, sent_b))
    gots_b = [to_device(sent_b[r], ROUTES[2 + r][1]) for r in range(2)]
    normed_grad = dot(projected_grad, w_qkv, NT)
    gots_a, normed_grad = lax.optimization_barrier((gots_a, normed_grad))
    first_group, = second_ring(kept_a, gots_a, 0)
    second_group, normed_grad = second_ring(kept_b, gots_b, 1, normed_grad)
    groups = [first_group, second_group]
    returned = from_behind(normed_grad[row_count:].astype(BF16), "seq", -1)
    returned = jnp.concatenate([jnp.zeros((row_count - CONTEXT, width), BF16), returned], axis=0)
    normed_grad = (normed_grad[:row_count] + returned.astype(F32)).astype(BF16)
    frame_grad = normalize_grad(frame_rows.astype(F32), stats[0][:, None], stats[1][:, None], normed_grad.astype(F32))
    share = width // (CHUNKS * CORES * Z)
    tiles = 4 * inner // PAIR
    shares = pl.pallas_call(
        pieces_kernel,
        in_specs=[VMEM_SPEC] * 2,
        out_shape=jax.ShapeDtypeStruct((Z, tiles * share, PAIR), BF16),
        scratch_shapes=[pltpu.VMEM((Z, tiles * share, PAIR), F32)],
        compiler_params=params(24),
        name="pieces",
    )(*[in_vmem(g) for g in groups])
    rings = [[place * XL + x for place in range(Z)] for x in range(XL)]
    shares = lax.all_to_all(shares, "seq", 0, 0, axis_index_groups=rings, tiled=True)
    total = pl.pallas_call(
        total_kernel,
        in_specs=[VMEM_SPEC],
        out_shape=jax.ShapeDtypeStruct((share, 4 * inner), F32),
        compiler_params=params(24),
        name="total",
    )(in_vmem(shares))
    return block_out[None], frame_grad.astype(BF16)[None], total


def solution(mesh):
    placed = (P("dp", "seq", None), P("dp", "seq", None), P("dp"), P(), P())
    return jax.shard_map(
        on_device,
        mesh=mesh,
        in_specs=placed,
        out_specs=(P("dp", "seq", None), P("dp", "seq", None), P(("dp", "seq"), None)),
        check_vma=False,
    )
```

```python
import jax
import jax.numpy as jnp
import numpy as np
from jax import lax
from jax.experimental import pallas as pl
from jax.experimental.pallas import tpu as pltpu
from jax.sharding import PartitionSpec as P

HEAD_DIM = 64
GROUP = 32
LEFT = 4
CONTEXT = LEFT * GROUP
PAIR = 2 * HEAD_DIM
F32 = jnp.float32
BF16 = jnp.bfloat16
NT = (((1,), (1,)), ((), ()))
NN = (((1,), (0,)), ((), ()))

Y, XH, CORES, Z, XL = 4, 2, 2, 8, 2
CHUNKS = Y * XH * XL

epsilon = 1e-05


def dot(a, b, dims=NN):
    return lax.dot_general(a, b, dims, preferred_element_type=F32)


def from_behind(value, axis, by):
    peers = lax.axis_size(axis)
    return lax.ppermute(value, axis, [(i, (i + by) % peers) for i in range(peers)])


def flat(y, xh, core, z, xl):
    return ((y * XH + xh) * CORES + core) * (Z * XL) + z * XL + xl


def to_device(value, where):
    pairs = []
    for place in np.ndindex(Y, XH, CORES, Z, XL):
        pairs.append((flat(*place), flat(*where(*place))))
    return lax.ppermute(value, ("dp", "seq"), pairs)


def to_core(y, xh, core, z, xl):
    return y, xh, 1 - core, z, xl


def to_x_near(y, xh, core, z, xl):
    return y, xh, core, z, 1 - xl


def to_x_mirror(y, xh, core, z, xl):
    return y, 1 - xh, core, z, 1 - xl


def to_y_near(y, xh, core, z, xl):
    return y ^ 1, xh, core, z, xl


def to_y_mirror(y, xh, core, z, xl):
    return 3 - y, xh, core, z, xl


def to_x_far(y, xh, core, z, xl):
    return y, 1 - xh, core, z, xl


def to_y_far(y, xh, core, z, xl):
    return y ^ 2, xh, core, z, xl


ROUTES = (
    (to_y_near, to_y_mirror),
    (to_y_mirror, to_y_near),
    (to_x_near, to_x_mirror),
    (to_x_mirror, to_x_near),
)
OWNERS = (
    (to_x_mirror, to_x_near, to_x_far),
    (to_y_mirror, to_y_near, to_y_far),
)


def halves(route, hi, lo):
    return (hi ^ lo, hi) if route % 2 == 0 else (hi, hi ^ lo)


def chunk_at(route, slot, y, xh, xl):
    bits = [(slot >> (3 - i)) & 1 for i in range(4)]
    x_first = route >= 2
    x_bits, y_bits = (bits[:2], bits[2:]) if x_first else (bits[2:], bits[:2])
    found = []
    for hi, lo, pair, order in ((y >> 1, y & 1, y_bits, 0 if x_first else route), (xh, xl, x_bits, route if x_first else 0)):
        first, second = halves(order, hi, lo)
        first, second = first ^ pair[0], second ^ pair[1]
        found.append((second, first ^ second) if order % 2 == 0 else (first, first ^ second))
    (yh, yl), (xh_to, xl_to) = found
    return ((yh * 2 + yl) * XH + xh_to) * XL + xl_to


def row_order(width):
    share = width // (CHUNKS * CORES * Z)
    order = np.arange(width // Y).reshape(XH, CORES, Z, XL, share).transpose(1, 0, 3, 2, 4).reshape(-1)
    return jnp.asarray(np.eye(width // Y, dtype=np.float32)[order], BF16)


def statistics(rows_in):
    average = jnp.mean(rows_in, axis=-1, keepdims=True)
    centered = rows_in - average
    variance = jnp.mean(centered * centered, axis=-1, keepdims=True)
    return average, lax.rsqrt(variance + epsilon)


def normalize_grad(rows_in, average, inverse, grad):
    normed = (rows_in - average) * inverse
    along = jnp.mean(grad * normed, axis=-1, keepdims=True)
    return inverse * (grad - jnp.mean(grad, axis=-1, keepdims=True) - normed * along)


SMEM_SPEC = pl.BlockSpec(memory_space=pltpu.SMEM)
VMEM_SPEC = pl.BlockSpec(memory_space=pltpu.VMEM)
HBM_SPEC = pl.BlockSpec(memory_space=pltpu.HBM)


def in_vmem(value):
    return pltpu.with_memory_space_constraint(value, pltpu.VMEM)


def in_hbm(value):
    return pltpu.with_memory_space_constraint(value, pltpu.HBM)


def cost(flops, nbytes, transcendentals=0):
    return pl.CostEstimate(flops=flops, bytes_accessed=nbytes, transcendentals=transcendentals)


def params(mebibytes):
    return pltpu.CompilerParams(vmem_limit_bytes=mebibytes * 2**20)


def turn(ref, order_ref, here, store):
    rows = order_ref.shape[0]
    half = rows // CORES
    for y in range(Y):
        turned = dot(order_ref[...], ref[:, y * rows : (y + 1) * rows].T).astype(BF16)
        first, second = turned[:half], turned[half:]
        at = slice(y * half, (y + 1) * half)
        store(at, jnp.where(here == 0, first, second), jnp.where(here == 0, second, first))


def last_rows(frames):
    rows, width = frames.shape

    pieces = 8

    def kernel(frames_ref, out_ref, sems):
        size = CONTEXT // pieces
        copies = [
            pltpu.make_async_copy(
                frames_ref.at[pl.ds(rows - CONTEXT + i * size, size)], out_ref.at[pl.ds(i * size, size)], sems.at[i]
            )
            for i in range(pieces)
        ]
        for copy in copies:
            copy.start()
        for copy in copies:
            copy.wait()

    return pl.pallas_call(
        kernel,
        in_specs=[HBM_SPEC],
        out_specs=VMEM_SPEC,
        out_shape=pltpu.VMEM((CONTEXT, width), BF16),
        scratch_shapes=[pltpu.SemaphoreType.DMA((pieces,))],
        compiler_params=params(4),
        cost_estimate=cost(1, 1),
        name="last_rows",
    )(in_hbm(frames))


def front_kernel(
    places, lengths_ref, order_ref, frames_ref, cotangent_ref, weight_ref, out_ref,
    qkv_ref, grad_ref, keep_ref, send_ref, stats_ref, weight, late_ref, dkv_ref, order,
    length, rows, cotangent, outer, normed, sems,
):
    here = places[1]
    tokens = rows.shape[0]
    thirds = weight.shape[1] // 3
    block = [slice(n * thirds, (n + 1) * thirds) for n in range(3)]
    small = [
        pltpu.make_async_copy(order_ref, order, sems.at[6]),
        pltpu.make_async_copy(lengths_ref, length, sems.at[7]),
    ]
    copies = [
        pltpu.make_async_copy(frames_ref, rows, sems.at[0]),
        pltpu.make_async_copy(cotangent_ref, cotangent, sems.at[1]),
        pltpu.make_async_copy(out_ref, outer, sems.at[2]),
    ] + [
        pltpu.make_async_copy(weight_ref.at[:, pl.ds(n * thirds, thirds)], weight.at[:, pl.ds(n * thirds, thirds)], sems.at[3 + n])
        for n in range(3)
    ]
    for copy in copies[:1] + small + copies[1:]:
        copy.start()

    def put(columns):
        def store(at, own, other):
            keep_ref[at, columns] = own
            send_ref[at, columns] = other

        return store

    copies[0].wait()
    values = rows[...].astype(F32)
    average, inverse = statistics(values)
    for n, column in enumerate((average, inverse)):
        stats_ref[n : n + 1, :] = jnp.broadcast_to(column, (tokens, PAIR)).T[:1]
    normed[...] = ((values - average) * inverse).astype(BF16)
    small[0].wait()
    turn(normed, order, here, put(slice(0, tokens)))
    copies[1].wait()
    turn(cotangent, order, here, put(slice(tokens, 2 * tokens)))
    copies[2].wait()
    grad_ref[...] = dot(cotangent[...], outer[...], NT).astype(BF16)
    for n in range(3):
        copies[3 + n].wait()
    qkv_ref[...] = dot(normed[...], weight[...]).astype(BF16)

    inner = thirds

    def operands(pair):
        q, k, v = pair_columns(pair, inner)
        return qkv_ref[CONTEXT:, q], qkv_ref[:, k], qkv_ref[:, v], grad_ref[CONTEXT:, q]

    def results(pair, mixed, dq, dk, dv):
        at = pair_columns(pair, inner)[0]
        late_ref[0, :, at] = mixed
        late_ref[1, :, at] = dq
        dkv_ref[0, :, at] = dk
        dkv_ref[1, :, at] = dv

    small[1].wait()
    attend(places[0] + CONTEXT, length[0], inner, operands, results)


def front(places, lengths, frames, cotangent, w_qkv, w_out):
    tokens, width = frames.shape
    inner = w_out.shape[0]
    order = row_order(width)
    turned = pltpu.VMEM((width // CORES, 2 * tokens), BF16)
    return pl.pallas_call(
        front_kernel,
        in_specs=[SMEM_SPEC] + [HBM_SPEC] * 6,
        out_specs=[VMEM_SPEC] * 9,
        out_shape=[
            pltpu.VMEM((tokens, 3 * inner), BF16),
            pltpu.VMEM((tokens, inner), BF16),
            turned,
            turned,
            pltpu.VMEM((2, tokens), F32),
            pltpu.VMEM((width, 3 * inner), BF16),
            pltpu.VMEM((2, CONTEXT, inner), BF16),
            pltpu.VMEM((2, tokens, inner), F32),
            pltpu.VMEM(order.shape, BF16),
        ],
        scratch_shapes=[
            pltpu.SMEM((1,), jnp.int32),
            pltpu.VMEM((tokens, width), BF16),
            pltpu.VMEM((tokens, width), BF16),
            pltpu.VMEM((inner, width), BF16),
            pltpu.VMEM((tokens, width), BF16),
            pltpu.SemaphoreType.DMA((8,)),
        ],
        compiler_params=params(24),
        cost_estimate=cost(12 * tokens * width * inner, 10 * inner * width),
        name="front",
    )(places, lengths, *[in_hbm(o) for o in (order, frames, cotangent, w_qkv, w_out)])


def pair_columns(pair, inner):
    return [slice(n * inner + pair * PAIR, n * inner + (pair + 1) * PAIR) for n in range(3)]


def attend(begin, length, inner, operands, results):
    lane = lax.broadcasted_iota(jnp.int32, (CONTEXT, PAIR), 1)
    heads = (lane < HEAD_DIM, lane >= HEAD_DIM)
    row_valid = begin + lax.broadcasted_iota(jnp.int32, (CONTEXT, PAIR), 0) < length
    col_valid = begin + lane < length
    keys = lax.broadcasted_iota(jnp.int32, (2 * CONTEXT, 2 * CONTEXT), 0)
    queries = lax.broadcasted_iota(jnp.int32, (2 * CONTEXT, 2 * CONTEXT), 1)
    key_block = keys // GROUP
    query_block = (queries % CONTEXT) // GROUP
    key_place = begin - CONTEXT + keys
    seen = (key_block >= query_block) & (key_block <= query_block + LEFT) & (key_place >= 0) & (key_place < length)
    zero = jnp.zeros((CONTEXT, PAIR), BF16)
    scale = HEAD_DIM ** (-0.5)

    def unstack(both):
        return jnp.concatenate([both[:HEAD_DIM, :CONTEXT], both[HEAD_DIM:, CONTEXT:]], axis=0)

    for pair in range(inner // PAIR):
        q, k2, v2, do = operands(pair)
        do = jnp.where(row_valid, do, zero)
        q = q * jnp.asarray(scale, BF16)
        q2 = jnp.concatenate([jnp.where(h, q, zero) for h in heads], axis=0)
        do2 = jnp.concatenate([jnp.where(h, do, zero) for h in heads], axis=0)
        scores = jnp.where(seen, dot(k2, q2, NT), -1e30)
        dprob = dot(v2, do2, NT)
        highest = jnp.max(scores, axis=0, keepdims=True)
        raised = jnp.exp(scores - highest)
        prob = raised * (1.0 / jnp.sum(raised, axis=0, keepdims=True))
        rounded = prob.astype(BF16)
        mixed = jnp.where(col_valid, unstack(dot(v2.T, rounded)), 0.0).T.astype(BF16)
        weighed = prob * dprob
        dscores = (weighed - prob * jnp.sum(weighed, axis=0, keepdims=True)).astype(BF16)
        dq = (unstack(dot(k2.T, dscores)) * scale).T.astype(BF16)
        results(pair, mixed, dq, dot(dscores, q2), dot(rounded, do2))


def early_kernel(
    places, lengths_ref, order_ref, frames_ref, weight_ref, qkv_ref, do_ref, late_ref, add_ref,
    out_ref, dkv_ref, turned_ref, length, normed, halo, sem,
):
    fetch = pltpu.make_async_copy(lengths_ref, length, sem)
    fetch.start()
    inner = do_ref.shape[1]
    rows = qkv_ref.shape[0]
    here = places[1]
    values = frames_ref[...].astype(F32)
    average, inverse = statistics(values)
    normed[...] = ((values - average) * inverse).astype(BF16)
    halo[...] = dot(normed[...], weight_ref[:, inner:]).astype(BF16)
    out_ref[:, CONTEXT:, :] = late_ref[...]
    dkv_ref[:, CONTEXT:rows, :inner] = add_ref[:, CONTEXT:, :].astype(BF16)

    def store(at, own, other):
        turned_ref[at, :] = own
        half = dkv_ref.shape[1]
        for n in range(2):
            first, last = max(at.start, n * half), min(at.stop, (n + 1) * half)
            if first < last:
                dkv_ref[n, first - n * half : last - n * half, inner:] = other[first - at.start : last - at.start]

    turn(normed, order_ref, here, store)

    def operands(pair):
        q, k, v = pair_columns(pair, inner)
        k2 = jnp.concatenate([halo[:, q], qkv_ref[:CONTEXT, k]], axis=0)
        v2 = jnp.concatenate([halo[:, k], qkv_ref[:CONTEXT, v]], axis=0)
        return qkv_ref[:CONTEXT, q], k2, v2, do_ref[:CONTEXT, q]

    def results(pair, mixed, dq, dk, dv):
        at = pair_columns(pair, inner)[0]
        out_ref[0, :CONTEXT, at] = mixed
        out_ref[1, :CONTEXT, at] = dq
        for n, grad in enumerate((dk, dv)):
            dkv_ref[n, rows:, at] = grad[:CONTEXT].astype(BF16)
            dkv_ref[n, :CONTEXT, at] = (grad[CONTEXT:] + add_ref[n, :CONTEXT, at]).astype(BF16)

    fetch.wait()
    attend(places[0], length[0], inner, operands, results)


def early_tile(places, lengths, order, frames, weight, qkv, attended_grad, late, late_grad):
    rows, inner = attended_grad.shape
    width = frames.shape[1]
    return pl.pallas_call(
        early_kernel,
        in_specs=[SMEM_SPEC, HBM_SPEC] + [VMEM_SPEC] * 7,
        out_specs=[VMEM_SPEC] * 3,
        out_shape=[
            pltpu.VMEM((2, rows, inner), BF16),
            pltpu.VMEM((2, rows + CONTEXT, inner + CONTEXT), BF16),
            pltpu.VMEM((width // CORES, CONTEXT), BF16),
        ],
        scratch_shapes=[
            pltpu.SMEM((1,), jnp.int32),
            pltpu.VMEM((CONTEXT, width), BF16),
            pltpu.VMEM((CONTEXT, 2 * inner), BF16),
            pltpu.SemaphoreType.DMA,
        ],
        compiler_params=params(16),
        cost_estimate=cost(28 * CONTEXT * 2 * CONTEXT * inner, 16 * CONTEXT * inner, CONTEXT * 4 * inner),
        name="attention_early",
    )(places, lengths, *[in_vmem(o) for o in (order, frames, weight, qkv, attended_grad, late, late_grad)])


def store_section(chunks, route, n, total, outs, held):
    half = CHUNKS // 2
    held[n] = total.reshape(held.shape[1:])
    for slot in range(CHUNKS):
        outs[n if slot < half else 2 + n][slot % half] = held[n, chunks[route, slot]].astype(BF16)


def own_kernel(left_ref, behind_ref, first_ref, second_ref, first_out, second_out):
    tokens = first_ref.shape[1]
    inner = first_ref.shape[2]
    left = jnp.concatenate([left_ref[:, :tokens], behind_ref[...]], axis=1)
    first_out[0] = dot(left_ref[:, tokens:], first_ref[0])
    first_out[1] = dot(left_ref[:, :tokens], first_ref[1])
    for n in range(2):
        second_out[n] = dot(left, second_ref[n, :, :inner])


def own_sums(left, behind, first, second):
    rows, inner = left.shape[0], first.shape[2]
    return pl.pallas_call(
        own_kernel,
        in_specs=[VMEM_SPEC] * 4,
        out_specs=[VMEM_SPEC] * 2,
        out_shape=[pltpu.VMEM((2, rows, inner), F32)] * 2,
        compiler_params=params(8),
        cost_estimate=cost(4 * 10**9, 1),
        name="own_sums",
    )(*[in_vmem(o) for o in (left, behind, first, second)])


def first_wave_kernel(chunks, left_other_ref, right_other_ref, own_ref, *refs):
    tokens = right_other_ref.shape[1]
    for n, at in enumerate((slice(tokens, 2 * tokens), slice(0, tokens))):
        total = own_ref[n] + dot(left_other_ref[:, at], right_other_ref[n])
        store_section(chunks, n, n, total, refs[:-1], refs[-1])


def second_wave_kernel(chunks, left_other_ref, right_other_ref, own_ref, *refs):
    tokens = left_other_ref.shape[1] // 2
    inner = right_other_ref.shape[2] - CONTEXT
    behind = jnp.concatenate([right_other_ref[n, :, inner:] for n in range(2)], axis=0)
    left = jnp.concatenate([left_other_ref[:, :tokens], behind], axis=1)
    for n in range(2):
        total = own_ref[n] + dot(left, right_other_ref[n, :, :inner])
        store_section(chunks, 2 + n, n, total, refs[:-1], refs[-1])


def weight_sections(kernel, chunks, operands, inner, flops, name):
    size = (operands[0].shape[0] // CHUNKS, inner)
    routes = 2
    outs = pl.pallas_call(
        kernel,
        in_specs=[SMEM_SPEC] + [VMEM_SPEC] * len(operands),
        out_specs=[VMEM_SPEC] * (2 * routes),
        out_shape=[pltpu.VMEM((CHUNKS // 2, *size), BF16)] * (2 * routes),
        scratch_shapes=[pltpu.VMEM((routes, CHUNKS, *size), F32)],
        compiler_params=params(24),
        cost_estimate=cost(flops, 1),
        name=name,
    )(chunks, *[in_vmem(o) for o in operands])
    return outs[:routes], outs[routes:]


def plus(*terms):
    return sum(t.astype(F32) for t in terms).astype(BF16)


def halve_kernel(*refs):
    for route in range(2):
        keep, got, kept, sent = refs[route::2]
        count = kept.shape[0]
        for ref, at in ((kept, slice(0, count)), (sent, slice(count, 2 * count))):
            ref[...] = (keep[at].astype(F32) + got[at].astype(F32)).astype(BF16)


def halve(keep, gots):
    count, *size = keep[0].shape
    outs = pl.pallas_call(
        halve_kernel,
        in_specs=[VMEM_SPEC] * 4,
        out_specs=[VMEM_SPEC] * 4,
        out_shape=[pltpu.VMEM((count // 2, *size), BF16)] * 4,
        compiler_params=params(8),
        cost_estimate=cost(1, 1),
        name="halve",
    )(*[in_vmem(o) for o in (*keep, *gots)])
    return outs[:2], outs[2:]


def pieces_kernel(*refs):
    ins, out_ref, held = refs[:-2], refs[-2], refs[-1]
    for ref, places in zip(ins, ((3, 0), (1, 2))):
        block = ref[...].astype(F32)
        tiles = block.shape[1] // PAIR // 2
        share = block.shape[0] // Z
        for n, place in enumerate(places):
            for t in range(tiles):
                rows = slice((place * tiles + t) * share, (place * tiles + t + 1) * share)
                column = (n * tiles + t) * PAIR
                for z in range(Z):
                    held[z, rows, :] = block[z * share : (z + 1) * share, column : column + PAIR]
    out_ref[...] = held[...].astype(BF16)


def total_kernel(in_ref, out_ref):
    total = in_ref[0].astype(F32)
    for z in range(1, Z):
        total += in_ref[z].astype(F32)
    share = out_ref.shape[0]
    for t in range(out_ref.shape[1] // PAIR):
        out_ref[:, t * PAIR : (t + 1) * PAIR] = total[t * share : (t + 1) * share]


def on_device(frames, cotangent, lengths, w_qkv, w_out):
    frame_rows = frames[0]
    grad_rows = cotangent[0]
    row_count, width = frame_rows.shape
    inner = w_out.shape[0]
    seq_index = lax.axis_index("seq")
    dp_index = lax.axis_index("dp")
    xl = seq_index % XL
    core, xh, y = dp_index % CORES, dp_index // CORES % XH, dp_index // (CORES * XH)
    places = jnp.stack([seq_index * row_count, core])
    chunks = jnp.stack([chunk_at(r, jnp.arange(CHUNKS), y, xh, xl) for r in range(len(ROUTES))])

    behind = from_behind(last_rows(frame_rows), "seq", 1)
    frame_rows, places, chunks = lax.optimization_barrier((frame_rows, places, chunks))
    qkv, attended_grad, left, left_out, stats, weight, late, late_grad, order = front(
        places, lengths, frame_rows, grad_rows, w_qkv, w_out
    )
    left_other = to_device(left_out, to_core)
    own, grads, left_behind = early_tile(places, lengths, order, behind, weight, qkv, attended_grad, late, late_grad)
    own_other = to_device(own, to_core)
    own_sum, grads_sum = own_sums(left, left_behind, own, grads)
    own_other, left_other, own_sum, grads_sum, grads = lax.optimization_barrier(
        (own_other, left_other, own_sum, grads_sum, grads)
    )
    grads_other = to_device(grads, to_core)
    keep_a, send_a = weight_sections(first_wave_kernel, chunks, (left_other, own_other, own_sum), inner, 1, "first_wave")
    keep_b, send_b = weight_sections(
        second_wave_kernel, chunks, (left_other, grads_other, grads_sum), inner, 3 * 10**9, "second_wave"
    )
    query_grad = jnp.concatenate([own[1], jnp.zeros((CONTEXT, inner), BF16)], axis=0)
    projected_grad = jnp.concatenate([query_grad, grads[0, :, :inner], grads[1, :, :inner]], axis=1)
    attended, projected_grad, send_b = lax.optimization_barrier((own[0], projected_grad, send_b))
    block_out = dot(attended, w_out).astype(BF16)
    def second_ring(kept, gots, n, *after):
        group = jnp.concatenate([plus(kept[r], gots[r]) for r in range(2)], axis=-1)
        slots, *after = lax.optimization_barrier(([group[slot] for slot in range(1, 4)], *after))
        others = [to_device(slots[i], OWNERS[n][i]) for i in (2, 0, 1)]
        return plus(group[0], *others), *after

    gots_a = [to_device(send_a[r], ROUTES[r][0]) for r in range(2)]
    gots_b = [to_device(send_b[r], ROUTES[2 + r][0]) for r in range(2)]
    gots_a, block_out = lax.optimization_barrier((gots_a, block_out))
    kept_a, sent_a = halve(keep_a, gots_a)
    gots_a = [to_device(sent_a[r], ROUTES[r][1]) for r in range(2)]
    kept_b, sent_b = halve(keep_b, gots_b)
    projected_grad, sent_b = lax.optimization_barrier((projected_grad, sent_b))
    gots_b = [to_device(sent_b[r], ROUTES[2 + r][1]) for r in range(2)]
    normed_grad = dot(projected_grad, w_qkv, NT)
    gots_a, normed_grad = lax.optimization_barrier((gots_a, normed_grad))
    first_group, = second_ring(kept_a, gots_a, 0)
    second_group, normed_grad = second_ring(kept_b, gots_b, 1, normed_grad)
    groups = [first_group, second_group]
    returned = from_behind(normed_grad[row_count:].astype(BF16), "seq", -1)
    returned = jnp.concatenate([jnp.zeros((row_count - CONTEXT, width), BF16), returned], axis=0)
    normed_grad = (normed_grad[:row_count] + returned.astype(F32)).astype(BF16)
    frame_grad = normalize_grad(frame_rows.astype(F32), stats[0][:, None], stats[1][:, None], normed_grad.astype(F32))
    share = width // (CHUNKS * CORES * Z)
    tiles = 4 * inner // PAIR
    shares = pl.pallas_call(
        pieces_kernel,
        in_specs=[VMEM_SPEC] * 2,
        out_shape=jax.ShapeDtypeStruct((Z, tiles * share, PAIR), BF16),
        scratch_shapes=[pltpu.VMEM((Z, tiles * share, PAIR), F32)],
        compiler_params=params(24),
        name="pieces",
    )(*[in_vmem(g) for g in groups])
    rings = [[place * XL + x for place in range(Z)] for x in range(XL)]
    shares = lax.all_to_all(shares, "seq", 0, 0, axis_index_groups=rings, tiled=True)
    total = pl.pallas_call(
        total_kernel,
        in_specs=[VMEM_SPEC],
        out_shape=jax.ShapeDtypeStruct((share, 4 * inner), F32),
        compiler_params=params(24),
        name="total",
    )(in_vmem(shares))
    return block_out[None], frame_grad.astype(BF16)[None], total


def solution(mesh):
    placed = (P("dp", "seq", None), P("dp", "seq", None), P("dp"), P(), P())
    return jax.shard_map(
        on_device,
        mesh=mesh,
        in_specs=placed,
        out_specs=(P("dp", "seq", None), P("dp", "seq", None), P(("dp", "seq"), None)),
        check_vma=False,
    )
```

```python
import jax
import jax.numpy as jnp
import numpy as np
from jax import lax
from jax.experimental import pallas as pl
from jax.experimental.pallas import tpu as pltpu
from jax.sharding import PartitionSpec as P

HEAD_DIM = 64
GROUP = 32
LEFT = 4
CONTEXT = LEFT * GROUP
PAIR = 2 * HEAD_DIM
F32 = jnp.float32
BF16 = jnp.bfloat16
NT = (((1,), (1,)), ((), ()))
NN = (((1,), (0,)), ((), ()))

Y, XH, CORES, Z, XL = 4, 2, 2, 8, 2
CHUNKS = Y * XH * XL

epsilon = 1e-05


def dot(a, b, dims=NN):
    return lax.dot_general(a, b, dims, preferred_element_type=F32)


def from_behind(value, axis, by):
    peers = lax.axis_size(axis)
    return lax.ppermute(value, axis, [(i, (i + by) % peers) for i in range(peers)])


def flat(y, xh, core, z, xl):
    return ((y * XH + xh) * CORES + core) * (Z * XL) + z * XL + xl


def to_device(value, where):
    pairs = []
    for place in np.ndindex(Y, XH, CORES, Z, XL):
        pairs.append((flat(*place), flat(*where(*place))))
    return lax.ppermute(value, ("dp", "seq"), pairs)


def to_core(y, xh, core, z, xl):
    return y, xh, 1 - core, z, xl


def to_x_near(y, xh, core, z, xl):
    return y, xh, core, z, 1 - xl


def to_x_mirror(y, xh, core, z, xl):
    return y, 1 - xh, core, z, 1 - xl


def to_y_near(y, xh, core, z, xl):
    return y ^ 1, xh, core, z, xl


def to_y_mirror(y, xh, core, z, xl):
    return 3 - y, xh, core, z, xl


def to_x_far(y, xh, core, z, xl):
    return y, 1 - xh, core, z, xl


def to_y_far(y, xh, core, z, xl):
    return y ^ 2, xh, core, z, xl


ROUTES = (
    (to_y_near, to_y_mirror),
    (to_y_mirror, to_y_near),
    (to_x_near, to_x_mirror),
    (to_x_mirror, to_x_near),
)
OWNERS = (
    (to_x_mirror, to_x_near, to_x_far),
    (to_y_mirror, to_y_near, to_y_far),
)


def halves(route, hi, lo):
    return (hi ^ lo, hi) if route % 2 == 0 else (hi, hi ^ lo)


def chunk_at(route, slot, y, xh, xl):
    bits = [(slot >> (3 - i)) & 1 for i in range(4)]
    x_first = route >= 2
    x_bits, y_bits = (bits[:2], bits[2:]) if x_first else (bits[2:], bits[:2])
    found = []
    for hi, lo, pair, order in ((y >> 1, y & 1, y_bits, 0 if x_first else route), (xh, xl, x_bits, route if x_first else 0)):
        first, second = halves(order, hi, lo)
        first, second = first ^ pair[0], second ^ pair[1]
        found.append((second, first ^ second) if order % 2 == 0 else (first, first ^ second))
    (yh, yl), (xh_to, xl_to) = found
    return ((yh * 2 + yl) * XH + xh_to) * XL + xl_to


def row_order(width):
    share = width // (CHUNKS * CORES * Z)
    order = np.arange(width // Y).reshape(XH, CORES, Z, XL, share).transpose(1, 0, 3, 2, 4).reshape(-1)
    return jnp.asarray(np.eye(width // Y, dtype=np.float32)[order], BF16)


def statistics(rows_in):
    average = jnp.mean(rows_in, axis=-1, keepdims=True)
    centered = rows_in - average
    variance = jnp.mean(centered * centered, axis=-1, keepdims=True)
    return average, lax.rsqrt(variance + epsilon)


def normalize_grad(rows_in, average, inverse, grad):
    normed = (rows_in - average) * inverse
    along = jnp.mean(grad * normed, axis=-1, keepdims=True)
    return inverse * (grad - jnp.mean(grad, axis=-1, keepdims=True) - normed * along)


SMEM_SPEC = pl.BlockSpec(memory_space=pltpu.SMEM)
VMEM_SPEC = pl.BlockSpec(memory_space=pltpu.VMEM)
HBM_SPEC = pl.BlockSpec(memory_space=pltpu.HBM)


def in_vmem(value):
    return pltpu.with_memory_space_constraint(value, pltpu.VMEM)


def in_hbm(value):
    return pltpu.with_memory_space_constraint(value, pltpu.HBM)


def cost(flops, nbytes, transcendentals=0):
    return pl.CostEstimate(flops=flops, bytes_accessed=nbytes, transcendentals=transcendentals)


def params(mebibytes):
    return pltpu.CompilerParams(vmem_limit_bytes=mebibytes * 2**20)


def turn(ref, order_ref, here, store):
    rows = order_ref.shape[0]
    half = rows // CORES
    for y in range(Y):
        turned = dot(order_ref[...], ref[:, y * rows : (y + 1) * rows].T).astype(BF16)
        first, second = turned[:half], turned[half:]
        at = slice(y * half, (y + 1) * half)
        store(at, jnp.where(here == 0, first, second), jnp.where(here == 0, second, first))


def last_rows(frames):
    rows, width = frames.shape

    pieces = 8

    def kernel(frames_ref, out_ref, sems):
        size = CONTEXT // pieces
        copies = [
            pltpu.make_async_copy(
                frames_ref.at[pl.ds(rows - CONTEXT + i * size, size)], out_ref.at[pl.ds(i * size, size)], sems.at[i]
            )
            for i in range(pieces)
        ]
        for copy in copies:
            copy.start()
        for copy in copies:
            copy.wait()

    return pl.pallas_call(
        kernel,
        in_specs=[HBM_SPEC],
        out_specs=VMEM_SPEC,
        out_shape=pltpu.VMEM((CONTEXT, width), BF16),
        scratch_shapes=[pltpu.SemaphoreType.DMA((pieces,))],
        compiler_params=params(4),
        cost_estimate=cost(1, 1),
        name="last_rows",
    )(in_hbm(frames))


def front_kernel(
    places, lengths_ref, order_ref, frames_ref, cotangent_ref, weight_ref, out_ref,
    qkv_ref, grad_ref, keep_ref, send_ref, stats_ref, weight, late_ref, dkv_ref, order,
    length, rows, cotangent, outer, normed, sems,
):
    here = places[1]
    tokens = rows.shape[0]
    thirds = weight.shape[1] // 3
    block = [slice(n * thirds, (n + 1) * thirds) for n in range(3)]
    small = [
        pltpu.make_async_copy(order_ref, order, sems.at[6]),
        pltpu.make_async_copy(lengths_ref, length, sems.at[7]),
    ]
    copies = [
        pltpu.make_async_copy(frames_ref, rows, sems.at[0]),
        pltpu.make_async_copy(cotangent_ref, cotangent, sems.at[1]),
        pltpu.make_async_copy(out_ref, outer, sems.at[2]),
    ] + [
        pltpu.make_async_copy(weight_ref.at[:, pl.ds(n * thirds, thirds)], weight.at[:, pl.ds(n * thirds, thirds)], sems.at[3 + n])
        for n in range(3)
    ]
    for copy in copies[:1] + small + copies[1:]:
        copy.start()

    def put(columns):
        def store(at, own, other):
            keep_ref[at, columns] = own
            send_ref[at, columns] = other

        return store

    copies[0].wait()
    values = rows[...].astype(F32)
    average, inverse = statistics(values)
    for n, column in enumerate((average, inverse)):
        stats_ref[n : n + 1, :] = jnp.broadcast_to(column, (tokens, PAIR)).T[:1]
    normed[...] = ((values - average) * inverse).astype(BF16)
    small[0].wait()
    turn(normed, order, here, put(slice(0, tokens)))
    copies[1].wait()
    turn(cotangent, order, here, put(slice(tokens, 2 * tokens)))
    copies[2].wait()
    grad_ref[...] = dot(cotangent[...], outer[...], NT).astype(BF16)
    for n in range(3):
        copies[3 + n].wait()
    qkv_ref[...] = dot(normed[...], weight[...]).astype(BF16)

    inner = thirds

    def operands(pair):
        q, k, v = pair_columns(pair, inner)
        return qkv_ref[CONTEXT:, q], qkv_ref[:, k], qkv_ref[:, v], grad_ref[CONTEXT:, q]

    def results(pair, mixed, dq, dk, dv):
        at = pair_columns(pair, inner)[0]
        late_ref[0, :, at] = mixed
        late_ref[1, :, at] = dq
        dkv_ref[0, :, at] = dk
        dkv_ref[1, :, at] = dv

    small[1].wait()
    attend(places[0] + CONTEXT, length[0], inner, operands, results)


def front(places, lengths, frames, cotangent, w_qkv, w_out):
    tokens, width = frames.shape
    inner = w_out.shape[0]
    order = row_order(width)
    turned = pltpu.VMEM((width // CORES, 2 * tokens), BF16)
    return pl.pallas_call(
        front_kernel,
        in_specs=[SMEM_SPEC] + [HBM_SPEC] * 6,
        out_specs=[VMEM_SPEC] * 9,
        out_shape=[
            pltpu.VMEM((tokens, 3 * inner), BF16),
            pltpu.VMEM((tokens, inner), BF16),
            turned,
            turned,
            pltpu.VMEM((2, tokens), F32),
            pltpu.VMEM((width, 3 * inner), BF16),
            pltpu.VMEM((2, CONTEXT, inner), BF16),
            pltpu.VMEM((2, tokens, inner), F32),
            pltpu.VMEM(order.shape, BF16),
        ],
        scratch_shapes=[
            pltpu.SMEM((1,), jnp.int32),
            pltpu.VMEM((tokens, width), BF16),
            pltpu.VMEM((tokens, width), BF16),
            pltpu.VMEM((inner, width), BF16),
            pltpu.VMEM((tokens, width), BF16),
            pltpu.SemaphoreType.DMA((8,)),
        ],
        compiler_params=params(24),
        cost_estimate=cost(12 * tokens * width * inner, 10 * inner * width),
        name="front",
    )(places, lengths, *[in_hbm(o) for o in (order, frames, cotangent, w_qkv, w_out)])


def pair_columns(pair, inner):
    return [slice(n * inner + pair * PAIR, n * inner + (pair + 1) * PAIR) for n in range(3)]


def attend(begin, length, inner, operands, results):
    lane = lax.broadcasted_iota(jnp.int32, (CONTEXT, PAIR), 1)
    heads = (lane < HEAD_DIM, lane >= HEAD_DIM)
    row_valid = begin + lax.broadcasted_iota(jnp.int32, (CONTEXT, PAIR), 0) < length
    col_valid = begin + lane < length
    keys = lax.broadcasted_iota(jnp.int32, (2 * CONTEXT, 2 * CONTEXT), 0)
    queries = lax.broadcasted_iota(jnp.int32, (2 * CONTEXT, 2 * CONTEXT), 1)
    key_block = keys // GROUP
    query_block = (queries % CONTEXT) // GROUP
    key_place = begin - CONTEXT + keys
    seen = (key_block >= query_block) & (key_block <= query_block + LEFT) & (key_place >= 0) & (key_place < length)
    zero = jnp.zeros((CONTEXT, PAIR), BF16)
    scale = HEAD_DIM ** (-0.5)

    def unstack(both):
        return jnp.concatenate([both[:HEAD_DIM, :CONTEXT], both[HEAD_DIM:, CONTEXT:]], axis=0)

    for pair in range(inner // PAIR):
        q, k2, v2, do = operands(pair)
        do = jnp.where(row_valid, do, zero)
        q = q * jnp.asarray(scale, BF16)
        q2 = jnp.concatenate([jnp.where(h, q, zero) for h in heads], axis=0)
        do2 = jnp.concatenate([jnp.where(h, do, zero) for h in heads], axis=0)
        scores = jnp.where(seen, dot(k2, q2, NT), -1e30)
        dprob = dot(v2, do2, NT)
        highest = jnp.max(scores, axis=0, keepdims=True)
        raised = jnp.exp(scores - highest)
        prob = raised * (1.0 / jnp.sum(raised, axis=0, keepdims=True))
        rounded = prob.astype(BF16)
        mixed = jnp.where(col_valid, unstack(dot(v2.T, rounded)), 0.0).T.astype(BF16)
        weighed = prob * dprob
        dscores = (weighed - prob * jnp.sum(weighed, axis=0, keepdims=True)).astype(BF16)
        dq = (unstack(dot(k2.T, dscores)) * scale).T.astype(BF16)
        results(pair, mixed, dq, dot(dscores, q2), dot(rounded, do2))


def early_kernel(
    places, lengths_ref, order_ref, frames_ref, weight_ref, qkv_ref, do_ref, late_ref, add_ref,
    out_ref, dkv_ref, turned_ref, length, normed, halo, sem,
):
    fetch = pltpu.make_async_copy(lengths_ref, length, sem)
    fetch.start()
    inner = do_ref.shape[1]
    rows = qkv_ref.shape[0]
    here = places[1]
    values = frames_ref[...].astype(F32)
    average, inverse = statistics(values)
    normed[...] = ((values - average) * inverse).astype(BF16)
    halo[...] = dot(normed[...], weight_ref[:, inner:]).astype(BF16)
    out_ref[:, CONTEXT:, :] = late_ref[...]
    dkv_ref[:, CONTEXT:rows, :inner] = add_ref[:, CONTEXT:, :].astype(BF16)

    def store(at, own, other):
        turned_ref[at, :] = own
        half = dkv_ref.shape[1]
        for n in range(2):
            first, last = max(at.start, n * half), min(at.stop, (n + 1) * half)
            if first < last:
                dkv_ref[n, first - n * half : last - n * half, inner:] = other[first - at.start : last - at.start]

    turn(normed, order_ref, here, store)

    def operands(pair):
        q, k, v = pair_columns(pair, inner)
        k2 = jnp.concatenate([halo[:, q], qkv_ref[:CONTEXT, k]], axis=0)
        v2 = jnp.concatenate([halo[:, k], qkv_ref[:CONTEXT, v]], axis=0)
        return qkv_ref[:CONTEXT, q], k2, v2, do_ref[:CONTEXT, q]

    def results(pair, mixed, dq, dk, dv):
        at = pair_columns(pair, inner)[0]
        out_ref[0, :CONTEXT, at] = mixed
        out_ref[1, :CONTEXT, at] = dq
        for n, grad in enumerate((dk, dv)):
            dkv_ref[n, rows:, at] = grad[:CONTEXT].astype(BF16)
            dkv_ref[n, :CONTEXT, at] = (grad[CONTEXT:] + add_ref[n, :CONTEXT, at]).astype(BF16)

    fetch.wait()
    attend(places[0], length[0], inner, operands, results)


def early_tile(places, lengths, order, frames, weight, qkv, attended_grad, late, late_grad):
    rows, inner = attended_grad.shape
    width = frames.shape[1]
    return pl.pallas_call(
        early_kernel,
        in_specs=[SMEM_SPEC, HBM_SPEC] + [VMEM_SPEC] * 7,
        out_specs=[VMEM_SPEC] * 3,
        out_shape=[
            pltpu.VMEM((2, rows, inner), BF16),
            pltpu.VMEM((2, rows + CONTEXT, inner + CONTEXT), BF16),
            pltpu.VMEM((width // CORES, CONTEXT), BF16),
        ],
        scratch_shapes=[
            pltpu.SMEM((1,), jnp.int32),
            pltpu.VMEM((CONTEXT, width), BF16),
            pltpu.VMEM((CONTEXT, 2 * inner), BF16),
            pltpu.SemaphoreType.DMA,
        ],
        compiler_params=params(16),
        cost_estimate=cost(28 * CONTEXT * 2 * CONTEXT * inner, 16 * CONTEXT * inner, CONTEXT * 4 * inner),
        name="attention_early",
    )(places, lengths, *[in_vmem(o) for o in (order, frames, weight, qkv, attended_grad, late, late_grad)])


def store_section(chunks, route, n, total, outs, held):
    half = CHUNKS // 2
    held[n] = total.reshape(held.shape[1:])
    for slot in range(CHUNKS):
        outs[n if slot < half else 2 + n][slot % half] = held[n, chunks[route, slot]].astype(BF16)


def own_kernel(left_ref, behind_ref, first_ref, second_ref, first_out, second_out):
    tokens = first_ref.shape[1]
    inner = first_ref.shape[2]
    left = jnp.concatenate([left_ref[:, :tokens], behind_ref[...]], axis=1)
    first_out[0] = dot(left_ref[:, tokens:], first_ref[0])
    first_out[1] = dot(left_ref[:, :tokens], first_ref[1])
    for n in range(2):
        second_out[n] = dot(left, second_ref[n, :, :inner])


def own_sums(left, behind, first, second):
    rows, inner = left.shape[0], first.shape[2]
    return pl.pallas_call(
        own_kernel,
        in_specs=[VMEM_SPEC] * 4,
        out_specs=[VMEM_SPEC] * 2,
        out_shape=[pltpu.VMEM((2, rows, inner), F32)] * 2,
        compiler_params=params(8),
        cost_estimate=cost(4 * 10**9, 1),
        name="own_sums",
    )(*[in_vmem(o) for o in (left, behind, first, second)])


def first_wave_kernel(chunks, left_other_ref, right_other_ref, own_ref, *refs):
    tokens = right_other_ref.shape[1]
    for n, at in enumerate((slice(tokens, 2 * tokens), slice(0, tokens))):
        total = own_ref[n] + dot(left_other_ref[:, at], right_other_ref[n])
        store_section(chunks, n, n, total, refs[:-1], refs[-1])


def second_wave_kernel(chunks, left_other_ref, right_other_ref, own_ref, *refs):
    tokens = left_other_ref.shape[1] // 2
    inner = right_other_ref.shape[2] - CONTEXT
    behind = jnp.concatenate([right_other_ref[n, :, inner:] for n in range(2)], axis=0)
    left = jnp.concatenate([left_other_ref[:, :tokens], behind], axis=1)
    for n in range(2):
        total = own_ref[n] + dot(left, right_other_ref[n, :, :inner])
        store_section(chunks, 2 + n, n, total, refs[:-1], refs[-1])


def weight_sections(kernel, chunks, operands, inner, flops, name):
    size = (operands[0].shape[0] // CHUNKS, inner)
    routes = 2
    outs = pl.pallas_call(
        kernel,
        in_specs=[SMEM_SPEC] + [VMEM_SPEC] * len(operands),
        out_specs=[VMEM_SPEC] * (2 * routes),
        out_shape=[pltpu.VMEM((CHUNKS // 2, *size), BF16)] * (2 * routes),
        scratch_shapes=[pltpu.VMEM((routes, CHUNKS, *size), F32)],
        compiler_params=params(24),
        cost_estimate=cost(flops, 1),
        name=name,
    )(chunks, *[in_vmem(o) for o in operands])
    return outs[:routes], outs[routes:]


def plus(*terms):
    return sum(t.astype(F32) for t in terms).astype(BF16)


def halve_kernel(*refs):
    for route in range(2):
        keep, got, kept, sent = refs[route::2]
        count = kept.shape[0]
        for ref, at in ((kept, slice(0, count)), (sent, slice(count, 2 * count))):
            ref[...] = (keep[at].astype(F32) + got[at].astype(F32)).astype(BF16)


def halve(keep, gots):
    count, *size = keep[0].shape
    outs = pl.pallas_call(
        halve_kernel,
        in_specs=[VMEM_SPEC] * 4,
        out_specs=[VMEM_SPEC] * 4,
        out_shape=[pltpu.VMEM((count // 2, *size), BF16)] * 4,
        compiler_params=params(8),
        cost_estimate=cost(1, 1),
        name="halve",
    )(*[in_vmem(o) for o in (*keep, *gots)])
    return outs[:2], outs[2:]


def pieces_kernel(*refs):
    ins, out_ref, held = refs[:-2], refs[-2], refs[-1]
    for ref, places in zip(ins, ((3, 0), (1, 2))):
        block = ref[...].astype(F32)
        tiles = block.shape[1] // PAIR // 2
        share = block.shape[0] // Z
        for n, place in enumerate(places):
            for t in range(tiles):
                rows = slice((place * tiles + t) * share, (place * tiles + t + 1) * share)
                column = (n * tiles + t) * PAIR
                for z in range(Z):
                    held[z, rows, :] = block[z * share : (z + 1) * share, column : column + PAIR]
    out_ref[...] = held[...].astype(BF16)


def total_kernel(in_ref, out_ref):
    total = in_ref[0].astype(F32)
    for z in range(1, Z):
        total += in_ref[z].astype(F32)
    share = out_ref.shape[0]
    for t in range(out_ref.shape[1] // PAIR):
        out_ref[:, t * PAIR : (t + 1) * PAIR] = total[t * share : (t + 1) * share]


def on_device(frames, cotangent, lengths, w_qkv, w_out):
    frame_rows = frames[0]
    grad_rows = cotangent[0]
    row_count, width = frame_rows.shape
    inner = w_out.shape[0]
    seq_index = lax.axis_index("seq")
    dp_index = lax.axis_index("dp")
    xl = seq_index % XL
    core, xh, y = dp_index % CORES, dp_index // CORES % XH, dp_index // (CORES * XH)
    places = jnp.stack([seq_index * row_count, core])
    chunks = jnp.stack([chunk_at(r, jnp.arange(CHUNKS), y, xh, xl) for r in range(len(ROUTES))])

    behind = from_behind(last_rows(frame_rows), "seq", 1)
    frame_rows, places, chunks = lax.optimization_barrier((frame_rows, places, chunks))
    qkv, attended_grad, left, left_out, stats, weight, late, late_grad, order = front(
        places, lengths, frame_rows, grad_rows, w_qkv, w_out
    )
    left_other = to_device(left_out, to_core)
    own, grads, left_behind = early_tile(places, lengths, order, behind, weight, qkv, attended_grad, late, late_grad)
    own_other = to_device(own, to_core)
    own_sum, grads_sum = own_sums(left, left_behind, own, grads)
    own_other, left_other, own_sum, grads_sum, grads = lax.optimization_barrier(
        (own_other, left_other, own_sum, grads_sum, grads)
    )
    grads_other = to_device(grads, to_core)
    keep_a, send_a = weight_sections(first_wave_kernel, chunks, (left_other, own_other, own_sum), inner, 1, "first_wave")
    keep_b, send_b = weight_sections(
        second_wave_kernel, chunks, (left_other, grads_other, grads_sum), inner, 3 * 10**9, "second_wave"
    )
    query_grad = jnp.concatenate([own[1], jnp.zeros((CONTEXT, inner), BF16)], axis=0)
    projected_grad = jnp.concatenate([query_grad, grads[0, :, :inner], grads[1, :, :inner]], axis=1)
    attended, projected_grad, send_b = lax.optimization_barrier((own[0], projected_grad, send_b))
    normed_grad = dot(projected_grad, w_qkv, NT)
    def second_ring(kept, gots, n, *after):
        group = jnp.concatenate([plus(kept[r], gots[r]) for r in range(2)], axis=-1)
        slots, *after = lax.optimization_barrier(([group[slot] for slot in range(1, 4)], *after))
        others = [to_device(slots[i], OWNERS[n][i]) for i in (2, 0, 1)]
        return plus(group[0], *others), *after

    gots_a = [to_device(send_a[r], ROUTES[r][0]) for r in range(2)]
    gots_b = [to_device(send_b[r], ROUTES[2 + r][0]) for r in range(2)]
    gots_a, normed_grad = lax.optimization_barrier((gots_a, normed_grad))
    kept_a, sent_a = halve(keep_a, gots_a)
    gots_a = [to_device(sent_a[r], ROUTES[r][1]) for r in range(2)]
    kept_b, sent_b = halve(keep_b, gots_b)
    attended, sent_b = lax.optimization_barrier((attended, sent_b))
    gots_b = [to_device(sent_b[r], ROUTES[2 + r][1]) for r in range(2)]
    block_out = dot(attended, w_out).astype(BF16)
    gots_a, block_out = lax.optimization_barrier((gots_a, block_out))
    first_group, = second_ring(kept_a, gots_a, 0)
    second_group, normed_grad = second_ring(kept_b, gots_b, 1, normed_grad)
    groups = [first_group, second_group]
    returned = from_behind(normed_grad[row_count:].astype(BF16), "seq", -1)
    returned = jnp.concatenate([jnp.zeros((row_count - CONTEXT, width), BF16), returned], axis=0)
    normed_grad = (normed_grad[:row_count] + returned.astype(F32)).astype(BF16)
    frame_grad = normalize_grad(frame_rows.astype(F32), stats[0][:, None], stats[1][:, None], normed_grad.astype(F32))
    share = width // (CHUNKS * CORES * Z)
    tiles = 4 * inner // PAIR
    shares = pl.pallas_call(
        pieces_kernel,
        in_specs=[VMEM_SPEC] * 2,
        out_shape=jax.ShapeDtypeStruct((Z, tiles * share, PAIR), BF16),
        scratch_shapes=[pltpu.VMEM((Z, tiles * share, PAIR), F32)],
        compiler_params=params(24),
        name="pieces",
    )(*[in_vmem(g) for g in groups])
    rings = [[place * XL + x for place in range(Z)] for x in range(XL)]
    shares = lax.all_to_all(shares, "seq", 0, 0, axis_index_groups=rings, tiled=True)
    total = pl.pallas_call(
        total_kernel,
        in_specs=[VMEM_SPEC],
        out_shape=jax.ShapeDtypeStruct((share, 4 * inner), F32),
        compiler_params=params(24),
        name="total",
    )(in_vmem(shares))
    return block_out[None], frame_grad.astype(BF16)[None], total


def solution(mesh):
    placed = (P("dp", "seq", None), P("dp", "seq", None), P("dp"), P(), P())
    return jax.shard_map(
        on_device,
        mesh=mesh,
        in_specs=placed,
        out_specs=(P("dp", "seq", None), P("dp", "seq", None), P(("dp", "seq"), None)),
        check_vma=False,
    )
```

```python
import jax
import jax.numpy as jnp
import numpy as np
from jax import lax
from jax.experimental import pallas as pl
from jax.experimental.pallas import tpu as pltpu
from jax.sharding import PartitionSpec as P

HEAD_DIM = 64
GROUP = 32
LEFT = 4
CONTEXT = LEFT * GROUP
PAIR = 2 * HEAD_DIM
F32 = jnp.float32
BF16 = jnp.bfloat16
NT = (((1,), (1,)), ((), ()))
NN = (((1,), (0,)), ((), ()))

Y, XH, CORES, Z, XL = 4, 2, 2, 8, 2
CHUNKS = Y * XH * XL

epsilon = 1e-05


def dot(a, b, dims=NN):
    return lax.dot_general(a, b, dims, preferred_element_type=F32)


def from_behind(value, axis, by):
    peers = lax.axis_size(axis)
    return lax.ppermute(value, axis, [(i, (i + by) % peers) for i in range(peers)])


def flat(y, xh, core, z, xl):
    return ((y * XH + xh) * CORES + core) * (Z * XL) + z * XL + xl


def to_device(value, where):
    pairs = []
    for place in np.ndindex(Y, XH, CORES, Z, XL):
        pairs.append((flat(*place), flat(*where(*place))))
    return lax.ppermute(value, ("dp", "seq"), pairs)


def to_core(y, xh, core, z, xl):
    return y, xh, 1 - core, z, xl


def to_x_near(y, xh, core, z, xl):
    return y, xh, core, z, 1 - xl


def to_x_mirror(y, xh, core, z, xl):
    return y, 1 - xh, core, z, 1 - xl


def to_y_near(y, xh, core, z, xl):
    return y ^ 1, xh, core, z, xl


def to_y_mirror(y, xh, core, z, xl):
    return 3 - y, xh, core, z, xl


def to_x_far(y, xh, core, z, xl):
    return y, 1 - xh, core, z, xl


def to_y_far(y, xh, core, z, xl):
    return y ^ 2, xh, core, z, xl


ROUTES = (
    (to_y_near, to_y_mirror),
    (to_y_mirror, to_y_near),
    (to_x_near, to_x_mirror),
    (to_x_mirror, to_x_near),
)
OWNERS = (
    (to_x_mirror, to_x_near, to_x_far),
    (to_y_mirror, to_y_near, to_y_far),
)


def halves(route, hi, lo):
    return (hi ^ lo, hi) if route % 2 == 0 else (hi, hi ^ lo)


def chunk_at(route, slot, y, xh, xl):
    bits = [(slot >> (3 - i)) & 1 for i in range(4)]
    x_first = route >= 2
    x_bits, y_bits = (bits[:2], bits[2:]) if x_first else (bits[2:], bits[:2])
    found = []
    for hi, lo, pair, order in ((y >> 1, y & 1, y_bits, 0 if x_first else route), (xh, xl, x_bits, route if x_first else 0)):
        first, second = halves(order, hi, lo)
        first, second = first ^ pair[0], second ^ pair[1]
        found.append((second, first ^ second) if order % 2 == 0 else (first, first ^ second))
    (yh, yl), (xh_to, xl_to) = found
    return ((yh * 2 + yl) * XH + xh_to) * XL + xl_to


def row_order(width):
    share = width // (CHUNKS * CORES * Z)
    order = np.arange(width // Y).reshape(XH, CORES, Z, XL, share).transpose(1, 0, 3, 2, 4).reshape(-1)
    return jnp.asarray(np.eye(width // Y, dtype=np.float32)[order], BF16)


def statistics(rows_in):
    average = jnp.mean(rows_in, axis=-1, keepdims=True)
    centered = rows_in - average
    variance = jnp.mean(centered * centered, axis=-1, keepdims=True)
    return average, lax.rsqrt(variance + epsilon)


def normalize_grad(rows_in, average, inverse, grad):
    normed = (rows_in - average) * inverse
    along = jnp.mean(grad * normed, axis=-1, keepdims=True)
    return inverse * (grad - jnp.mean(grad, axis=-1, keepdims=True) - normed * along)


SMEM_SPEC = pl.BlockSpec(memory_space=pltpu.SMEM)
VMEM_SPEC = pl.BlockSpec(memory_space=pltpu.VMEM)
HBM_SPEC = pl.BlockSpec(memory_space=pltpu.HBM)


def in_vmem(value):
    return pltpu.with_memory_space_constraint(value, pltpu.VMEM)


def in_hbm(value):
    return pltpu.with_memory_space_constraint(value, pltpu.HBM)


def cost(flops, nbytes, transcendentals=0):
    return pl.CostEstimate(flops=flops, bytes_accessed=nbytes, transcendentals=transcendentals)


def params(mebibytes):
    return pltpu.CompilerParams(vmem_limit_bytes=mebibytes * 2**20)


def turn(ref, order_ref, here, store):
    rows = order_ref.shape[0]
    half = rows // CORES
    for y in range(Y):
        turned = dot(order_ref[...], ref[:, y * rows : (y + 1) * rows].T).astype(BF16)
        first, second = turned[:half], turned[half:]
        at = slice(y * half, (y + 1) * half)
        store(at, jnp.where(here == 0, first, second), jnp.where(here == 0, second, first))


def last_rows(frames):
    rows, width = frames.shape

    pieces = 8

    def kernel(frames_ref, out_ref, sems):
        size = CONTEXT // pieces
        copies = [
            pltpu.make_async_copy(
                frames_ref.at[pl.ds(rows - CONTEXT + i * size, size)], out_ref.at[pl.ds(i * size, size)], sems.at[i]
            )
            for i in range(pieces)
        ]
        for copy in copies:
            copy.start()
        for copy in copies:
            copy.wait()

    return pl.pallas_call(
        kernel,
        in_specs=[HBM_SPEC],
        out_specs=VMEM_SPEC,
        out_shape=pltpu.VMEM((CONTEXT, width), BF16),
        scratch_shapes=[pltpu.SemaphoreType.DMA((pieces,))],
        compiler_params=params(4),
        cost_estimate=cost(1, 1),
        name="last_rows",
    )(in_hbm(frames))


def front_kernel(
    places, lengths_ref, order_ref, frames_ref, cotangent_ref, weight_ref, out_ref,
    qkv_ref, grad_ref, keep_ref, send_ref, stats_ref, weight, late_ref, dkv_ref, order,
    length, rows, cotangent, outer, normed, sems,
):
    here = places[1]
    tokens = rows.shape[0]
    thirds = weight.shape[1] // 3
    block = [slice(n * thirds, (n + 1) * thirds) for n in range(3)]
    small = [
        pltpu.make_async_copy(order_ref, order, sems.at[6]),
        pltpu.make_async_copy(lengths_ref, length, sems.at[7]),
    ]
    copies = [
        pltpu.make_async_copy(frames_ref, rows, sems.at[0]),
        pltpu.make_async_copy(cotangent_ref, cotangent, sems.at[1]),
        pltpu.make_async_copy(out_ref, outer, sems.at[2]),
    ] + [
        pltpu.make_async_copy(weight_ref.at[:, pl.ds(n * thirds, thirds)], weight.at[:, pl.ds(n * thirds, thirds)], sems.at[3 + n])
        for n in range(3)
    ]
    for copy in copies[:1] + small + copies[1:]:
        copy.start()

    def put(columns):
        def store(at, own, other):
            keep_ref[at, columns] = own
            send_ref[at, columns] = other

        return store

    copies[0].wait()
    values = rows[...].astype(F32)
    average, inverse = statistics(values)
    for n, column in enumerate((average, inverse)):
        stats_ref[n : n + 1, :] = jnp.broadcast_to(column, (tokens, PAIR)).T[:1]
    normed[...] = ((values - average) * inverse).astype(BF16)
    small[0].wait()
    turn(normed, order, here, put(slice(0, tokens)))
    copies[1].wait()
    turn(cotangent, order, here, put(slice(tokens, 2 * tokens)))
    copies[2].wait()
    grad_ref[...] = dot(cotangent[...], outer[...], NT).astype(BF16)
    for n in range(3):
        copies[3 + n].wait()
    qkv_ref[...] = dot(normed[...], weight[...]).astype(BF16)

    inner = thirds

    def operands(pair):
        q, k, v = pair_columns(pair, inner)
        return qkv_ref[CONTEXT:, q], qkv_ref[:, k], qkv_ref[:, v], grad_ref[CONTEXT:, q]

    def results(pair, mixed, dq, dk, dv):
        at = pair_columns(pair, inner)[0]
        late_ref[0, :, at] = mixed
        late_ref[1, :, at] = dq
        dkv_ref[0, :, at] = dk
        dkv_ref[1, :, at] = dv

    small[1].wait()
    attend(places[0] + CONTEXT, length[0], inner, operands, results)


def front(places, lengths, frames, cotangent, w_qkv, w_out):
    tokens, width = frames.shape
    inner = w_out.shape[0]
    order = row_order(width)
    turned = pltpu.VMEM((width // CORES, 2 * tokens), BF16)
    return pl.pallas_call(
        front_kernel,
        in_specs=[SMEM_SPEC] + [HBM_SPEC] * 6,
        out_specs=[VMEM_SPEC] * 9,
        out_shape=[
            pltpu.VMEM((tokens, 3 * inner), BF16),
            pltpu.VMEM((tokens, inner), BF16),
            turned,
            turned,
            pltpu.VMEM((2, tokens), F32),
            pltpu.VMEM((width, 3 * inner), BF16),
            pltpu.VMEM((2, CONTEXT, inner), BF16),
            pltpu.VMEM((2, tokens, inner), F32),
            pltpu.VMEM(order.shape, BF16),
        ],
        scratch_shapes=[
            pltpu.SMEM((1,), jnp.int32),
            pltpu.VMEM((tokens, width), BF16),
            pltpu.VMEM((tokens, width), BF16),
            pltpu.VMEM((inner, width), BF16),
            pltpu.VMEM((tokens, width), BF16),
            pltpu.SemaphoreType.DMA((8,)),
        ],
        compiler_params=params(24),
        cost_estimate=cost(12 * tokens * width * inner, 10 * inner * width),
        name="front",
    )(places, lengths, *[in_hbm(o) for o in (order, frames, cotangent, w_qkv, w_out)])


def pair_columns(pair, inner):
    return [slice(n * inner + pair * PAIR, n * inner + (pair + 1) * PAIR) for n in range(3)]


def attend(begin, length, inner, operands, results):
    lane = lax.broadcasted_iota(jnp.int32, (CONTEXT, PAIR), 1)
    heads = (lane < HEAD_DIM, lane >= HEAD_DIM)
    row_valid = begin + lax.broadcasted_iota(jnp.int32, (CONTEXT, PAIR), 0) < length
    col_valid = begin + lane < length
    keys = lax.broadcasted_iota(jnp.int32, (2 * CONTEXT, 2 * CONTEXT), 0)
    queries = lax.broadcasted_iota(jnp.int32, (2 * CONTEXT, 2 * CONTEXT), 1)
    key_block = keys // GROUP
    query_block = (queries % CONTEXT) // GROUP
    key_place = begin - CONTEXT + keys
    seen = (key_block >= query_block) & (key_block <= query_block + LEFT) & (key_place >= 0) & (key_place < length)
    zero = jnp.zeros((CONTEXT, PAIR), BF16)
    scale = HEAD_DIM ** (-0.5)

    def unstack(both):
        return jnp.concatenate([both[:HEAD_DIM, :CONTEXT], both[HEAD_DIM:, CONTEXT:]], axis=0)

    for pair in range(inner // PAIR):
        q, k2, v2, do = operands(pair)
        do = jnp.where(row_valid, do, zero)
        q = q * jnp.asarray(scale, BF16)
        q2 = jnp.concatenate([jnp.where(h, q, zero) for h in heads], axis=0)
        do2 = jnp.concatenate([jnp.where(h, do, zero) for h in heads], axis=0)
        scores = jnp.where(seen, dot(k2, q2, NT), -1e30)
        dprob = dot(v2, do2, NT)
        highest = jnp.max(scores, axis=0, keepdims=True)
        raised = jnp.exp(scores - highest)
        prob = raised * (1.0 / jnp.sum(raised, axis=0, keepdims=True))
        rounded = prob.astype(BF16)
        mixed = jnp.where(col_valid, unstack(dot(v2.T, rounded)), 0.0).T.astype(BF16)
        weighed = prob * dprob
        dscores = (weighed - prob * jnp.sum(weighed, axis=0, keepdims=True)).astype(BF16)
        dq = (unstack(dot(k2.T, dscores)) * scale).T.astype(BF16)
        results(pair, mixed, dq, dot(dscores, q2), dot(rounded, do2))


def early_kernel(
    places, lengths_ref, order_ref, frames_ref, weight_ref, qkv_ref, do_ref, late_ref, add_ref,
    out_ref, dkv_ref, turned_ref, length, normed, halo, sem,
):
    fetch = pltpu.make_async_copy(lengths_ref, length, sem)
    fetch.start()
    inner = do_ref.shape[1]
    rows = qkv_ref.shape[0]
    here = places[1]
    values = frames_ref[...].astype(F32)
    average, inverse = statistics(values)
    normed[...] = ((values - average) * inverse).astype(BF16)
    halo[...] = dot(normed[...], weight_ref[:, inner:]).astype(BF16)
    out_ref[:, CONTEXT:, :] = late_ref[...]
    dkv_ref[:, CONTEXT:rows, :inner] = add_ref[:, CONTEXT:, :].astype(BF16)

    def store(at, own, other):
        turned_ref[at, :] = own
        half = dkv_ref.shape[1]
        for n in range(2):
            first, last = max(at.start, n * half), min(at.stop, (n + 1) * half)
            if first < last:
                dkv_ref[n, first - n * half : last - n * half, inner:] = other[first - at.start : last - at.start]

    turn(normed, order_ref, here, store)

    def operands(pair):
        q, k, v = pair_columns(pair, inner)
        k2 = jnp.concatenate([halo[:, q], qkv_ref[:CONTEXT, k]], axis=0)
        v2 = jnp.concatenate([halo[:, k], qkv_ref[:CONTEXT, v]], axis=0)
        return qkv_ref[:CONTEXT, q], k2, v2, do_ref[:CONTEXT, q]

    def results(pair, mixed, dq, dk, dv):
        at = pair_columns(pair, inner)[0]
        out_ref[0, :CONTEXT, at] = mixed
        out_ref[1, :CONTEXT, at] = dq
        for n, grad in enumerate((dk, dv)):
            dkv_ref[n, rows:, at] = grad[:CONTEXT].astype(BF16)
            dkv_ref[n, :CONTEXT, at] = (grad[CONTEXT:] + add_ref[n, :CONTEXT, at]).astype(BF16)

    fetch.wait()
    attend(places[0], length[0], inner, operands, results)


def early_tile(places, lengths, order, frames, weight, qkv, attended_grad, late, late_grad):
    rows, inner = attended_grad.shape
    width = frames.shape[1]
    return pl.pallas_call(
        early_kernel,
        in_specs=[SMEM_SPEC, HBM_SPEC] + [VMEM_SPEC] * 7,
        out_specs=[VMEM_SPEC] * 3,
        out_shape=[
            pltpu.VMEM((2, rows, inner), BF16),
            pltpu.VMEM((2, rows + CONTEXT, inner + CONTEXT), BF16),
            pltpu.VMEM((width // CORES, CONTEXT), BF16),
        ],
        scratch_shapes=[
            pltpu.SMEM((1,), jnp.int32),
            pltpu.VMEM((CONTEXT, width), BF16),
            pltpu.VMEM((CONTEXT, 2 * inner), BF16),
            pltpu.SemaphoreType.DMA,
        ],
        compiler_params=params(16),
        cost_estimate=cost(28 * CONTEXT * 2 * CONTEXT * inner, 16 * CONTEXT * inner, CONTEXT * 4 * inner),
        name="attention_early",
    )(places, lengths, *[in_vmem(o) for o in (order, frames, weight, qkv, attended_grad, late, late_grad)])


def store_section(places, route, n, total, outs, held):
    half = CHUNKS // 2
    held[n] = total.reshape(held.shape[1:])
    for slot in range(CHUNKS):
        outs[n if slot < half else 2 + n][slot % half] = held[n, chunk_at(route, slot, places[2], places[3], places[4])].astype(BF16)


def own_kernel(left_ref, behind_ref, first_ref, second_ref, first_out, second_out):
    tokens = first_ref.shape[1]
    inner = first_ref.shape[2]
    left = jnp.concatenate([left_ref[:, :tokens], behind_ref[...]], axis=1)
    first_out[0] = dot(left_ref[:, tokens:], first_ref[0])
    first_out[1] = dot(left_ref[:, :tokens], first_ref[1])
    for n in range(2):
        second_out[n] = dot(left, second_ref[n, :, :inner])


def own_sums(left, behind, first, second):
    rows, inner = left.shape[0], first.shape[2]
    return pl.pallas_call(
        own_kernel,
        in_specs=[VMEM_SPEC] * 4,
        out_specs=[VMEM_SPEC] * 2,
        out_shape=[pltpu.VMEM((2, rows, inner), F32)] * 2,
        compiler_params=params(8),
        cost_estimate=cost(4 * 10**9, 1),
        name="own_sums",
    )(*[in_vmem(o) for o in (left, behind, first, second)])


def first_wave_kernel(places, left_other_ref, right_other_ref, own_ref, *refs):
    tokens = right_other_ref.shape[1]
    for n, at in enumerate((slice(tokens, 2 * tokens), slice(0, tokens))):
        total = own_ref[n] + dot(left_other_ref[:, at], right_other_ref[n])
        store_section(places, n, n, total, refs[:-1], refs[-1])


def second_wave_kernel(places, left_other_ref, right_other_ref, own_ref, *refs):
    tokens = left_other_ref.shape[1] // 2
    inner = right_other_ref.shape[2] - CONTEXT
    behind = jnp.concatenate([right_other_ref[n, :, inner:] for n in range(2)], axis=0)
    left = jnp.concatenate([left_other_ref[:, :tokens], behind], axis=1)
    for n in range(2):
        total = own_ref[n] + dot(left, right_other_ref[n, :, :inner])
        store_section(places, 2 + n, n, total, refs[:-1], refs[-1])


def weight_sections(kernel, places, operands, inner, flops, name):
    size = (operands[0].shape[0] // CHUNKS, inner)
    routes = 2
    outs = pl.pallas_call(
        kernel,
        in_specs=[SMEM_SPEC] + [VMEM_SPEC] * len(operands),
        out_specs=[VMEM_SPEC] * (2 * routes),
        out_shape=[pltpu.VMEM((CHUNKS // 2, *size), BF16)] * (2 * routes),
        scratch_shapes=[pltpu.VMEM((routes, CHUNKS, *size), F32)],
        compiler_params=params(24),
        cost_estimate=cost(flops, 1),
        name=name,
    )(places, *[in_vmem(o) for o in operands])
    return outs[:routes], outs[routes:]


def plus(*terms):
    return sum(t.astype(F32) for t in terms).astype(BF16)


def halve_kernel(*refs):
    for route in range(2):
        keep, got, kept, sent = refs[route::2]
        count = kept.shape[0]
        for ref, at in ((kept, slice(0, count)), (sent, slice(count, 2 * count))):
            ref[...] = (keep[at].astype(F32) + got[at].astype(F32)).astype(BF16)


def halve(keep, gots):
    count, *size = keep[0].shape
    outs = pl.pallas_call(
        halve_kernel,
        in_specs=[VMEM_SPEC] * 4,
        out_specs=[VMEM_SPEC] * 4,
        out_shape=[pltpu.VMEM((count // 2, *size), BF16)] * 4,
        compiler_params=params(8),
        cost_estimate=cost(1, 1),
        name="halve",
    )(*[in_vmem(o) for o in (*keep, *gots)])
    return outs[:2], outs[2:]


def pieces_kernel(*refs):
    ins, out_ref, held = refs[:-2], refs[-2], refs[-1]
    for ref, places in zip(ins, ((3, 0), (1, 2))):
        block = ref[...].astype(F32)
        tiles = block.shape[1] // PAIR // 2
        share = block.shape[0] // Z
        for n, place in enumerate(places):
            for t in range(tiles):
                rows = slice((place * tiles + t) * share, (place * tiles + t + 1) * share)
                column = (n * tiles + t) * PAIR
                for z in range(Z):
                    held[z, rows, :] = block[z * share : (z + 1) * share, column : column + PAIR]
    out_ref[...] = held[...].astype(BF16)


def total_kernel(in_ref, out_ref):
    total = in_ref[0].astype(F32)
    for z in range(1, Z):
        total += in_ref[z].astype(F32)
    share = out_ref.shape[0]
    for t in range(out_ref.shape[1] // PAIR):
        out_ref[:, t * PAIR : (t + 1) * PAIR] = total[t * share : (t + 1) * share]


def on_device(frames, cotangent, lengths, w_qkv, w_out):
    frame_rows = frames[0]
    grad_rows = cotangent[0]
    row_count, width = frame_rows.shape
    inner = w_out.shape[0]
    seq_index = lax.axis_index("seq")
    dp_index = lax.axis_index("dp")
    xl = seq_index % XL
    core, xh, y = dp_index % CORES, dp_index // CORES % XH, dp_index // (CORES * XH)
    places = jnp.stack([seq_index * row_count, core, y, xh, xl])

    behind = from_behind(last_rows(frame_rows), "seq", 1)
    frame_rows, places = lax.optimization_barrier((frame_rows, places))
    qkv, attended_grad, left, left_out, stats, weight, late, late_grad, order = front(
        places, lengths, frame_rows, grad_rows, w_qkv, w_out
    )
    left_other = to_device(left_out, to_core)
    own, grads, left_behind = early_tile(places, lengths, order, behind, weight, qkv, attended_grad, late, late_grad)
    own_other = to_device(own, to_core)
    own_sum, grads_sum = own_sums(left, left_behind, own, grads)
    own_other, left_other, own_sum, grads_sum, grads = lax.optimization_barrier(
        (own_other, left_other, own_sum, grads_sum, grads)
    )
    grads_other = to_device(grads, to_core)
    keep_a, send_a = weight_sections(first_wave_kernel, places, (left_other, own_other, own_sum), inner, 1, "first_wave")
    keep_b, send_b = weight_sections(
        second_wave_kernel, places, (left_other, grads_other, grads_sum), inner, 3 * 10**9, "second_wave"
    )
    query_grad = jnp.concatenate([own[1], jnp.zeros((CONTEXT, inner), BF16)], axis=0)
    projected_grad = jnp.concatenate([query_grad, grads[0, :, :inner], grads[1, :, :inner]], axis=1)
    attended, projected_grad, send_b = lax.optimization_barrier((own[0], projected_grad, send_b))
    normed_grad = dot(projected_grad, w_qkv, NT)
    def second_ring(kept, gots, n, *after):
        group = jnp.concatenate([plus(kept[r], gots[r]) for r in range(2)], axis=-1)
        slots, *after = lax.optimization_barrier(([group[slot] for slot in range(1, 4)], *after))
        others = [to_device(slots[i], OWNERS[n][i]) for i in (2, 0, 1)]
        return plus(group[0], *others), *after

    gots_a = [to_device(send_a[r], ROUTES[r][0]) for r in range(2)]
    gots_b = [to_device(send_b[r], ROUTES[2 + r][0]) for r in range(2)]
    gots_a, normed_grad = lax.optimization_barrier((gots_a, normed_grad))
    kept_a, sent_a = halve(keep_a, gots_a)
    gots_a = [to_device(sent_a[r], ROUTES[r][1]) for r in range(2)]
    kept_b, sent_b = halve(keep_b, gots_b)
    attended, sent_b = lax.optimization_barrier((attended, sent_b))
    gots_b = [to_device(sent_b[r], ROUTES[2 + r][1]) for r in range(2)]
    block_out = dot(attended, w_out).astype(BF16)
    gots_a, block_out = lax.optimization_barrier((gots_a, block_out))
    first_group, = second_ring(kept_a, gots_a, 0)
    second_group, normed_grad = second_ring(kept_b, gots_b, 1, normed_grad)
    groups = [first_group, second_group]
    returned = from_behind(normed_grad[row_count:].astype(BF16), "seq", -1)
    returned = jnp.concatenate([jnp.zeros((row_count - CONTEXT, width), BF16), returned], axis=0)
    normed_grad = (normed_grad[:row_count] + returned.astype(F32)).astype(BF16)
    frame_grad = normalize_grad(frame_rows.astype(F32), stats[0][:, None], stats[1][:, None], normed_grad.astype(F32))
    share = width // (CHUNKS * CORES * Z)
    tiles = 4 * inner // PAIR
    shares = pl.pallas_call(
        pieces_kernel,
        in_specs=[VMEM_SPEC] * 2,
        out_shape=jax.ShapeDtypeStruct((Z, tiles * share, PAIR), BF16),
        scratch_shapes=[pltpu.VMEM((Z, tiles * share, PAIR), F32)],
        compiler_params=params(24),
        name="pieces",
    )(*[in_vmem(g) for g in groups])
    rings = [[place * XL + x for place in range(Z)] for x in range(XL)]
    shares = lax.all_to_all(shares, "seq", 0, 0, axis_index_groups=rings, tiled=True)
    total = pl.pallas_call(
        total_kernel,
        in_specs=[VMEM_SPEC],
        out_shape=jax.ShapeDtypeStruct((share, 4 * inner), F32),
        compiler_params=params(24),
        name="total",
    )(in_vmem(shares))
    return block_out[None], frame_grad.astype(BF16)[None], total


def solution(mesh):
    placed = (P("dp", "seq", None), P("dp", "seq", None), P("dp"), P(), P())
    return jax.shard_map(
        on_device,
        mesh=mesh,
        in_specs=placed,
        out_specs=(P("dp", "seq", None), P("dp", "seq", None), P(("dp", "seq"), None)),
        check_vma=False,
    )
```

```python
import jax
import jax.numpy as jnp
import numpy as np
from jax import lax
from jax.experimental import pallas as pl
from jax.experimental.pallas import tpu as pltpu
from jax.sharding import PartitionSpec as P

HEAD_DIM = 64
GROUP = 32
LEFT = 4
CONTEXT = LEFT * GROUP
PAIR = 2 * HEAD_DIM
F32 = jnp.float32
BF16 = jnp.bfloat16
NT = (((1,), (1,)), ((), ()))
NN = (((1,), (0,)), ((), ()))

Y, XH, CORES, Z, XL = 4, 2, 2, 8, 2
CHUNKS = Y * XH * XL

epsilon = 1e-05


def dot(a, b, dims=NN):
    return lax.dot_general(a, b, dims, preferred_element_type=F32)


def from_behind(value, axis, by):
    peers = lax.axis_size(axis)
    return lax.ppermute(value, axis, [(i, (i + by) % peers) for i in range(peers)])


def flat(y, xh, core, z, xl):
    return ((y * XH + xh) * CORES + core) * (Z * XL) + z * XL + xl


def to_device(value, where):
    pairs = []
    for place in np.ndindex(Y, XH, CORES, Z, XL):
        pairs.append((flat(*place), flat(*where(*place))))
    return lax.ppermute(value, ("dp", "seq"), pairs)


def to_core(y, xh, core, z, xl):
    return y, xh, 1 - core, z, xl


def to_x_near(y, xh, core, z, xl):
    return y, xh, core, z, 1 - xl


def to_x_mirror(y, xh, core, z, xl):
    return y, 1 - xh, core, z, 1 - xl


def to_y_near(y, xh, core, z, xl):
    return y ^ 1, xh, core, z, xl


def to_y_mirror(y, xh, core, z, xl):
    return 3 - y, xh, core, z, xl


def to_x_far(y, xh, core, z, xl):
    return y, 1 - xh, core, z, xl


def to_y_far(y, xh, core, z, xl):
    return y ^ 2, xh, core, z, xl


ROUTES = (
    (to_y_near, to_y_mirror),
    (to_y_mirror, to_y_near),
    (to_x_near, to_x_mirror),
    (to_x_mirror, to_x_near),
)
OWNERS = (
    (to_x_mirror, to_x_near, to_x_far),
    (to_y_mirror, to_y_near, to_y_far),
)


def halves(route, hi, lo):
    return (hi ^ lo, hi) if route % 2 == 0 else (hi, hi ^ lo)


def chunk_at(route, slot, y, xh, xl):
    bits = [(slot >> (3 - i)) & 1 for i in range(4)]
    x_first = route >= 2
    x_bits, y_bits = (bits[:2], bits[2:]) if x_first else (bits[2:], bits[:2])
    found = []
    for hi, lo, pair, order in ((y >> 1, y & 1, y_bits, 0 if x_first else route), (xh, xl, x_bits, route if x_first else 0)):
        first, second = halves(order, hi, lo)
        first, second = first ^ pair[0], second ^ pair[1]
        found.append((second, first ^ second) if order % 2 == 0 else (first, first ^ second))
    (yh, yl), (xh_to, xl_to) = found
    return ((yh * 2 + yl) * XH + xh_to) * XL + xl_to


def row_order(width):
    share = width // (CHUNKS * CORES * Z)
    order = np.arange(width // Y).reshape(XH, CORES, Z, XL, share).transpose(1, 0, 3, 2, 4).reshape(-1)
    return jnp.asarray(np.eye(width // Y, dtype=np.float32)[order], BF16)


def statistics(rows_in):
    average = jnp.mean(rows_in, axis=-1, keepdims=True)
    centered = rows_in - average
    variance = jnp.mean(centered * centered, axis=-1, keepdims=True)
    return average, lax.rsqrt(variance + epsilon)


def normalize_grad(rows_in, average, inverse, grad):
    normed = (rows_in - average) * inverse
    along = jnp.mean(grad * normed, axis=-1, keepdims=True)
    return inverse * (grad - jnp.mean(grad, axis=-1, keepdims=True) - normed * along)


SMEM_SPEC = pl.BlockSpec(memory_space=pltpu.SMEM)
VMEM_SPEC = pl.BlockSpec(memory_space=pltpu.VMEM)
HBM_SPEC = pl.BlockSpec(memory_space=pltpu.HBM)


def in_vmem(value):
    return pltpu.with_memory_space_constraint(value, pltpu.VMEM)


def in_hbm(value):
    return pltpu.with_memory_space_constraint(value, pltpu.HBM)


def cost(flops, nbytes, transcendentals=0):
    return pl.CostEstimate(flops=flops, bytes_accessed=nbytes, transcendentals=transcendentals)


def params(mebibytes):
    return pltpu.CompilerParams(vmem_limit_bytes=mebibytes * 2**20)


def turn(ref, order_ref, here, store):
    rows = order_ref.shape[0]
    half = rows // CORES
    for y in range(Y):
        turned = dot(order_ref[...], ref[:, y * rows : (y + 1) * rows].T).astype(BF16)
        first, second = turned[:half], turned[half:]
        at = slice(y * half, (y + 1) * half)
        store(at, jnp.where(here == 0, first, second), jnp.where(here == 0, second, first))


def last_rows(frames):
    rows, width = frames.shape

    pieces = 8

    def kernel(frames_ref, out_ref, sems):
        size = CONTEXT // pieces
        copies = [
            pltpu.make_async_copy(
                frames_ref.at[pl.ds(rows - CONTEXT + i * size, size)], out_ref.at[pl.ds(i * size, size)], sems.at[i]
            )
            for i in range(pieces)
        ]
        for copy in copies:
            copy.start()
        for copy in copies:
            copy.wait()

    return pl.pallas_call(
        kernel,
        in_specs=[HBM_SPEC],
        out_specs=VMEM_SPEC,
        out_shape=pltpu.VMEM((CONTEXT, width), BF16),
        scratch_shapes=[pltpu.SemaphoreType.DMA((pieces,))],
        compiler_params=params(4),
        cost_estimate=cost(1, 1),
        name="last_rows",
    )(in_hbm(frames))


def front_kernel(
    places, lengths_ref, order_ref, frames_ref, cotangent_ref, weight_ref, out_ref,
    qkv_ref, grad_ref, keep_ref, send_ref, stats_ref, weight, late_ref, dkv_ref, order,
    length, rows, cotangent, outer, normed, sems,
):
    here = places[1]
    tokens = rows.shape[0]
    thirds = weight.shape[1] // 3
    block = [slice(n * thirds, (n + 1) * thirds) for n in range(3)]
    small = [
        pltpu.make_async_copy(order_ref, order, sems.at[6]),
        pltpu.make_async_copy(lengths_ref, length, sems.at[7]),
    ]
    copies = [
        pltpu.make_async_copy(frames_ref, rows, sems.at[0]),
        pltpu.make_async_copy(cotangent_ref, cotangent, sems.at[1]),
        pltpu.make_async_copy(out_ref, outer, sems.at[2]),
    ] + [
        pltpu.make_async_copy(weight_ref.at[:, pl.ds(n * thirds, thirds)], weight.at[:, pl.ds(n * thirds, thirds)], sems.at[3 + n])
        for n in range(3)
    ]
    for copy in copies[:1] + small + copies[1:]:
        copy.start()

    def put(columns):
        def store(at, own, other):
            keep_ref[at, columns] = own
            send_ref[at, columns] = other

        return store

    copies[0].wait()
    values = rows[...].astype(F32)
    average, inverse = statistics(values)
    for n, column in enumerate((average, inverse)):
        stats_ref[n : n + 1, :] = jnp.broadcast_to(column, (tokens, PAIR)).T[:1]
    normed[...] = ((values - average) * inverse).astype(BF16)
    small[0].wait()
    turn(normed, order, here, put(slice(0, tokens)))
    copies[1].wait()
    turn(cotangent, order, here, put(slice(tokens, 2 * tokens)))
    copies[2].wait()
    grad_ref[...] = dot(cotangent[...], outer[...], NT).astype(BF16)
    for n in range(3):
        copies[3 + n].wait()
    qkv_ref[...] = dot(normed[...], weight[...]).astype(BF16)

    inner = thirds

    def operands(pair):
        q, k, v = pair_columns(pair, inner)
        return qkv_ref[CONTEXT:, q], qkv_ref[:, k], qkv_ref[:, v], grad_ref[CONTEXT:, q]

    def results(pair, mixed, dq, dk, dv):
        at = pair_columns(pair, inner)[0]
        late_ref[0, :, at] = mixed
        late_ref[1, :, at] = dq
        dkv_ref[0, :, at] = dk
        dkv_ref[1, :, at] = dv

    small[1].wait()
    attend(places[0] + CONTEXT, length[0], inner, operands, results)


def front(places, lengths, frames, cotangent, w_qkv, w_out):
    tokens, width = frames.shape
    inner = w_out.shape[0]
    order = row_order(width)
    turned = pltpu.VMEM((width // CORES, 2 * tokens), BF16)
    return pl.pallas_call(
        front_kernel,
        in_specs=[SMEM_SPEC] + [HBM_SPEC] * 6,
        out_specs=[VMEM_SPEC] * 9,
        out_shape=[
            pltpu.VMEM((tokens, 3 * inner), BF16),
            pltpu.VMEM((tokens, inner), BF16),
            turned,
            turned,
            pltpu.VMEM((2, tokens), F32),
            pltpu.VMEM((width, 3 * inner), BF16),
            pltpu.VMEM((2, CONTEXT, inner), BF16),
            pltpu.VMEM((2, tokens, inner), F32),
            pltpu.VMEM(order.shape, BF16),
        ],
        scratch_shapes=[
            pltpu.SMEM((1,), jnp.int32),
            pltpu.VMEM((tokens, width), BF16),
            pltpu.VMEM((tokens, width), BF16),
            pltpu.VMEM((inner, width), BF16),
            pltpu.VMEM((tokens, width), BF16),
            pltpu.SemaphoreType.DMA((8,)),
        ],
        compiler_params=params(24),
        cost_estimate=cost(12 * tokens * width * inner, 10 * inner * width),
        name="front",
    )(places, lengths, *[in_hbm(o) for o in (order, frames, cotangent, w_qkv, w_out)])


def pair_columns(pair, inner):
    return [slice(n * inner + pair * PAIR, n * inner + (pair + 1) * PAIR) for n in range(3)]


def attend(begin, length, inner, operands, results):
    lane = lax.broadcasted_iota(jnp.int32, (CONTEXT, PAIR), 1)
    heads = (lane < HEAD_DIM, lane >= HEAD_DIM)
    row_valid = begin + lax.broadcasted_iota(jnp.int32, (CONTEXT, PAIR), 0) < length
    col_valid = begin + lane < length
    keys = lax.broadcasted_iota(jnp.int32, (2 * CONTEXT, 2 * CONTEXT), 0)
    queries = lax.broadcasted_iota(jnp.int32, (2 * CONTEXT, 2 * CONTEXT), 1)
    key_block = keys // GROUP
    query_block = (queries % CONTEXT) // GROUP
    key_place = begin - CONTEXT + keys
    seen = (key_block >= query_block) & (key_block <= query_block + LEFT) & (key_place >= 0) & (key_place < length)
    zero = jnp.zeros((CONTEXT, PAIR), BF16)
    scale = HEAD_DIM ** (-0.5)

    def unstack(both):
        return jnp.concatenate([both[:HEAD_DIM, :CONTEXT], both[HEAD_DIM:, CONTEXT:]], axis=0)

    for pair in range(inner // PAIR):
        q, k2, v2, do = operands(pair)
        do = jnp.where(row_valid, do, zero)
        q = q * jnp.asarray(scale, BF16)
        q2 = jnp.concatenate([jnp.where(h, q, zero) for h in heads], axis=0)
        do2 = jnp.concatenate([jnp.where(h, do, zero) for h in heads], axis=0)
        scores = jnp.where(seen, dot(k2, q2, NT), -1e30)
        dprob = dot(v2, do2, NT)
        highest = jnp.max(scores, axis=0, keepdims=True)
        raised = jnp.exp(scores - highest)
        prob = raised * (1.0 / jnp.sum(raised, axis=0, keepdims=True))
        rounded = prob.astype(BF16)
        mixed = jnp.where(col_valid, unstack(dot(v2.T, rounded)), 0.0).T.astype(BF16)
        weighed = prob * dprob
        dscores = (weighed - prob * jnp.sum(weighed, axis=0, keepdims=True)).astype(BF16)
        dq = (unstack(dot(k2.T, dscores)) * scale).T.astype(BF16)
        results(pair, mixed, dq, dot(dscores, q2), dot(rounded, do2))


def early_kernel(
    places, lengths_ref, order_ref, frames_ref, weight_ref, qkv_ref, do_ref, late_ref, add_ref,
    out_ref, dkv_ref, turned_ref, length, normed, halo, sem,
):
    fetch = pltpu.make_async_copy(lengths_ref, length, sem)
    fetch.start()
    inner = do_ref.shape[1]
    rows = qkv_ref.shape[0]
    here = places[1]
    values = frames_ref[...].astype(F32)
    average, inverse = statistics(values)
    normed[...] = ((values - average) * inverse).astype(BF16)
    halo[...] = dot(normed[...], weight_ref[:, inner:]).astype(BF16)
    out_ref[:, CONTEXT:, :] = late_ref[...]
    dkv_ref[:, CONTEXT:rows, :inner] = add_ref[:, CONTEXT:, :].astype(BF16)

    def store(at, own, other):
        turned_ref[at, :] = own
        half = dkv_ref.shape[1]
        for n in range(2):
            first, last = max(at.start, n * half), min(at.stop, (n + 1) * half)
            if first < last:
                dkv_ref[n, first - n * half : last - n * half, inner:] = other[first - at.start : last - at.start]

    turn(normed, order_ref, here, store)

    def operands(pair):
        q, k, v = pair_columns(pair, inner)
        k2 = jnp.concatenate([halo[:, q], qkv_ref[:CONTEXT, k]], axis=0)
        v2 = jnp.concatenate([halo[:, k], qkv_ref[:CONTEXT, v]], axis=0)
        return qkv_ref[:CONTEXT, q], k2, v2, do_ref[:CONTEXT, q]

    def results(pair, mixed, dq, dk, dv):
        at = pair_columns(pair, inner)[0]
        out_ref[0, :CONTEXT, at] = mixed
        out_ref[1, :CONTEXT, at] = dq
        for n, grad in enumerate((dk, dv)):
            dkv_ref[n, rows:, at] = grad[:CONTEXT].astype(BF16)
            dkv_ref[n, :CONTEXT, at] = (grad[CONTEXT:] + add_ref[n, :CONTEXT, at]).astype(BF16)

    fetch.wait()
    attend(places[0], length[0], inner, operands, results)


def early_tile(places, lengths, order, frames, weight, qkv, attended_grad, late, late_grad):
    rows, inner = attended_grad.shape
    width = frames.shape[1]
    return pl.pallas_call(
        early_kernel,
        in_specs=[SMEM_SPEC, HBM_SPEC] + [VMEM_SPEC] * 7,
        out_specs=[VMEM_SPEC] * 3,
        out_shape=[
            pltpu.VMEM((2, rows, inner), BF16),
            pltpu.VMEM((2, rows + CONTEXT, inner + CONTEXT), BF16),
            pltpu.VMEM((width // CORES, CONTEXT), BF16),
        ],
        scratch_shapes=[
            pltpu.SMEM((1,), jnp.int32),
            pltpu.VMEM((CONTEXT, width), BF16),
            pltpu.VMEM((CONTEXT, 2 * inner), BF16),
            pltpu.SemaphoreType.DMA,
        ],
        compiler_params=params(16),
        cost_estimate=cost(28 * CONTEXT * 2 * CONTEXT * inner, 16 * CONTEXT * inner, CONTEXT * 4 * inner),
        name="attention_early",
    )(places, lengths, *[in_vmem(o) for o in (order, frames, weight, qkv, attended_grad, late, late_grad)])


def store_section(chunks, route, n, total, outs, held):
    half = CHUNKS // 2
    held[n] = total.astype(BF16).reshape(held.shape[1:])
    for slot in range(CHUNKS):
        outs[n if slot < half else 2 + n][slot % half] = held[n, chunks[route, slot]]


def own_kernel(left_ref, behind_ref, first_ref, second_ref, first_out, second_out):
    tokens = first_ref.shape[1]
    inner = first_ref.shape[2]
    left = jnp.concatenate([left_ref[:, :tokens], behind_ref[...]], axis=1)
    first_out[0] = dot(left_ref[:, tokens:], first_ref[0])
    first_out[1] = dot(left_ref[:, :tokens], first_ref[1])
    for n in range(2):
        second_out[n] = dot(left, second_ref[n, :, :inner])


def own_sums(left, behind, first, second):
    rows, inner = left.shape[0], first.shape[2]
    return pl.pallas_call(
        own_kernel,
        in_specs=[VMEM_SPEC] * 4,
        out_specs=[VMEM_SPEC] * 2,
        out_shape=[pltpu.VMEM((2, rows, inner), F32)] * 2,
        compiler_params=params(8),
        cost_estimate=cost(4 * 10**9, 1),
        name="own_sums",
    )(*[in_vmem(o) for o in (left, behind, first, second)])


def first_wave_kernel(chunks, left_other_ref, right_other_ref, own_ref, *refs):
    tokens = right_other_ref.shape[1]
    for n, at in enumerate((slice(tokens, 2 * tokens), slice(0, tokens))):
        total = own_ref[n] + dot(left_other_ref[:, at], right_other_ref[n])
        store_section(chunks, n, n, total, refs[:-1], refs[-1])


def second_wave_kernel(chunks, left_other_ref, right_other_ref, own_ref, *refs):
    tokens = left_other_ref.shape[1] // 2
    inner = right_other_ref.shape[2] - CONTEXT
    behind = jnp.concatenate([right_other_ref[n, :, inner:] for n in range(2)], axis=0)
    left = jnp.concatenate([left_other_ref[:, :tokens], behind], axis=1)
    for n in range(2):
        total = own_ref[n] + dot(left, right_other_ref[n, :, :inner])
        store_section(chunks, 2 + n, n, total, refs[:-1], refs[-1])


def weight_sections(kernel, chunks, operands, inner, flops, name):
    size = (operands[0].shape[0] // CHUNKS, inner)
    routes = 2
    outs = pl.pallas_call(
        kernel,
        in_specs=[SMEM_SPEC] + [VMEM_SPEC] * len(operands),
        out_specs=[VMEM_SPEC] * (2 * routes),
        out_shape=[pltpu.VMEM((CHUNKS // 2, *size), BF16)] * (2 * routes),
        scratch_shapes=[pltpu.VMEM((routes, CHUNKS, *size), BF16)],
        compiler_params=params(24),
        cost_estimate=cost(flops, 1),
        name=name,
    )(chunks, *[in_vmem(o) for o in operands])
    return outs[:routes], outs[routes:]


def plus(*terms):
    return sum(t.astype(F32) for t in terms).astype(BF16)


def halve_kernel(*refs):
    for route in range(2):
        keep, got, kept, sent = refs[route::2]
        count = kept.shape[0]
        for ref, at in ((kept, slice(0, count)), (sent, slice(count, 2 * count))):
            ref[...] = (keep[at].astype(F32) + got[at].astype(F32)).astype(BF16)


def halve(keep, gots):
    count, *size = keep[0].shape
    outs = pl.pallas_call(
        halve_kernel,
        in_specs=[VMEM_SPEC] * 4,
        out_specs=[VMEM_SPEC] * 4,
        out_shape=[pltpu.VMEM((count // 2, *size), BF16)] * 4,
        compiler_params=params(8),
        cost_estimate=cost(1, 1),
        name="halve",
    )(*[in_vmem(o) for o in (*keep, *gots)])
    return outs[:2], outs[2:]


def pieces_kernel(*refs):
    ins, out_ref, held = refs[:-2], refs[-2], refs[-1]
    for ref, places in zip(ins, ((3, 0), (1, 2))):
        block = ref[...].astype(F32)
        tiles = block.shape[1] // PAIR // 2
        share = block.shape[0] // Z
        for n, place in enumerate(places):
            for t in range(tiles):
                rows = slice((place * tiles + t) * share, (place * tiles + t + 1) * share)
                column = (n * tiles + t) * PAIR
                for z in range(Z):
                    held[z, rows, :] = block[z * share : (z + 1) * share, column : column + PAIR]
    out_ref[...] = held[...].astype(BF16)


def total_kernel(in_ref, out_ref):
    total = in_ref[0].astype(F32)
    for z in range(1, Z):
        total += in_ref[z].astype(F32)
    share = out_ref.shape[0]
    for t in range(out_ref.shape[1] // PAIR):
        out_ref[:, t * PAIR : (t + 1) * PAIR] = total[t * share : (t + 1) * share]


def on_device(frames, cotangent, lengths, w_qkv, w_out):
    frame_rows = frames[0]
    grad_rows = cotangent[0]
    row_count, width = frame_rows.shape
    inner = w_out.shape[0]
    seq_index = lax.axis_index("seq")
    dp_index = lax.axis_index("dp")
    xl = seq_index % XL
    core, xh, y = dp_index % CORES, dp_index // CORES % XH, dp_index // (CORES * XH)
    places = jnp.stack([seq_index * row_count, core])
    chunks = jnp.stack([chunk_at(r, jnp.arange(CHUNKS), y, xh, xl) for r in range(len(ROUTES))])

    behind = from_behind(last_rows(frame_rows), "seq", 1)
    frame_rows, places, chunks = lax.optimization_barrier((frame_rows, places, chunks))
    qkv, attended_grad, left, left_out, stats, weight, late, late_grad, order = front(
        places, lengths, frame_rows, grad_rows, w_qkv, w_out
    )
    left_other = to_device(left_out, to_core)
    own, grads, left_behind = early_tile(places, lengths, order, behind, weight, qkv, attended_grad, late, late_grad)
    own_other = to_device(own, to_core)
    own_sum, grads_sum = own_sums(left, left_behind, own, grads)
    own_other, left_other, own_sum, grads_sum, grads = lax.optimization_barrier(
        (own_other, left_other, own_sum, grads_sum, grads)
    )
    grads_other = to_device(grads, to_core)
    keep_a, send_a = weight_sections(first_wave_kernel, chunks, (left_other, own_other, own_sum), inner, 1, "first_wave")
    keep_b, send_b = weight_sections(
        second_wave_kernel, chunks, (left_other, grads_other, grads_sum), inner, 3 * 10**9, "second_wave"
    )
    query_grad = jnp.concatenate([own[1], jnp.zeros((CONTEXT, inner), BF16)], axis=0)
    projected_grad = jnp.concatenate([query_grad, grads[0, :, :inner], grads[1, :, :inner]], axis=1)
    attended, projected_grad, send_b = lax.optimization_barrier((own[0], projected_grad, send_b))
    normed_grad = dot(projected_grad, w_qkv, NT)
    def second_ring(kept, gots, n, *after):
        group = jnp.concatenate([plus(kept[r], gots[r]) for r in range(2)], axis=-1)
        slots, *after = lax.optimization_barrier(([group[slot] for slot in range(1, 4)], *after))
        others = [to_device(slots[i], OWNERS[n][i]) for i in (2, 0, 1)]
        return plus(group[0], *others), *after

    gots_a = [to_device(send_a[r], ROUTES[r][0]) for r in range(2)]
    gots_b = [to_device(send_b[r], ROUTES[2 + r][0]) for r in range(2)]
    gots_a, normed_grad = lax.optimization_barrier((gots_a, normed_grad))
    kept_a, sent_a = halve(keep_a, gots_a)
    gots_a = [to_device(sent_a[r], ROUTES[r][1]) for r in range(2)]
    kept_b, sent_b = halve(keep_b, gots_b)
    attended, sent_b = lax.optimization_barrier((attended, sent_b))
    gots_b = [to_device(sent_b[r], ROUTES[2 + r][1]) for r in range(2)]
    block_out = dot(attended, w_out).astype(BF16)
    gots_a, block_out = lax.optimization_barrier((gots_a, block_out))
    first_group, = second_ring(kept_a, gots_a, 0)
    second_group, normed_grad = second_ring(kept_b, gots_b, 1, normed_grad)
    groups = [first_group, second_group]
    returned = from_behind(normed_grad[row_count:].astype(BF16), "seq", -1)
    returned = jnp.concatenate([jnp.zeros((row_count - CONTEXT, width), BF16), returned], axis=0)
    normed_grad = (normed_grad[:row_count] + returned.astype(F32)).astype(BF16)
    frame_grad = normalize_grad(frame_rows.astype(F32), stats[0][:, None], stats[1][:, None], normed_grad.astype(F32))
    share = width // (CHUNKS * CORES * Z)
    tiles = 4 * inner // PAIR
    shares = pl.pallas_call(
        pieces_kernel,
        in_specs=[VMEM_SPEC] * 2,
        out_shape=jax.ShapeDtypeStruct((Z, tiles * share, PAIR), BF16),
        scratch_shapes=[pltpu.VMEM((Z, tiles * share, PAIR), F32)],
        compiler_params=params(24),
        name="pieces",
    )(*[in_vmem(g) for g in groups])
    rings = [[place * XL + x for place in range(Z)] for x in range(XL)]
    shares = lax.all_to_all(shares, "seq", 0, 0, axis_index_groups=rings, tiled=True)
    total = pl.pallas_call(
        total_kernel,
        in_specs=[VMEM_SPEC],
        out_shape=jax.ShapeDtypeStruct((share, 4 * inner), F32),
        compiler_params=params(24),
        name="total",
    )(in_vmem(shares))
    return block_out[None], frame_grad.astype(BF16)[None], total


def solution(mesh):
    placed = (P("dp", "seq", None), P("dp", "seq", None), P("dp"), P(), P())
    return jax.shard_map(
        on_device,
        mesh=mesh,
        in_specs=placed,
        out_specs=(P("dp", "seq", None), P("dp", "seq", None), P(("dp", "seq"), None)),
        check_vma=False,
    )
```
